32 devices in a mesh: dp: 16 (over z, x, core), head: 2 (over y).
Axes of the slice: x: 2, y: 2, z: 4, core: 2. Of those that a mesh axis runs over, the one named last changes fastest.
Arguments:
- block_in: bfloat16 [16, 1024, 768], P('dp', 'head'), may hold values from -8 to 8
- text: bfloat16 [16, 256, 1024], P('dp'), may hold values from -6 to 6
- timesteps: int32 [16], P('dp'), may hold values from 0 to 999
- frame_mask: int32 [16, 1024], P('dp'), may hold values from 0 to 1, as said below
- text_mask: int32 [16, 256], P('dp'), may hold values from 0 to 1, as said below
- cotangent: bfloat16 [16, 1024, 768], P('dp', 'head'), may hold values from -6 to 6
- w_ada: float32 [768, 4608], P(('dp', 'head')), may hold values from -0.625 to 0.625
- w_qkv: float32 [768, 2304], P(('dp', 'head')), may hold values from -0.21875 to 0.21875
- w_out: float32 [768, 768], P(('dp', 'head')), may hold values from -3.5 to 3.5
- w_cq: float32 [768, 768], P(('dp', 'head')), may hold values from -0.21875 to 0.21875
- w_cout: float32 [768, 768], P(('dp', 'head')), may hold values from -1.75 to 1.75
- w_ckv: float32 [1024, 2, 768], P('dp', None, 'head'), may hold values from -0.1875 to 0.1875
- w_fc1: float32 [768, 3072], P('dp', 'head'), may hold values from -0.21875 to 0.21875
- w_fc2: float32 [3072, 768], P('head', 'dp'), may hold values from -0.109375 to 0.109375
- row_state: float32 [8704], replicated, may hold values from 2.2439396e-08 to 5.983839e-07, as said below
- col_state: float32 [14592], replicated, may hold values from 2.2439396e-08 to 5.983839e-07, as said below
Outputs:
- block_out: bfloat16 [16, 1024, 768], P('dp', 'head')
- input_grad: bfloat16 [16, 1024, 768], P('dp', 'head')
- grad_norm: float32 [], replicated
- row_new: float32 [8704], replicated
- col_new: float32 [14592], replicated
- grad_ada: float32 [768, 4608], P(('dp', 'head'))
- grad_qkv: float32 [768, 2304], P(('dp', 'head'))
- grad_out: float32 [768, 768], P(('dp', 'head'))
- grad_cq: float32 [768, 768], P(('dp', 'head'))
- grad_cout: float32 [768, 768], P(('dp', 'head'))
- grad_ckv: float32 [1024, 2, 768], P('dp', None, 'head')
- grad_fc1: float32 [768, 3072], P('dp', 'head')
- grad_fc2: float32 [3072, 768], P('head', 'dp')
- new_ada: float32 [768, 4608], P(('dp', 'head'))
- new_qkv: float32 [768, 2304], P(('dp', 'head'))
- new_out: float32 [768, 768], P(('dp', 'head'))
- new_cq: float32 [768, 768], P(('dp', 'head'))
- new_cout: float32 [768, 768], P(('dp', 'head'))
- new_ckv: float32 [1024, 2, 768], P('dp', None, 'head')
- new_fc1: float32 [768, 3072], P('dp', 'head')
- new_fc2: float32 [3072, 768], P('head', 'dp')
The draws below stay inside these ranges and needn't reach their ends.
Inputs may be any that keep to these rules, and one draw needn't show every extreme that they name: `frame_mask`: each clip's frame mask is 1 on a prefix of 256 to 1024 frames and 0 after it; in each aligned block of 4 clips, one clip has all 1024 frames. `text_mask`: each clip's text mask is 1 on a prefix of 77 to 256 tokens and 0 after it; some clip has 77 tokens and some has 256. `row_state`: Positive. `col_state`: Positive.
All inputs are finite; a program needn't handle non-finite values.
Results may differ from the reference program's by a relative error of at most 0.023.
The reference program's roundings to bfloat16 on the way count: a program that leaves them out, or rounds other values in their place, can miss the bound.
Values may be sent and summed in bfloat16 or wider, within the bound.
No kernel may reach another device: no remote copies, remote signals or barrier semaphores. Data moves between devices by JAX's collectives and lax.ppermute only.
A program may use at most 192 MiB of HBM per device.

```python
import jax
import jax.numpy as jnp
from jax import lax

D = 768
FF = 3072
DT = 1024
HD = 64
F = 1024
L = 256
TEXT_MIN = 77
CLIPS = 16


def draw_block_in(key, part):
    key = jax.random.fold_in(key, 11)
    ramp = jnp.arange(D, dtype=jnp.float32) / (D - 1)
    base = jax.random.normal(key, (CLIPS, F, D), jnp.float32)
    scale = 0.6 + 1.2 * ramp
    return jnp.clip(base * scale, -8.0, 8.0).astype(jnp.bfloat16)


def draw_frame_mask(key, part):
    key = jax.random.fold_in(key, 12)
    first_key, second_key = jax.random.split(key)
    lengths = jax.random.randint(first_key, (CLIPS,), F // 4, F + 1)
    picked = jax.random.randint(second_key, (CLIPS // 4,), 0, 4)
    full_clip = jnp.arange(CLIPS) % 4 == jnp.repeat(picked, 4)
    lengths = jnp.where(full_clip, F, lengths)
    return (jnp.arange(F)[None, :] < lengths[:, None]).astype(jnp.int32)


def draw_text_mask(key, part):
    key = jax.random.fold_in(key, 13)
    first_key, second_key = jax.random.split(key)
    lengths = jax.random.randint(first_key, (CLIPS,), TEXT_MIN, L + 1)
    chosen = jax.random.randint(second_key, (), 0, CLIPS)
    positions = jnp.arange(CLIPS)
    lengths = jnp.where(positions == chosen, L, lengths)
    lengths = jnp.where(positions == (chosen + 1) % CLIPS, TEXT_MIN, lengths)
    return (jnp.arange(L)[None, :] < lengths[:, None]).astype(jnp.int32)


def falling_state(key, segments, top):
    unit = 1.0 / (12 * D * D + 2 * D * DT + 2 * D * FF)
    ramps = jnp.concatenate([jnp.arange(size, dtype=jnp.float32) / (size - 1) for size in segments])
    spread = jnp.exp(jax.random.uniform(key, ramps.shape, jnp.float32, -0.35, 0.35))
    return unit * jnp.exp(jnp.log(top) * (1.0 - ramps)) * spread


def draw_row_state(key, part):
    key = jax.random.fold_in(key, 14)
    segments = [D, D, D, D, D, DT, D, FF]
    return falling_state(key, segments, 4.0)


def draw_col_state(key, part):
    key = jax.random.fold_in(key, 15)
    segments = [6 * D, 3 * D, D, D, D, 2 * D, FF, D]
    return falling_state(key, segments, 4.0)


def touch_ends(entries, stream_key, low, high):
    shape = entries.shape
    place = [jax.random.randint(jax.random.fold_in(stream_key, axis), (), 0, shape[axis]) for axis in range(len(shape))]
    entries = entries.at[tuple(place)].set(low)
    longest = shape.index(max(shape))
    place[longest] = (place[longest] + 1) % shape[longest]
    return entries.at[tuple(place)].set(high)


def block_scale(key, extent, cuts, smallest, high):
    def one(position, blocks):
        draws = jax.random.uniform(jax.random.fold_in(jax.random.fold_in(key, 6), position), (blocks,), jnp.float32, smallest / len(cuts), high / len(cuts))
        return jnp.repeat(jnp.exp(draws), extent[position] // blocks).reshape((-1,) + (1,) * (len(extent) - position - 1))

    factor_of = one(*cuts[0])
    for cut in cuts[1:]:
        factor_of = factor_of * one(*cut)
    return factor_of


def centred(own_key, extent, width, most, shards=(), kind=jnp.bfloat16):
    values = jax.random.normal(own_key, extent, jnp.float32) * width
    if len(shards) > 0:
        values = block_scale(own_key, extent, shards, -0.22, 0.18) * values
    return jnp.clip(values, min=-most, max=most).astype(kind)


def setup_inputs(seed: int = 0) -> dict:
    key_of = jax.random.split(jax.random.key(seed), 17)
    block_in = draw_block_in(jax.random.fold_in(key_of[16], 71), 0)
    text = centred(key_of[1], (CLIPS, L, DT), 1.0, 6.0, ((0, 16),))
    timesteps = touch_ends(jax.random.randint(key_of[2], (CLIPS,), 0, 1000), jax.random.fold_in(key_of[2], 1), 0, 999).astype(jnp.int32)
    frame_mask = draw_frame_mask(jax.random.fold_in(key_of[16], 71), 0)
    text_mask = draw_text_mask(jax.random.fold_in(key_of[16], 71), 0)
    cotangent = centred(key_of[5], (CLIPS, F, D), 1.0, 6.0, ((0, 16), (1, 2)))
    w_ada = centred(key_of[6], (D, 6 * D), (D // 8) ** -0.5, 0.625, ((0, 32),), jnp.float32)
    w_qkv = centred(key_of[7], (D, 3 * D), D ** -0.5, 0.21875, ((0, 32),), jnp.float32)
    w_out = centred(key_of[8], (D, D), (D * 4 // F) ** -0.5, 3.5, ((0, 32),), jnp.float32)
    w_cq = centred(key_of[9], (D, D), D ** -0.5, 0.21875, ((0, 32),), jnp.float32)
    w_cout = centred(key_of[10], (D, D), (D * 4 // L) ** -0.5, 1.75, ((0, 32),), jnp.float32)
    w_ckv = centred(key_of[11], (DT, 2, D), DT ** -0.5, 0.1875, ((0, 16), (2, 2)), jnp.float32)
    w_fc1 = centred(key_of[12], (D, FF), D ** -0.5, 0.21875, ((0, 16), (1, 2)), jnp.float32)
    w_fc2 = centred(key_of[13], (FF, D), FF ** -0.5, 0.109375, ((0, 2), (1, 16)), jnp.float32)
    row_state = draw_row_state(jax.random.fold_in(key_of[16], 71), 0)
    col_state = draw_col_state(jax.random.fold_in(key_of[16], 71), 0)
    return dict(block_in=block_in, text=text, timesteps=timesteps, frame_mask=frame_mask, text_mask=text_mask, cotangent=cotangent, w_ada=w_ada, w_qkv=w_qkv, w_out=w_out, w_cq=w_cq, w_cout=w_cout, w_ckv=w_ckv, w_fc1=w_fc1, w_fc2=w_fc2, row_state=row_state, col_state=col_state)


@jax.custom_vjp
def low(v):
    return lax.optimization_barrier(v.astype(jnp.bfloat16)).astype(jnp.float32)

@jax.custom_vjp
def low_back(v):
    return v

def low_keep(v):
    return (low(v), None)

def low_pass(kept, grad):
    return (grad,)

def back_keep(v):
    return (v, None)

def back_low(kept, grad):
    return (low(grad),)
low.defvjp(low_keep, low_pass)
low_back.defvjp(back_keep, back_low)
PRECISE = lax.Precision.HIGHEST
EPS_NORM = 1e-06
EPS_FACTOR = 1e-30
CLIP_NORM = 1.0
CLIP_UPDATE = 0.25
DECAY_RATE = 0.5
RELATIVE_RATE = 4.0
SCALE_FLOOR = 0.001
SCORE_SCALE = 0.125
MASKED_SCORE = -1e+30

def embed(timestep, model_width):
    halfway = model_width // 2
    freqs = jnp.exp(-jnp.log(10000.0) * jnp.arange(halfway, dtype=jnp.float32) / halfway)
    angles = timestep.astype(jnp.float32)[..., None] * freqs
    return jnp.concatenate([jnp.cos(angles), jnp.sin(angles)], axis=-1)

def layer_norm(values):
    centered = values - lax.optimization_barrier(jnp.mean(values, axis=-1, keepdims=True))
    variance = lax.optimization_barrier(jnp.mean(centered * centered, axis=-1, keepdims=True))
    return centered * lax.rsqrt(variance + EPS_NORM)

def modulate(values, shift, scale):
    return layer_norm(values) * (1.0 + scale) + shift

def head_attend(pieces):
    queries, keys, values, allowed = pieces
    scores = low_back(jnp.dot(queries, keys.T, precision=PRECISE) * SCORE_SCALE)
    scores = jnp.where(allowed[None, :], scores, MASKED_SCORE)
    peak = lax.optimization_barrier(jnp.max(scores, axis=-1, keepdims=True))
    exponent = jnp.exp(scores - peak)
    probs = exponent / lax.optimization_barrier(jnp.sum(exponent, axis=-1, keepdims=True))
    return jnp.dot(low(probs), values, precision=PRECISE)

def split_heads(tensor, head_count):
    return tensor.reshape(tensor.shape[0], head_count, HD).transpose(1, 0, 2)

def attend(queries, keys, values, allowed):
    head_count = queries.shape[1] // HD
    result = lax.map(jax.checkpoint(head_attend), (split_heads(queries, head_count), split_heads(keys, head_count), split_heads(values, head_count), jnp.broadcast_to(allowed, (head_count, allowed.shape[0]))))
    return result.transpose(1, 0, 2).reshape(queries.shape[0], -1)

def clip_forward(weights, inputs, clip_text, clip_step, frames_allowed, tokens_allowed):
    w_ada, w_qkv, w_out, w_cq, w_cout, w_ckv, w_fc1, w_fc2 = weights
    condition = low(jax.nn.silu(embed(clip_step, D)))
    modulation = jnp.dot(condition, low(w_ada), precision=PRECISE)
    shift_self, scale_self, gate_self, shift_mlp, scale_mlp, gate_mlp = jnp.split(modulation, 6)
    self_input = low(modulate(inputs, shift_self, scale_self))
    projected = jnp.dot(self_input, low(w_qkv), precision=PRECISE)
    queries = low(low_back(projected[:, :D]))
    keys = low(low_back(projected[:, D:2 * D]))
    values = low(low_back(projected[:, 2 * D:]))
    self_attn = low(low_back(attend(queries, keys, values, frames_allowed)))
    self_branch = low_back(jnp.dot(self_attn, low(w_out), precision=PRECISE))
    after_self = inputs + gate_self * self_branch
    cross_input = low(layer_norm(after_self))
    cross_query = low(low_back(jnp.dot(cross_input, low(w_cq), precision=PRECISE)))
    text_pair = low(low_back(jnp.einsum('ld,dke->lke', clip_text, low(w_ckv), precision=PRECISE)))
    cross_attn = low(low_back(attend(cross_query, text_pair[:, 0], text_pair[:, 1], tokens_allowed)))
    cross_branch = low_back(jnp.dot(cross_attn, low(w_cout), precision=PRECISE))
    after_cross = after_self + cross_branch
    mlp_input = low(modulate(after_cross, shift_mlp, scale_mlp))
    hidden_pre = low_back(jnp.dot(mlp_input, low(w_fc1), precision=PRECISE))
    hidden_act = low(jax.nn.gelu(hidden_pre))
    mlp_branch = low_back(jnp.dot(hidden_act, low(w_fc2), precision=PRECISE))
    return after_cross + gate_mlp * mlp_branch

def reference(block_in, text, timesteps, frame_mask, text_mask, cotangent, w_ada, w_qkv, w_out, w_cq, w_cout, w_ckv, w_fc1, w_fc2, row_state, col_state):
    masters = (w_ada, w_qkv, w_out, w_cq, w_cout, w_ckv, w_fc1, w_fc2)

    def one_clip(totals, pieces):
        clip_in, clip_text, clip_step, clip_frames, clip_tokens, clip_cot = pieces

        def forward(weights, values):
            return clip_forward(weights, values, clip_text.astype(jnp.float32), clip_step, clip_frames > 0, clip_tokens > 0)
        result, backward = jax.vjp(forward, masters, clip_in.astype(jnp.float32))
        weight_grads, value_grads = backward(clip_cot.astype(jnp.float32))
        totals = jax.tree.map(jnp.add, totals, weight_grads)
        return (totals, (result.astype(jnp.bfloat16), value_grads.astype(jnp.bfloat16)))
    zeros = tuple((jnp.zeros(master.shape, jnp.float32) for master in masters))
    grads, (block_out, input_grad) = lax.scan(one_clip, zeros, (block_in, text, timesteps, frame_mask, text_mask, cotangent))
    matrices = [grad.reshape(grad.shape[0], -1) for grad in grads]
    total = sum((jnp.sum(matrix * matrix) for matrix in matrices))
    grad_norm = jnp.sqrt(total)
    factor = 1.0 / jnp.maximum(1.0, grad_norm / CLIP_NORM)
    row_parts, col_parts, clipped, updated = ([], [], [], [])
    row_at, col_at = (0, 0)
    for matrix, master in zip(matrices, masters):
        height, breadth = matrix.shape
        clipped_grad = matrix * factor
        row_part = DECAY_RATE * row_state[row_at:row_at + height] + (1.0 - DECAY_RATE) * (lax.optimization_barrier(jnp.mean(clipped_grad * clipped_grad, axis=1)) + EPS_FACTOR)
        col_part = DECAY_RATE * col_state[col_at:col_at + breadth] + (1.0 - DECAY_RATE) * (lax.optimization_barrier(jnp.mean(clipped_grad * clipped_grad, axis=0)) + EPS_FACTOR)
        row_at = row_at + height
        col_at = col_at + breadth
        estimate = row_part[:, None] * col_part[None, :] / jnp.mean(row_part)
        update = clipped_grad * lax.rsqrt(estimate)
        update = update / jnp.maximum(1.0, jnp.sqrt(jnp.mean(update * update)) / CLIP_UPDATE)
        flat_master = master.reshape(height, breadth)
        rate = RELATIVE_RATE * jnp.maximum(SCALE_FLOOR, jnp.sqrt(jnp.mean(flat_master * flat_master)))
        row_parts.append(row_part)
        col_parts.append(col_part)
        clipped.append(clipped_grad.reshape(master.shape))
        updated.append((flat_master - rate * update).reshape(master.shape))
    row_new = jnp.concatenate(row_parts)
    col_new = jnp.concatenate(col_parts)
    grad_ada, grad_qkv, grad_out, grad_cq, grad_cout, grad_ckv, grad_fc1, grad_fc2 = clipped
    new_ada, new_qkv, new_out, new_cq, new_cout, new_ckv, new_fc1, new_fc2 = updated
    return (block_out, input_grad, grad_norm, row_new, col_new, grad_ada, grad_qkv, grad_out, grad_cq, grad_cout, grad_ckv, grad_fc1, grad_fc2, new_ada, new_qkv, new_out, new_cq, new_cout, new_ckv, new_fc1, new_fc2)
```

```python
import functools

import jax
import jax.numpy as jnp
from jax import lax
from jax.experimental import pallas as pl
from jax.experimental.pallas import tpu as pltpu
from jax.sharding import PartitionSpec as P

D = 768
FF = 3072
DT = 1024
HD = 64
HALF = FF // 2

PRECISE = lax.Precision.HIGHEST
FLOAT = jnp.float32
BFLOAT = jnp.bfloat16
EPS_NORM = 1e-06
EPS_FACTOR = 1e-30
CLIP_NORM = 1.0
CLIP_UPDATE = 0.25
DECAY_RATE = 0.5
RELATIVE_RATE = 4.0
SCALE_FLOOR = 0.001
SCORE_SCALE = 0.125
MASKED_SCORE = -1e30
ALL = ("dp", "head")
PAIR = 2 * HD
PAIRS = D // PAIR


def embed_part(steps, first, count):
    halfway = D // 2
    place = first + jnp.arange(count)
    freqs = jnp.exp(-jnp.log(10000.0) * (place % halfway).astype(FLOAT) / halfway)
    angles = steps.astype(FLOAT)[:, None] * freqs
    waves = jnp.where(place < halfway, jnp.cos(angles), jnp.sin(angles))
    return jax.nn.silu(waves).astype(BFLOAT)


def layer_norm(values):
    centered = values - jnp.mean(values, axis=-1, keepdims=True)
    variance = jnp.mean(centered * centered, axis=-1, keepdims=True)
    return centered * lax.rsqrt(variance + EPS_NORM)


def modulate(values, shift, scale):
    return layer_norm(values) * (1.0 + scale) + shift


def core_link():
    return ("dp", 1)


def row_link():
    return ("head", 1)


def far_links():
    masks, mask = [], 2
    while mask < lax.axis_size("dp"):
        masks.append(mask)
        mask = mask * 2
    return [("dp", mask) for mask in masks]


def dp_bits():
    return lax.axis_size("dp").bit_length() - 1


def bit_of(link):
    return (lax.axis_index(link[0]) // link[1]) % 2


def cross(values, link):
    pairs = [(place, place ^ link[1]) for place in range(lax.axis_size(link[0]))]
    return lax.ppermute(values, link[0], pairs)


def dim_of(link, head_first):
    if link[0] == "head":
        return 0 if head_first else dp_bits()
    return (1 if head_first else 0) + dp_bits() - link[1].bit_length()


def grow(block, link, head_first):
    other = cross(block, link)
    upper = bit_of(link) == 1
    low = jnp.where(upper, other, block)
    high = jnp.where(upper, block, other)
    return jnp.concatenate([low, high], axis=dim_of(link, head_first))


def shrink(block, link, head_first, kind=BFLOAT):
    dim, bit = dim_of(link, head_first), bit_of(link)
    kept = lax.dynamic_slice_in_dim(block, bit, 1, axis=dim)
    sent = lax.dynamic_slice_in_dim(block, 1 - bit, 1, axis=dim)
    return (kept.astype(FLOAT) + cross(sent.astype(BFLOAT), link).astype(FLOAT)).astype(kind)


def gather_shard(shard, head_first, row_early):
    block = shard.reshape((1,) * (dp_bits() + 1) + shard.shape)
    far = far_links()
    plane = [row_link(), far[0]] if row_early else [far[0], row_link()]
    for link in far[1:] + plane + [core_link()]:
        block = grow(block, link, head_first)
    return block


def scatter_sum(block, head_first, row_early):
    far = far_links()
    plane = [far[0], row_link()] if row_early else [row_link(), far[0]]
    order = [core_link()] + plane + far[:0:-1]
    for place, link in enumerate(order):
        block = shrink(block, link, head_first, FLOAT if place == len(order) - 1 else BFLOAT)
    return block.reshape(block.shape[dp_bits() + 1 :])


def split_rows(matrix):
    bits = dp_bits() + 1
    return matrix.reshape((2,) * bits + (matrix.shape[0] // 2**bits, matrix.shape[1]))


def split_halves(matrices):
    bits = dp_bits()
    return matrices.reshape(
        (2,) * (bits + 1) + (matrices.shape[1] // 2**bits, matrices.shape[2])
    )


def sum_all(values):
    for link in [core_link(), row_link()] + far_links():
        values = values + cross(values, link)
    return values


def swap_place(values):
    pairs = []
    for place in range(lax.axis_size("dp")):
        for head in range(2):
            pairs.append((place * 2 + head, ((place & ~1) | head) * 2 + (place & 1)))
    return lax.ppermute(values, ALL, pairs)


def from_clip_core(values):
    pairs = []
    for place in range(0, lax.axis_size("dp"), 2):
        for head in range(2):
            pairs.append(((place + head) * 2 + head, (place + 1 - head) * 2 + head))
    own = bit_of(core_link()) == bit_of(row_link())
    return jnp.where(own, values, lax.ppermute(values, ALL, pairs))


def nt(left, right):
    return lax.dot_general(left, right, (((1,), (1,)), ((), ())), preferred_element_type=FLOAT)


def nn(left, right):
    return lax.dot_general(left, right, (((1,), (0,)), ((), ())), preferred_element_type=FLOAT)


def lanes_of(length):
    return lax.broadcasted_iota(jnp.int32, (length, PAIR), 1)


def with_spare(pair, head, spare):
    lane = lanes_of(pair.shape[0])
    rest = jnp.where(lane == HD * (1 - head), spare, jnp.zeros_like(pair))
    return jnp.where(lane // HD == head, pair, rest)


def attend_kernel(blocks, *refs):
    query_ref = refs[0]
    key_refs, value_refs, bias_refs = refs[1 : 1 + 3 * blocks : 3], refs[2 : 2 + 3 * blocks : 3], refs[3 : 3 + 3 * blocks : 3]
    out_ref, log_ref = refs[1 + 3 * blocks :]
    queries = query_ref[...] * jnp.asarray(SCORE_SCALE, BFLOAT)
    one = jnp.ones((1, 1), BFLOAT)
    values_t = [ref[...].T for ref in value_refs]
    results, logs = [], []
    for head in range(2):
        query = with_spare(queries, head, one)
        scores = [
            nt(with_spare(key_ref[...], head, bias_ref[...]), query)
            for key_ref, bias_ref in zip(key_refs, bias_refs)
        ]
        peak = functools.reduce(
            jnp.maximum, [jnp.max(score, axis=0, keepdims=True) for score in scores]
        )
        total = None
        for score, value_t in zip(scores, values_t):
            probs = jnp.exp(score - peak).astype(BFLOAT)
            row = lax.broadcasted_iota(jnp.int32, value_t.shape, 0)
            term = nn(jnp.where(row // HD == head, value_t, one), probs)
            total = term if total is None else total + term
        weight = total[HD * (1 - head) : HD * (1 - head) + 1, :]
        results.append(total[HD * head : HD * (head + 1), :] / weight)
        logs.append(peak + jnp.log(weight))
    out_ref[...] = jnp.concatenate(results, axis=0).T.astype(BFLOAT)
    log_ref[0] = jnp.concatenate(logs, axis=0)


def back_kernel(blocks, *refs):
    query_ref, out_ref, grad_ref, log_ref = refs[:4]
    ins = refs[4 : 4 + 3 * blocks]
    key_refs, value_refs, bias_refs = ins[0::3], ins[1::3], ins[2::3]
    query_grad_ref = refs[4 + 3 * blocks]
    pair_grad_refs = refs[5 + 3 * blocks :]
    queries = query_ref[...] * jnp.asarray(SCORE_SCALE, BFLOAT)
    out_grad = grad_ref[...]
    zero = jnp.zeros((1, 1), BFLOAT)
    one = jnp.ones((1, 1), BFLOAT)
    product = out_ref[...].astype(FLOAT) * out_grad.astype(FLOAT)
    chooser = (
        lax.broadcasted_iota(jnp.int32, (8, PAIR), 1) // HD
        == lax.broadcasted_iota(jnp.int32, (8, PAIR), 0)
    ).astype(FLOAT)
    inner = lax.dot_general(
        chooser, product, (((1,), (1,)), ((), ())), precision=PRECISE, preferred_element_type=FLOAT
    )
    keys_t = [ref[...].T for ref in key_refs]
    query_parts = [None, None]
    for block in range(blocks):
        key_grad, value_grad = None, None
        for head in range(2):
            grad_here = with_spare(out_grad, head, zero)
            score = nt(
                with_spare(key_refs[block][...], head, bias_refs[block][...]),
                with_spare(queries, head, one),
            )
            probs = jnp.exp(score - log_ref[0, head : head + 1, :])
            prob_grad = nt(value_refs[block][...], grad_here)
            score_grad = (probs * (prob_grad - inner[head : head + 1, :])).astype(BFLOAT)
            value_term = nn(probs.astype(BFLOAT), grad_here)
            key_term = nn(score_grad, with_spare(queries, head, zero))
            query_term = nn(keys_t[block][HD * head : HD * (head + 1), :], score_grad)
            value_grad = value_term if value_grad is None else value_grad + value_term
            key_grad = key_term if key_grad is None else key_grad + key_term
            query_parts[head] = (
                query_term if query_parts[head] is None else query_parts[head] + query_term
            )
        pair_grad_refs[block][0] = key_grad.astype(BFLOAT)
        pair_grad_refs[block][1] = value_grad.astype(BFLOAT)
    joined = jnp.concatenate(query_parts, axis=0) * SCORE_SCALE
    query_grad_ref[...] = joined.T.astype(BFLOAT)


def column_block(length):
    return pl.BlockSpec((length, PAIR), lambda pair: (0, pair))


def value_block(length):
    return pl.BlockSpec((length, PAIR), lambda pair: (0, pair + PAIRS))


def whole_block(shape):
    return pl.BlockSpec(shape, lambda pair: (0,) * len(shape))


def log_block(frames):
    return pl.BlockSpec((1, 2, frames), lambda pair: (pair, 0, 0))


def key_specs(key_values):
    specs, operands = [], []
    for joint, bias in key_values:
        length = joint.shape[0]
        specs += [column_block(length), value_block(length), whole_block((length, PAIR))]
        operands += [joint, joint, bias]
    return specs, operands


def attend(queries, key_values):
    frames, blocks = queries.shape[0], len(key_values)
    length = sum(joint.shape[0] for joint, _ in key_values)
    specs, operands = key_specs(key_values)
    return pl.pallas_call(
        functools.partial(attend_kernel, blocks),
        grid=(PAIRS,),
        in_specs=[column_block(frames)] + specs,
        out_specs=[column_block(frames), log_block(frames)],
        out_shape=[
            jax.ShapeDtypeStruct((frames, D), BFLOAT),
            jax.ShapeDtypeStruct((PAIRS, 2, frames), FLOAT),
        ],
        compiler_params=pltpu.CompilerParams(vmem_limit_bytes=48 * 1024 * 1024),
        cost_estimate=pl.CostEstimate(
            flops=16 * frames * length * D,
            bytes_accessed=4 * frames * D + 4 * length * D,
            transcendentals=12 * frames * length,
        ),
    )(queries, *operands)


def attend_back(queries, out, out_grad, logs, key_values):
    frames, blocks = queries.shape[0], len(key_values)
    length = sum(joint.shape[0] for joint, _ in key_values)
    specs, operands = key_specs(key_values)
    return pl.pallas_call(
        functools.partial(back_kernel, blocks),
        grid=(PAIRS,),
        in_specs=[column_block(frames)] * 3 + [log_block(frames)] + specs,
        out_specs=[column_block(frames)]
        + [
            pl.BlockSpec((2, joint.shape[0], PAIR), lambda pair: (0, 0, pair))
            for joint, _ in key_values
        ],
        out_shape=[jax.ShapeDtypeStruct((frames, D), BFLOAT)]
        + [jax.ShapeDtypeStruct((2, joint.shape[0], D), BFLOAT) for joint, _ in key_values],
        compiler_params=pltpu.CompilerParams(vmem_limit_bytes=48 * 1024 * 1024),
        cost_estimate=pl.CostEstimate(
            flops=40 * frames * length * D,
            bytes_accessed=8 * frames * D + 8 * length * D,
            transcendentals=12 * frames * length,
        ),
    )(queries, out, out_grad, logs, *operands)


def bias_of(allowed):
    column = jnp.where(allowed > 0, 0.0, MASKED_SCORE).astype(BFLOAT)
    return jnp.broadcast_to(column[:, None], (allowed.shape[0], PAIR))


def spread(piece, total_len, offset):
    return lax.dynamic_update_slice(jnp.zeros((total_len,), FLOAT), piece, (offset,))


def per_device(
    block_in,
    text,
    timesteps,
    frame_mask,
    text_mask,
    cotangent,
    w_ada,
    w_qkv,
    w_out,
    w_cq,
    w_cout,
    w_ckv,
    w_fc1,
    w_fc2,
    row_state,
    col_state,
):
    clips = lax.axis_size("dp")
    devices = clips * 2
    data_at = lax.axis_index("dp")
    head_at = lax.axis_index("head")
    flat_at = data_at * 2 + head_at
    frames = block_in.shape[1]
    rows = w_qkv.shape[0]

    mlp_shard = jnp.concatenate([w_fc1.astype(BFLOAT), w_fc2.T.astype(BFLOAT)], axis=0)
    mlp_all = lax.all_gather(mlp_shard, ALL, axis=0, tiled=False)
    query_out = gather_shard(
        jnp.concatenate([w_qkv[:, :D], w_out], axis=1).astype(BFLOAT), False, False
    ).reshape(D, 2 * D)
    w_key_value = gather_shard(w_qkv[:, D:].astype(BFLOAT), False, True).reshape(D, 2 * D)
    w_query, w_project = query_out[:, :D], query_out[:, D:]

    inputs = swap_place(block_in[0]).astype(FLOAT)
    out_grad = swap_place(cotangent[0]).astype(FLOAT)
    masks = from_clip_core(jnp.concatenate([frame_mask[0], text_mask[0]]))
    clip_text = from_clip_core(text[0])
    core_at = data_at % 2
    own_allowed = lax.dynamic_slice_in_dim(masks, core_at * frames, frames)
    other_allowed = lax.dynamic_slice_in_dim(masks, (1 - core_at) * frames, frames)
    own_bias, other_bias = bias_of(own_allowed), bias_of(other_allowed)
    text_bias = bias_of(masks[2 * frames :])

    steps = lax.dynamic_update_slice(jnp.zeros((clips,), jnp.int32), timesteps, (data_at,))
    for link in [core_link()] + far_links():
        steps = steps + cross(steps, link)
    condition = embed_part(steps, flat_at * rows, rows)
    modulation = jnp.dot(condition, w_ada.astype(BFLOAT), preferred_element_type=FLOAT)
    modulation = modulation.reshape(clips // 2, 2, 6 * D)
    kept = lax.dynamic_slice_in_dim(modulation, head_at, 1, axis=1)
    sent = lax.dynamic_slice_in_dim(modulation, 1 - head_at, 1, axis=1)
    modulation = (kept + cross(sent, row_link())).reshape(clips // 2, 6 * D)
    for link in far_links():
        bit = bit_of(link)
        halves = modulation.reshape(-1, 2, 6 * D)
        kept = lax.dynamic_slice_in_dim(halves, bit, 1, axis=1)
        sent = lax.dynamic_slice_in_dim(halves, 1 - bit, 1, axis=1)
        modulation = (kept + cross(sent, link)).reshape(-1, 6 * D)
    modulation = modulation + cross(modulation, core_link())
    shift_self, scale_self, gate_self, shift_mlp, scale_mlp, gate_mlp = jnp.split(
        modulation, 6, axis=-1
    )

    self_input = modulate(inputs, shift_self, scale_self).astype(BFLOAT)
    key_value = nn(self_input, w_key_value).astype(BFLOAT)
    query = nn(self_input, w_query).astype(BFLOAT)
    other_key_value = cross(key_value, core_link())

    cross_pair = gather_shard(
        jnp.concatenate([w_cq, w_cout], axis=1).astype(BFLOAT), False, False
    ).reshape(D, 2 * D)
    w_cross_query, w_cross_project = cross_pair[:, :D], cross_pair[:, D:]
    w_text = gather_shard(
        w_ckv.astype(BFLOAT).reshape(w_ckv.shape[0], D), True, True
    ).reshape(2, DT, D)

    self_keys = [(key_value, own_bias), (other_key_value, other_bias)]
    self_attn, self_logs = attend(query, self_keys)
    self_branch = nn(self_attn, w_project)
    after_self = inputs + gate_self * self_branch

    text_halves = jnp.einsum(
        "ld,hde->hle", clip_text, w_text, preferred_element_type=FLOAT
    ).astype(BFLOAT)
    text_pair = (
        text_halves.reshape(2, clip_text.shape[0], 2, D // 2)
        .transpose(1, 2, 0, 3)
        .reshape(clip_text.shape[0], 2 * D)
    )
    cross_input = layer_norm(after_self).astype(BFLOAT)
    cross_query = nn(cross_input, w_cross_query).astype(BFLOAT)
    text_keys = [(text_pair, text_bias)]
    cross_attn, cross_logs = attend(cross_query, text_keys)
    after_cross = after_self + nn(cross_attn, w_cross_project)

    mlp_input = modulate(after_cross, shift_mlp, scale_mlp).astype(BFLOAT)
    mlp_all = mlp_all.reshape(clips, 2, 2, rows * 2, HALF).transpose(2, 1, 0, 3, 4)
    fc1_halves, fc2_halves = mlp_all.reshape(2, 2, D, HALF)
    hidden_pre = jnp.einsum("fd,hdk->hfk", mlp_input, fc1_halves, preferred_element_type=FLOAT)
    hidden_act = jax.nn.gelu(hidden_pre).astype(BFLOAT)
    mlp_branch = jnp.einsum("hfk,hdk->fd", hidden_act, fc2_halves, preferred_element_type=FLOAT)
    block_out = swap_place((after_cross + gate_mlp * mlp_branch).astype(BFLOAT))

    gate_mlp_grad = jnp.sum(out_grad * mlp_branch, axis=0, keepdims=True)
    mlp_grad = (gate_mlp * out_grad).astype(BFLOAT)
    grad_fc2_part = jnp.einsum(
        "fd,hfk->hdk", mlp_grad, hidden_act, preferred_element_type=FLOAT
    ).astype(BFLOAT)
    act_grad = jnp.einsum("fd,hdk->hfk", mlp_grad, fc2_halves, preferred_element_type=FLOAT)
    gelu_back = jax.vjp(jax.nn.gelu, hidden_pre)[1]
    pre_grad = gelu_back(act_grad)[0].astype(BFLOAT)
    grad_fc1_part = jnp.einsum(
        "fd,hfk->hdk", mlp_input, pre_grad, preferred_element_type=FLOAT
    ).astype(BFLOAT)
    mlp_parts = jnp.stack([grad_fc1_part, grad_fc2_part]).reshape(2, 2, clips, rows * 2, HALF)
    mlp_raw = lax.psum_scatter(
        mlp_parts.transpose(2, 1, 0, 3, 4).reshape(devices, 2, rows * 2, HALF),
        ALL,
        scatter_dimension=0,
        tiled=False,
    ).astype(FLOAT)
    mlp_in_grad = jnp.einsum("hfk,hdk->fd", pre_grad, fc1_halves, preferred_element_type=FLOAT)
    mlp_back = jax.vjp(modulate, after_cross, shift_mlp, scale_mlp)[1]
    cross_res_grad, shift_mlp_grad, scale_mlp_grad = mlp_back(mlp_in_grad)
    cross_res_grad = out_grad + cross_res_grad

    cross_out_grad = cross_res_grad.astype(BFLOAT)
    grad_cout_part = jnp.einsum(
        "fd,fe->de", cross_attn, cross_out_grad, preferred_element_type=FLOAT
    ).astype(BFLOAT)
    cross_attn_grad = nt(cross_out_grad, w_cross_project).astype(BFLOAT)
    cross_query_grad, text_pair_grad = attend_back(
        cross_query, cross_attn, cross_attn_grad, cross_logs, text_keys
    )
    text_grad_halves = text_pair_grad.reshape(2, -1, 2, D // 2).transpose(2, 1, 0, 3)
    grad_ckv_part = jnp.einsum(
        "ld,hle->hde",
        clip_text,
        text_grad_halves.reshape(2, -1, D),
        preferred_element_type=FLOAT,
    ).astype(BFLOAT)
    grad_cq_part = jnp.einsum(
        "fd,fe->de", cross_input, cross_query_grad, preferred_element_type=FLOAT
    ).astype(BFLOAT)
    cross_raw = scatter_sum(
        split_rows(jnp.concatenate([grad_cq_part, grad_cout_part], axis=1)), False, False
    )
    ckv_raw = scatter_sum(split_halves(grad_ckv_part), True, True)
    cross_in_grad = nt(cross_query_grad, w_cross_query)
    norm_back = jax.vjp(layer_norm, after_self)[1]
    self_res_grad = cross_res_grad + norm_back(cross_in_grad)[0]

    gate_self_grad = jnp.sum(self_res_grad * self_branch, axis=0, keepdims=True)
    self_out_grad = (gate_self * self_res_grad).astype(BFLOAT)
    grad_out_part = jnp.einsum(
        "fd,fe->de", self_attn, self_out_grad, preferred_element_type=FLOAT
    ).astype(BFLOAT)
    self_attn_grad = nt(self_out_grad, w_project).astype(BFLOAT)
    query_grad, own_pair_grad, other_pair_grad = attend_back(
        query, self_attn, self_attn_grad, self_logs, self_keys
    )
    pair_grad = (
        own_pair_grad.astype(FLOAT) + cross(other_pair_grad, core_link()).astype(FLOAT)
    ).astype(BFLOAT)
    grad_query_part = jnp.einsum(
        "fd,fe->de", self_input, query_grad, preferred_element_type=FLOAT
    ).astype(BFLOAT)
    grad_pair_part = jnp.einsum(
        "fd,kfe->dke", self_input, pair_grad, preferred_element_type=FLOAT
    ).astype(BFLOAT)
    query_out_raw = scatter_sum(
        split_rows(jnp.concatenate([grad_query_part, grad_out_part], axis=1)), False, False
    )
    pair_raw = scatter_sum(split_rows(grad_pair_part.reshape(D, 2 * D)), False, True)
    in_grad_normed = nt(query_grad, w_query) + jnp.einsum(
        "kfe,dke->fd", pair_grad, w_key_value.reshape(D, 2, D), preferred_element_type=FLOAT
    )
    self_back = jax.vjp(modulate, inputs, shift_self, scale_self)[1]
    input_res_grad, shift_self_grad, scale_self_grad = self_back(in_grad_normed)
    input_grad = swap_place((self_res_grad + input_res_grad).astype(BFLOAT))

    modulation_grad = jnp.concatenate(
        [
            shift_self_grad,
            scale_self_grad,
            gate_self_grad,
            shift_mlp_grad,
            scale_mlp_grad,
            gate_mlp_grad,
        ],
        axis=-1,
    )
    modulation_grad = modulation_grad + cross(modulation_grad, core_link())
    modulation_grad = modulation_grad.reshape((1,) * dp_bits() + (6 * D,))
    for link in far_links()[::-1] + [row_link()]:
        other = cross(modulation_grad, link)
        upper = bit_of(link) == 1
        dim = dp_bits() - 1 if link[0] == "head" else dp_bits() - link[1].bit_length()
        modulation_grad = jnp.concatenate(
            [
                jnp.where(upper, other, modulation_grad),
                jnp.where(upper, modulation_grad, other),
            ],
            axis=dim,
        )
    ada_raw = jnp.einsum(
        "cr,cx->rx",
        condition.astype(FLOAT),
        modulation_grad.reshape(clips, 6 * D),
        precision=PRECISE,
    )

    qkv_raw = jnp.concatenate([query_out_raw[:, :D], pair_raw], axis=1)
    raw_grads = [
        ada_raw,
        qkv_raw,
        query_out_raw[:, D:],
        cross_raw[:, :D],
        cross_raw[:, D:],
        ckv_raw,
        mlp_raw[0],
        mlp_raw[1],
    ]
    masters = [
        w_ada,
        w_qkv,
        w_out,
        w_cq,
        w_cout,
        w_ckv.reshape(w_ckv.shape[0], D),
        w_fc1,
        w_fc2.T,
    ]
    full_rows = [D, D, D, D, D, DT, D, FF]
    full_cols = [6 * D, 3 * D, D, D, D, 2 * D, FF, D]
    squares = [grad * grad for grad in raw_grads]
    across = [jnp.sum(square, axis=1) for square in squares]
    down = [jnp.sum(square, axis=0) for square in squares]
    row_list = [spread(piece, D, flat_at * rows) for piece in across[:5]] + [
        spread(across[5], DT, data_at * across[5].shape[0]),
        spread(across[6], D, data_at * across[6].shape[0]),
        spread(down[7], FF, head_at * HALF),
    ]
    text_down = lax.dynamic_update_slice(
        jnp.zeros((2, D), FLOAT), down[5].reshape(2, D // 2), (0, head_at * (D // 2))
    )
    col_list = down[:5] + [
        text_down.reshape(-1),
        spread(down[6], FF, head_at * HALF),
        spread(across[7], D, data_at * across[7].shape[0]),
    ]
    weight_local = jnp.stack([jnp.sum(master * master) for master in masters])
    sums = sum_all(jnp.concatenate(row_list + col_list + [weight_local]))
    row_total, col_total = sum(full_rows), sum(full_cols)
    row_sums = sums[:row_total]
    col_sums = sums[row_total : row_total + col_total]
    weight_total = sums[row_total + col_total :]
    grad_norm = jnp.sqrt(jnp.sum(row_sums))
    factor = 1.0 / jnp.maximum(1.0, grad_norm / CLIP_NORM)
    row_divisor = jnp.concatenate(
        [
            jnp.full((rows_len,), float(cols_len), FLOAT)
            for rows_len, cols_len in zip(full_rows, full_cols)
        ]
    )
    col_divisor = jnp.concatenate(
        [
            jnp.full((cols_len,), float(rows_len), FLOAT)
            for rows_len, cols_len in zip(full_rows, full_cols)
        ]
    )
    square_factor = factor * factor
    row_new = DECAY_RATE * row_state + (1.0 - DECAY_RATE) * (
        square_factor * row_sums / row_divisor + EPS_FACTOR
    )
    col_new = DECAY_RATE * col_state + (1.0 - DECAY_RATE) * (
        square_factor * col_sums / col_divisor + EPS_FACTOR
    )
    clipped = [grad * factor for grad in raw_grads]
    updates = []
    row_at, col_at = (0, 0)
    for place, shard in enumerate(clipped):
        row_segment = row_new[row_at : row_at + full_rows[place]]
        col_segment = col_new[col_at : col_at + full_cols[place]]
        row_at = row_at + full_rows[place]
        col_at = col_at + full_cols[place]
        if place < 5:
            row_here = lax.dynamic_slice_in_dim(row_segment, flat_at * rows, rows)
            col_here = col_segment
        elif place == 5:
            length = shard.shape[0]
            row_here = lax.dynamic_slice_in_dim(row_segment, data_at * length, length)
            col_here = lax.dynamic_slice(
                col_segment.reshape(2, D), (0, head_at * (D // 2)), (2, D // 2)
            ).reshape(-1)
        elif place == 6:
            length = shard.shape[0]
            row_here = lax.dynamic_slice_in_dim(row_segment, data_at * length, length)
            col_here = lax.dynamic_slice_in_dim(col_segment, head_at * HALF, HALF)
        else:
            length = shard.shape[0]
            row_here = lax.dynamic_slice_in_dim(col_segment, data_at * length, length)
            col_here = lax.dynamic_slice_in_dim(row_segment, head_at * HALF, HALF)
        estimate = row_here[:, None] * col_here[None, :] / jnp.mean(row_segment)
        updates.append(shard * lax.rsqrt(estimate))
    update_total = sum_all(jnp.stack([jnp.sum(update * update) for update in updates]))
    entry_counts = jnp.array(
        [float(rows_len * cols_len) for rows_len, cols_len in zip(full_rows, full_cols)], FLOAT
    )
    limits = jnp.maximum(1.0, jnp.sqrt(update_total / entry_counts) / CLIP_UPDATE)
    rates = RELATIVE_RATE * jnp.maximum(SCALE_FLOOR, jnp.sqrt(weight_total / entry_counts))
    updated = [
        master - rates[place] * (update / limits[place])
        for place, (master, update) in enumerate(zip(masters, updates))
    ]
    clipped[5] = clipped[5].reshape(w_ckv.shape)
    updated[5] = updated[5].reshape(w_ckv.shape)
    clipped[7] = clipped[7].T
    updated[7] = updated[7].T
    return (
        block_out[None],
        input_grad[None],
        grad_norm,
        row_new,
        col_new,
        *clipped,
        *updated,
    )


def solution(mesh):
    return jax.shard_map(
        per_device,
        mesh=mesh,
        in_specs=(
            P("dp", "head", None),
            P("dp", None, None),
            P("dp"),
            P("dp", None),
            P("dp", None),
            P("dp", "head", None),
            P(("dp", "head"), None),
            P(("dp", "head"), None),
            P(("dp", "head"), None),
            P(("dp", "head"), None),
            P(("dp", "head"), None),
            P("dp", None, "head"),
            P("dp", "head"),
            P("head", "dp"),
            P(),
            P(),
        ),
        out_specs=(
            P("dp", "head", None),
            P("dp", "head", None),
            P(),
            P(),
            P(),
            P(("dp", "head"), None),
            P(("dp", "head"), None),
            P(("dp", "head"), None),
            P(("dp", "head"), None),
            P(("dp", "head"), None),
            P("dp", None, "head"),
            P("dp", "head"),
            P("head", "dp"),
            P(("dp", "head"), None),
            P(("dp", "head"), None),
            P(("dp", "head"), None),
            P(("dp", "head"), None),
            P(("dp", "head"), None),
            P("dp", None, "head"),
            P("dp", "head"),
            P("head", "dp"),
        ),
        check_vma=False,
    )
```

```python
import functools

import jax
import jax.numpy as jnp
from jax import lax
from jax.experimental import pallas as pl
from jax.experimental.pallas import tpu as pltpu
from jax.sharding import PartitionSpec as P

D = 768
FF = 3072
DT = 1024
HD = 64
HALF = FF // 2

PRECISE = lax.Precision.HIGHEST
FLOAT = jnp.float32
BFLOAT = jnp.bfloat16
EPS_NORM = 1e-06
EPS_FACTOR = 1e-30
CLIP_NORM = 1.0
CLIP_UPDATE = 0.25
DECAY_RATE = 0.5
RELATIVE_RATE = 4.0
SCALE_FLOOR = 0.001
SCORE_SCALE = 0.125
MASKED_SCORE = -1e30
ALL = ("dp", "head")
PAIR = 2 * HD
PAIRS = D // PAIR


def embed_part(steps, first, count):
    halfway = D // 2
    place = first + jnp.arange(count)
    freqs = jnp.exp(-jnp.log(10000.0) * (place % halfway).astype(FLOAT) / halfway)
    angles = steps.astype(FLOAT)[:, None] * freqs
    waves = jnp.where(place < halfway, jnp.cos(angles), jnp.sin(angles))
    return jax.nn.silu(waves).astype(BFLOAT)


def layer_norm(values):
    centered = values - jnp.mean(values, axis=-1, keepdims=True)
    variance = jnp.mean(centered * centered, axis=-1, keepdims=True)
    return centered * lax.rsqrt(variance + EPS_NORM)


def modulate(values, shift, scale):
    return layer_norm(values) * (1.0 + scale) + shift


def core_link():
    return ("dp", 1)


def row_link():
    return ("head", 1)


def far_links():
    masks, mask = [], 2
    while mask < lax.axis_size("dp"):
        masks.append(mask)
        mask = mask * 2
    return [("dp", mask) for mask in masks]


def dp_bits():
    return lax.axis_size("dp").bit_length() - 1


def bit_of(link):
    return (lax.axis_index(link[0]) // link[1]) % 2


def cross(values, link):
    pairs = [(place, place ^ link[1]) for place in range(lax.axis_size(link[0]))]
    return lax.ppermute(values, link[0], pairs)


def dim_of(link, head):
    if link[0] == "head":
        return {"first": 0, "last": dp_bits(), "columns": dp_bits() + 1}[head]
    return (1 if head == "first" else 0) + dp_bits() - link[1].bit_length()


def leading(head):
    return dp_bits() + (0 if head == "columns" else 1)


def grow(block, link, head):
    other = cross(block, link)
    upper = bit_of(link) == 1
    low = jnp.where(upper, other, block)
    high = jnp.where(upper, block, other)
    return jnp.concatenate([low, high], axis=dim_of(link, head))


def shrink(block, link, head, kind=BFLOAT):
    dim, bit = dim_of(link, head), bit_of(link)
    half = block.shape[dim] // 2
    kept = lax.dynamic_slice_in_dim(block, bit * half, half, axis=dim)
    sent = lax.dynamic_slice_in_dim(block, (1 - bit) * half, half, axis=dim)
    return (kept.astype(FLOAT) + cross(sent.astype(BFLOAT), link).astype(FLOAT)).astype(kind)


class Chain:
    def __init__(self, state, steps):
        self.state, self.steps = state, list(steps)

    def advance(self, count=1):
        for _ in range(min(count, len(self.steps))):
            self.state = self.steps.pop(0)(self.state)
        return self

    def finish(self):
        return self.advance(len(self.steps)).state


def tie(chains, *values):
    states, values = lax.optimization_barrier(([chain.state for chain in chains], values))
    for chain, state in zip(chains, states):
        chain.state = state
    return values


def gather_chain(shard, head, row_early):
    block = shard.reshape((1,) * leading(head) + shard.shape)
    far = far_links()
    plane = [row_link(), far[0]] if row_early else [far[0], row_link()]
    links = far[1:] + plane + [core_link()]
    return Chain(block, [lambda state, link=link: grow(state, link, head) for link in links])


def scatter_chain(matrix, head, row_early):
    bits = leading(head)
    rows, columns = matrix.shape[-2:]
    split = dp_bits() if head == "first" else bits
    block = matrix.reshape((2,) * bits + (rows // 2**split, columns))
    far = far_links()
    plane = [far[0], row_link()] if row_early else [row_link(), far[0]]
    order = [core_link()] + plane + far[:0:-1]
    kinds = [BFLOAT] * (len(order) - 1) + [FLOAT]
    steps = [
        lambda state, link=link, kind=kind: shrink(state, link, head, kind)
        for link, kind in zip(order, kinds)
    ]
    return Chain(block, steps + [lambda state: state.reshape(state.shape[bits:])])


def sum_all(values):
    for link in [core_link(), row_link()] + far_links():
        values = values + cross(values, link)
    return values


def on_own_chip():
    return bit_of(core_link()) == bit_of(row_link())


def swap_place(values):
    pairs = []
    for place in range(lax.axis_size("dp")):
        for head in range(2):
            if place & 1 != head:
                pairs.append((place * 2 + head, ((place & ~1) | head) * 2 + (place & 1)))
    return jnp.where(on_own_chip(), values, lax.ppermute(values, ALL, pairs))


def from_clip_core(values):
    pairs = []
    for place in range(0, lax.axis_size("dp"), 2):
        for head in range(2):
            pairs.append(((place + head) * 2 + head, (place + 1 - head) * 2 + head))
    return jnp.where(on_own_chip(), values, lax.ppermute(values, ALL, pairs))


def nt(left, right):
    return lax.dot_general(left, right, (((1,), (1,)), ((), ())), preferred_element_type=FLOAT)


def nn(left, right):
    return lax.dot_general(left, right, (((1,), (0,)), ((), ())), preferred_element_type=FLOAT)


def lanes_of(length):
    return lax.broadcasted_iota(jnp.int32, (length, PAIR), 1)


def with_spare(pair, head, spare):
    lane = lanes_of(pair.shape[0])
    rest = jnp.where(lane == HD * (1 - head), spare, jnp.zeros_like(pair))
    return jnp.where(lane // HD == head, pair, rest)


def attend_kernel(blocks, *refs):
    query_ref = refs[0]
    key_refs, value_refs, bias_refs = refs[1 : 1 + 3 * blocks : 3], refs[2 : 2 + 3 * blocks : 3], refs[3 : 3 + 3 * blocks : 3]
    out_ref, log_ref = refs[1 + 3 * blocks :]
    queries = query_ref[...] * jnp.asarray(SCORE_SCALE, BFLOAT)
    one = jnp.ones((1, 1), BFLOAT)
    values_t = [ref[...].T for ref in value_refs]
    results, logs = [], []
    for head in range(2):
        query = with_spare(queries, head, one)
        scores = [
            nt(with_spare(key_ref[...], head, bias_ref[...]), query)
            for key_ref, bias_ref in zip(key_refs, bias_refs)
        ]
        peak = functools.reduce(
            jnp.maximum, [jnp.max(score, axis=0, keepdims=True) for score in scores]
        )
        total = None
        for score, value_t in zip(scores, values_t):
            probs = jnp.exp(score - peak).astype(BFLOAT)
            row = lax.broadcasted_iota(jnp.int32, value_t.shape, 0)
            term = nn(jnp.where(row // HD == head, value_t, one), probs)
            total = term if total is None else total + term
        weight = total[HD * (1 - head) : HD * (1 - head) + 1, :]
        results.append(total[HD * head : HD * (head + 1), :] / weight)
        logs.append(peak + jnp.log(weight))
    out_ref[...] = jnp.concatenate(results, axis=0).T.astype(BFLOAT)
    log_ref[0] = jnp.concatenate(logs, axis=0)


def back_kernel(blocks, places, *refs):
    query_ref, out_ref, grad_ref, log_ref = refs[:4]
    ins = refs[4 : 4 + 3 * blocks]
    key_refs, value_refs, bias_refs = ins[0::3], ins[1::3], ins[2::3]
    query_grad_ref = refs[4 + 3 * blocks]
    pair_grad_refs = refs[5 + 3 * blocks :]
    queries = query_ref[...] * jnp.asarray(SCORE_SCALE, BFLOAT)
    out_grad = grad_ref[...]
    zero = jnp.zeros((1, 1), BFLOAT)
    one = jnp.ones((1, 1), BFLOAT)
    product = out_ref[...].astype(FLOAT) * out_grad.astype(FLOAT)
    chooser = (
        lax.broadcasted_iota(jnp.int32, (8, PAIR), 1) // HD
        == lax.broadcasted_iota(jnp.int32, (8, PAIR), 0)
    ).astype(FLOAT)
    inner = lax.dot_general(
        chooser, product, (((1,), (1,)), ((), ())), precision=PRECISE, preferred_element_type=FLOAT
    )
    keys_t = [ref[...].T for ref in key_refs]
    query_parts = [None, None]
    for block in range(blocks):
        key_grad, value_grad = None, None
        for head in range(2):
            grad_here = with_spare(out_grad, head, zero)
            score = nt(
                with_spare(key_refs[block][...], head, bias_refs[block][...]),
                with_spare(queries, head, one),
            )
            probs = jnp.exp(score - log_ref[0, head : head + 1, :])
            prob_grad = nt(value_refs[block][...], grad_here)
            score_grad = (probs * (prob_grad - inner[head : head + 1, :])).astype(BFLOAT)
            value_term = nn(probs.astype(BFLOAT), grad_here)
            key_term = nn(score_grad, with_spare(queries, head, zero))
            query_term = nn(keys_t[block][HD * head : HD * (head + 1), :], score_grad)
            value_grad = value_term if value_grad is None else value_grad + value_term
            key_grad = key_term if key_grad is None else key_grad + key_term
            query_parts[head] = (
                query_term if query_parts[head] is None else query_parts[head] + query_term
            )
        key_at, value_at = places(pl.program_id(0))
        key_at = pl.multiple_of(key_at * PAIR, PAIR)
        value_at = pl.multiple_of(value_at * PAIR, PAIR)
        pair_grad_refs[block][:, pl.ds(key_at, PAIR)] = key_grad.astype(BFLOAT)
        pair_grad_refs[block][:, pl.ds(value_at, PAIR)] = value_grad.astype(BFLOAT)
    joined = jnp.concatenate(query_parts, axis=0) * SCORE_SCALE
    query_grad_ref[...] = joined.T.astype(BFLOAT)


def column_block(length):
    return pl.BlockSpec((length, PAIR), lambda pair: (0, pair))


def plain_places(pair):
    return pair, pair + PAIRS


def half_places(pair):
    half, part = pair // (PAIRS // 2), pair % (PAIRS // 2)
    return half * PAIRS + part, half * PAIRS + PAIRS // 2 + part


def whole_block(shape):
    return pl.BlockSpec(shape, lambda pair: (0,) * len(shape))


def log_block(frames):
    return pl.BlockSpec((1, 2, frames), lambda pair: (pair, 0, 0))


def key_specs(key_values, places):
    specs, operands = [], []
    for joint, bias in key_values:
        length = joint.shape[0]
        specs += [
            pl.BlockSpec((length, PAIR), lambda pair: (0, places(pair)[0])),
            pl.BlockSpec((length, PAIR), lambda pair: (0, places(pair)[1])),
            whole_block((length, PAIR)),
        ]
        operands += [joint, joint, bias]
    return specs, operands


KERNEL = pltpu.CompilerParams(vmem_limit_bytes=48 * 1024 * 1024)
LIGHT = pl.CostEstimate(flops=1000, bytes_accessed=1000, transcendentals=0)


def attend(queries, key_values, places):
    frames, blocks = queries.shape[0], len(key_values)
    specs, operands = key_specs(key_values, places)
    return pl.pallas_call(
        functools.partial(attend_kernel, blocks),
        grid=(PAIRS,),
        in_specs=[column_block(frames)] + specs,
        out_specs=[column_block(frames), log_block(frames)],
        out_shape=[
            jax.ShapeDtypeStruct((frames, D), BFLOAT),
            jax.ShapeDtypeStruct((PAIRS, 2, frames), FLOAT),
        ],
        compiler_params=KERNEL,
        cost_estimate=LIGHT,
    )(queries, *operands)


def attend_back(queries, out, out_grad, logs, key_values, places):
    frames, blocks = queries.shape[0], len(key_values)
    specs, operands = key_specs(key_values, places)
    return pl.pallas_call(
        functools.partial(back_kernel, blocks, places),
        grid=(PAIRS,),
        in_specs=[column_block(frames)] * 3 + [log_block(frames)] + specs,
        out_specs=[column_block(frames)] + [whole_block(joint.shape) for joint, _ in key_values],
        out_shape=[jax.ShapeDtypeStruct((frames, D), BFLOAT)]
        + [jax.ShapeDtypeStruct(joint.shape, BFLOAT) for joint, _ in key_values],
        compiler_params=KERNEL,
        cost_estimate=LIGHT,
    )(queries, out, out_grad, logs, *operands)


def outer_kernel(*refs):
    out_ref, count = refs[-1], len(refs) // 2
    at = 0
    for place in range(count):
        left, right = refs[2 * place], refs[2 * place + 1]
        width = right.shape[1]
        product = lax.dot_general(
            left[...], right[...], (((0,), (0,)), ((), ())), preferred_element_type=FLOAT
        )
        out_ref[:, at : at + width] = product.astype(BFLOAT)
        at += width


def outer(*pairs):
    operands = [matrix for pair in pairs for matrix in pair]
    shape = (pairs[0][0].shape[1], sum(right.shape[1] for _, right in pairs))
    return pl.pallas_call(
        outer_kernel,
        out_shape=jax.ShapeDtypeStruct(shape, BFLOAT),
        compiler_params=KERNEL,
        cost_estimate=LIGHT,
    )(*operands)


def bias_of(allowed):
    column = jnp.where(allowed > 0, 0.0, MASKED_SCORE).astype(BFLOAT)
    return jnp.broadcast_to(column[:, None], (allowed.shape[0], PAIR))


LINE = 128
ROW_SIZES = [D, D, D, D, D, DT, D, FF]
COL_SIZES = [6 * D, 3 * D, D, D, D, 2 * D, FF, D]
ROW_LINES = sum(ROW_SIZES) // LINE
COL_LINES = sum(COL_SIZES) // LINE
STAT_LINES = ROW_LINES + COL_LINES + 2


def starts_of(sizes, first):
    starts = []
    for size in sizes:
        starts.append(first)
        first += size // LINE
    return starts


ROW_STARTS = starts_of(ROW_SIZES, 0)
COL_STARTS = starts_of(COL_SIZES, ROW_LINES)


def lines_at(line, shape):
    return lax.broadcasted_iota(jnp.int32, shape, 1) + line * LINE


def down_lines(column, offset, lines):
    shape = (column.shape[0], LINE)
    wanted = lax.broadcasted_iota(jnp.int32, shape, 0) + offset
    return [
        jnp.sum(jnp.where(lines_at(line, shape) == wanted, column, 0.0), axis=0, keepdims=True)
        for line in range(lines)
    ]


def from_lines(lines, offset, count):
    shape = (count, LINE)
    wanted = lax.broadcasted_iota(jnp.int32, shape, 0) + offset
    total = jnp.zeros(shape, FLOAT)
    for line in range(lines.shape[0]):
        here = jnp.where(lines_at(line, shape) == wanted, lines[line : line + 1, :], 0.0)
        total = total + here
    return jnp.sum(total, axis=1, keepdims=True)


def pieces_of(grad_refs):
    ada, query_out, key_value, cross_pair, text_pair, mlp = grad_refs
    return [
        [(ada, 0, 6 * D)],
        [(query_out, 0, D), (key_value, 0, 2 * D)],
        [(query_out, D, D)],
        [(cross_pair, 0, D)],
        [(cross_pair, D, D)],
        [(text_pair, 0, D)],
        [(mlp, 0, HALF)],
        [(mlp, HALF, HALF)],
    ]


def statistics_kernel(place_ref, weight_ref, *refs):
    grad_refs, out_ref = refs[:6], refs[6]
    data_at, head_at = place_ref[0], place_ref[1]
    flat_at = data_at * 2 + head_at
    out_ref[STAT_LINES - 2 : STAT_LINES - 1, :] = weight_ref[...]
    out_ref[STAT_LINES - 1 : STAT_LINES, :] = jnp.zeros((1, LINE), FLOAT)
    for place, parts in enumerate(pieces_of(grad_refs)):
        across, down = 0.0, []
        for ref, first, columns in parts:
            rows = ref.shape[0]
            wide = jnp.zeros((rows, LINE), FLOAT)
            for line in range(columns // LINE):
                piece = ref[:, first + line * LINE : first + (line + 1) * LINE]
                square = piece * piece
                wide = wide + square
                down.append(jnp.sum(square, axis=0, keepdims=True))
            across = across + jnp.sum(wide, axis=1, keepdims=True)
        offset = (flat_at if place < 5 else data_at) * rows
        row_start, col_start = ROW_STARTS[place], COL_STARTS[place]
        if place == 7:
            row_start, col_start = col_start, row_start
        row_lines = (COL_SIZES if place == 7 else ROW_SIZES)[place] // LINE
        for line, entry in enumerate(down_lines(across, offset, row_lines)):
            out_ref[row_start + line : row_start + line + 1, :] = entry
        groups = {5: 2}.get(place, 1)
        size = len(down) // groups
        for line, entry in enumerate(down):
            if place < 5:
                out_ref[col_start + line : col_start + line + 1, :] = entry
            else:
                for half in range(2):
                    at = col_start + (line // size * 2 + half) * size + line % size
                    out_ref[at : at + 1, :] = jnp.where(head_at == half, entry, 0.0)


def lane_of(lines, lane):
    shape = (1, LINE)
    here = lax.broadcasted_iota(jnp.int32, shape, 1) == lane
    return jnp.sum(jnp.where(here, lines, 0.0), axis=1, keepdims=True)


def update_kernel(place_ref, sums_ref, row_ref, col_ref, *refs):
    grad_refs, outs = refs[:6], refs[6:]
    row_out, col_out, norm_out, total_out = outs[:4]
    clipped_refs, update_refs = outs[4:12], outs[12:20]
    data_at, head_at = place_ref[0], place_ref[1]
    flat_at = data_at * 2 + head_at
    row_sums = sums_ref[0:ROW_LINES, :]
    square_total = jnp.sum(jnp.sum(row_sums, axis=0, keepdims=True), axis=1, keepdims=True)
    norm = jnp.sqrt(square_total)
    factor = 1.0 / jnp.maximum(1.0, norm / CLIP_NORM)
    norm_out[...] = jnp.broadcast_to(norm, (1, LINE))
    square_factor = factor * factor
    lane = lax.broadcasted_iota(jnp.int32, (1, LINE), 1)
    totals = jnp.zeros((1, LINE), FLOAT)
    for place, parts in enumerate(pieces_of(grad_refs)):
        rows_len, cols_len = ROW_SIZES[place], COL_SIZES[place]
        row_from, row_to = ROW_STARTS[place], ROW_STARTS[place] + rows_len // LINE
        col_from, col_to = COL_STARTS[place], COL_STARTS[place] + cols_len // LINE
        new_row = DECAY_RATE * row_ref[row_from:row_to, :] + (1.0 - DECAY_RATE) * (
            square_factor * sums_ref[row_from:row_to, :] / float(cols_len) + EPS_FACTOR
        )
        col_from, col_to = col_from - ROW_LINES, col_to - ROW_LINES
        new_col = DECAY_RATE * col_ref[col_from:col_to, :] + (1.0 - DECAY_RATE) * (
            square_factor
            * sums_ref[ROW_LINES + col_from : ROW_LINES + col_to, :]
            / float(rows_len)
            + EPS_FACTOR
        )
        row_out[row_from:row_to, :] = new_row
        col_out[col_from:col_to, :] = new_col
        row_mean = (
            jnp.sum(jnp.sum(new_row, axis=0, keepdims=True), axis=1, keepdims=True) / rows_len
        )
        rows = parts[0][0].shape[0]
        offset = (flat_at if place < 5 else data_at) * rows
        if place == 7:
            down = lax.rsqrt(from_lines(new_col, offset, rows))
            across = jnp.where(head_at == 0, new_row[:12], new_row[12:])
            across = lax.rsqrt(across / row_mean)
        else:
            down = lax.rsqrt(from_lines(new_row, offset, rows) / row_mean)
            if place == 5:
                keys = jnp.where(head_at == 0, new_col[0:3], new_col[3:6])
                values = jnp.where(head_at == 0, new_col[6:9], new_col[9:12])
                across = lax.rsqrt(jnp.concatenate([keys, values], axis=0))
            elif place == 6:
                across = lax.rsqrt(jnp.where(head_at == 0, new_col[:12], new_col[12:]))
            else:
                across = lax.rsqrt(new_col)
        square = jnp.zeros((rows, LINE), FLOAT)
        line_at = 0
        for ref, first, columns in parts:
            for line in range(columns // LINE):
                piece = ref[:, first + line * LINE : first + (line + 1) * LINE] * factor
                update = piece * (down * across[line_at : line_at + 1, :])
                clipped_refs[place][:, line_at * LINE : (line_at + 1) * LINE] = piece
                update_refs[place][:, line_at * LINE : (line_at + 1) * LINE] = update
                square = square + update * update
                line_at += 1
        total = jnp.sum(jnp.sum(square, axis=0, keepdims=True), axis=1, keepdims=True)
        totals = jnp.where(lane == place, total, totals)
    total_out[...] = totals


def apply_kernel(total_ref, weight_ref, *refs):
    for place in range(8):
        entries = float(ROW_SIZES[place] * COL_SIZES[place])
        total = lane_of(total_ref[...], place)
        weight = lane_of(weight_ref[...], place)
        limit = jnp.maximum(1.0, jnp.sqrt(total / entries) / CLIP_UPDATE)
        rate = RELATIVE_RATE * jnp.maximum(SCALE_FLOOR, jnp.sqrt(weight / entries))
        scale = rate / limit
        refs[16 + place][...] = refs[place][...] - scale * refs[8 + place][...]


def weight_kernel(*refs):
    lane = lax.broadcasted_iota(jnp.int32, (1, LINE), 1)
    totals = jnp.zeros((1, LINE), FLOAT)
    for place in range(8):
        matrix = refs[place][...]
        total = jnp.sum(jnp.sum(matrix * matrix, axis=0, keepdims=True), axis=1, keepdims=True)
        totals = jnp.where(lane == place, total, totals)
    refs[8][...] = totals


def whole_call(kernel, shapes, *operands, places=0):
    memory = [pl.BlockSpec(memory_space=pltpu.SMEM)] * places
    memory += [pl.BlockSpec(memory_space=pltpu.VMEM)] * (len(operands) - places)
    return pl.pallas_call(
        kernel,
        in_specs=memory,
        out_specs=[pl.BlockSpec(memory_space=pltpu.VMEM)] * len(shapes),
        out_shape=[jax.ShapeDtypeStruct(shape, FLOAT) for shape in shapes],
        compiler_params=KERNEL,
        cost_estimate=LIGHT,
    )(*operands)


def mlp_outer_kernel(input_ref, grad_ref, pre_ref, act_ref, out_ref):
    turn = (((0,), (0,)), ((), ()))
    width = pre_ref.shape[2]
    for at in range(0, width, D):
        first = lax.dot_general(
            input_ref[...], pre_ref[0, :, at : at + D], turn, preferred_element_type=FLOAT
        )
        out_ref[0, :, at : at + D] = first.astype(BFLOAT)
        second = lax.dot_general(
            grad_ref[...], act_ref[0, :, at : at + D], turn, preferred_element_type=FLOAT
        )
        out_ref[0, :, width + at : width + at + D] = second.astype(BFLOAT)


def mlp_outer(mlp_input, mlp_grad, pre_grad, hidden_act):
    frames, width = mlp_input.shape[0], pre_grad.shape[2]
    whole = pl.BlockSpec((frames, D), lambda half: (0, 0))
    hidden = pl.BlockSpec((1, frames, width), lambda half: (half, 0, 0))
    return pl.pallas_call(
        mlp_outer_kernel,
        grid=(2,),
        in_specs=[whole, whole, hidden, hidden],
        out_specs=pl.BlockSpec((1, D, 2 * width), lambda half: (half, 0, 0)),
        out_shape=jax.ShapeDtypeStruct((2, D, 2 * width), BFLOAT),
        compiler_params=KERNEL,
        cost_estimate=LIGHT,
    )(mlp_input, mlp_grad, pre_grad, hidden_act)


def per_device(
    block_in,
    text,
    timesteps,
    frame_mask,
    text_mask,
    cotangent,
    w_ada,
    w_qkv,
    w_out,
    w_cq,
    w_cout,
    w_ckv,
    w_fc1,
    w_fc2,
    row_state,
    col_state,
):
    clips = lax.axis_size("dp")
    devices = clips * 2
    data_at = lax.axis_index("dp")
    head_at = lax.axis_index("head")
    flat_at = data_at * 2 + head_at
    frames = block_in.shape[1]
    rows = w_qkv.shape[0]

    first = [
        gather_chain(
            jnp.concatenate([w_qkv[:, :D], w_out], axis=1).astype(BFLOAT), "last", False
        ),
        gather_chain(w_qkv[:, D:].astype(BFLOAT), "last", True),
    ]
    second = [
        gather_chain(jnp.concatenate([w_cq, w_cout], axis=1).astype(BFLOAT), "last", False),
        gather_chain(w_ckv.astype(BFLOAT).reshape(w_ckv.shape[0], D), "columns", True),
    ]
    masters = [
        w_ada,
        w_qkv,
        w_out,
        w_cq,
        w_cout,
        w_ckv.reshape(w_ckv.shape[0], D),
        w_fc1,
        w_fc2.T,
    ]
    mlp_shard = jnp.concatenate([w_fc1.astype(BFLOAT), w_fc2.T.astype(BFLOAT)], axis=1)
    mlp_all = lax.all_gather(mlp_shard, ("head", "dp"), axis=0, tiled=True)

    def add_step(link):
        return lambda state: state + cross(state, link)

    def project(steps):
        condition = embed_part(steps, flat_at * rows, rows)
        product = jnp.dot(condition, w_ada.astype(BFLOAT), preferred_element_type=FLOAT)
        return condition, product.reshape(clips // 2, 2, 6 * D)

    def keep_step(link):
        def step(state):
            condition, product = state
            bit = bit_of(link)
            product = product.reshape(-1, 2, 6 * D)
            kept = lax.dynamic_slice_in_dim(product, bit, 1, axis=1)
            sent = lax.dynamic_slice_in_dim(product, 1 - bit, 1, axis=1)
            return condition, (kept + cross(sent, link)).reshape(-1, 6 * D)

        return step

    def last_step(state):
        condition, product = state
        return condition, product + cross(product, core_link())

    steps = lax.dynamic_update_slice(jnp.zeros((clips,), jnp.int32), timesteps, (data_at,))
    timing = Chain(
        steps,
        [add_step(link) for link in [core_link()] + far_links()[1:] + far_links()[:1]]
        + [lambda steps: keep_step(row_link())(project(steps))]
        + [keep_step(link) for link in far_links()]
        + [last_step],
    )
    slots, far_count = len(first[0].steps), len(far_links()) - 1
    for slot in range(slots):
        timing.advance({0: 1 + far_count, 1: 3, 2: far_count, 3: 1}.get(slot, 0))
        for chain in first:
            chain.advance()
        if slot >= 2:
            for chain in second:
                chain.advance()
        if slot == 0:
            block_in, joint_mask, text = tie(
                [timing] + first,
                block_in,
                jnp.concatenate([frame_mask[0], text_mask[0]]),
                text,
            )
            inputs = swap_place(block_in[0])
            masks = from_clip_core(joint_mask)
            clip_text = from_clip_core(text[0])
        elif slot == 1:
            tie([timing] + first)
        elif slot < slots - 1:
            tie([timing] + first + second)
        else:
            masters = tie([timing] + first, *masters)
            (weight_squares,) = whole_call(weight_kernel, [(1, LINE)], *masters)
    condition, modulation = timing.finish()
    query_out, w_key_value = [chain.finish().reshape(D, 2 * D) for chain in first]
    w_query, w_project = query_out[:, :D], query_out[:, D:]

    inputs = inputs.astype(FLOAT)
    core_at = data_at % 2
    own_allowed = lax.dynamic_slice_in_dim(masks, core_at * frames, frames)
    other_allowed = lax.dynamic_slice_in_dim(masks, (1 - core_at) * frames, frames)
    own_bias, other_bias = bias_of(own_allowed), bias_of(other_allowed)
    text_bias = bias_of(masks[2 * frames :])
    shift_self, scale_self, gate_self, shift_mlp, scale_mlp, gate_mlp = jnp.split(
        modulation, 6, axis=-1
    )

    out_grad = swap_place(cotangent[0])
    self_input = modulate(inputs, shift_self, scale_self).astype(BFLOAT)
    key_value = nn(self_input, w_key_value).astype(BFLOAT)
    query = nn(self_input, w_query).astype(BFLOAT)
    other_key_value = cross(key_value, core_link())
    for chain in second:
        chain.advance()
    query, other_key_value = tie(second, query, other_key_value)
    cross_pair, w_text = [chain.finish() for chain in second]
    cross_pair, w_text = cross_pair.reshape(D, 2 * D), w_text.reshape(DT, 2 * D)
    w_cross_query, w_cross_project = cross_pair[:, :D], cross_pair[:, D:]

    self_keys = [(key_value, own_bias), (other_key_value, other_bias)]
    self_attn, self_logs = attend(query, self_keys, plain_places)
    self_branch = nn(self_attn, w_project)
    after_self = inputs + gate_self * self_branch

    text_pair = nn(clip_text, w_text).astype(BFLOAT)
    cross_input = layer_norm(after_self).astype(BFLOAT)
    cross_query = nn(cross_input, w_cross_query).astype(BFLOAT)
    text_keys = [(text_pair, text_bias)]
    cross_attn, cross_logs = attend(cross_query, text_keys, half_places)
    after_cross = after_self + nn(cross_attn, w_cross_project)

    mlp_input = modulate(after_cross, shift_mlp, scale_mlp).astype(BFLOAT)
    mlp_input, out_grad = tie([], mlp_input, out_grad)
    out_grad = out_grad.astype(FLOAT)
    mlp_all = mlp_all.reshape(2, D, 2 * HALF)
    fc1_halves, fc2_halves = mlp_all[:, :, :HALF], mlp_all[:, :, HALF:]
    hidden_pre = jnp.einsum("fd,hdk->hfk", mlp_input, fc1_halves, preferred_element_type=FLOAT)
    hidden_act = jax.nn.gelu(hidden_pre).astype(BFLOAT)
    mlp_grad = (gate_mlp * out_grad).astype(BFLOAT)
    act_grad = jnp.einsum("fd,hdk->hfk", mlp_grad, fc2_halves, preferred_element_type=FLOAT)
    gelu_back = jax.vjp(jax.nn.gelu, hidden_pre)[1]
    pre_grad = gelu_back(act_grad)[0].astype(BFLOAT)
    mlp_part = mlp_outer(mlp_input, mlp_grad, pre_grad, hidden_act)
    mlp_part, hidden_act, pre_grad = tie([], mlp_part, hidden_act, pre_grad)
    mlp_raw = lax.psum_scatter(
        mlp_part.reshape(2 * D, 2 * HALF), ("head", "dp"), scatter_dimension=0, tiled=True
    ).astype(FLOAT)

    mlp_branch = jnp.einsum("hfk,hdk->fd", hidden_act, fc2_halves, preferred_element_type=FLOAT)
    block_out = (after_cross + gate_mlp * mlp_branch).astype(BFLOAT)
    gate_mlp_grad = jnp.sum(out_grad * mlp_branch, axis=0, keepdims=True)
    mlp_in_grad = jnp.einsum("hfk,hdk->fd", pre_grad, fc1_halves, preferred_element_type=FLOAT)
    mlp_back = jax.vjp(modulate, after_cross, shift_mlp, scale_mlp)[1]
    cross_res_grad, shift_mlp_grad, scale_mlp_grad = mlp_back(mlp_in_grad)
    cross_res_grad = out_grad + cross_res_grad
    cross_res_grad, block_out, gate_mlp_grad = tie([], cross_res_grad, block_out, gate_mlp_grad)

    cross_out_grad = cross_res_grad.astype(BFLOAT)
    cross_attn_grad = nt(cross_out_grad, w_cross_project).astype(BFLOAT)
    cross_query_grad, text_pair_grad = attend_back(
        cross_query, cross_attn, cross_attn_grad, cross_logs, text_keys, half_places
    )
    cross_chains = [
        scatter_chain(
            outer((cross_input, cross_query_grad), (cross_attn, cross_out_grad)), "last", False
        ),
        scatter_chain(outer((clip_text, text_pair_grad)), "columns", True),
    ]
    (cross_query_grad,) = tie(cross_chains, cross_query_grad)
    for chain in cross_chains:
        chain.advance()
    cross_in_grad = nt(cross_query_grad, w_cross_query)
    norm_back = jax.vjp(layer_norm, after_self)[1]
    self_res_grad = cross_res_grad + norm_back(cross_in_grad)[0]

    gate_self_grad = jnp.sum(self_res_grad * self_branch, axis=0, keepdims=True)
    self_out_grad = (gate_self * self_res_grad).astype(BFLOAT)
    self_attn_grad = nt(self_out_grad, w_project).astype(BFLOAT)
    self_attn_grad, self_out_grad = tie(cross_chains, self_attn_grad, self_out_grad)
    for chain in cross_chains:
        chain.advance()
    query_grad, own_pair_grad, other_pair_grad = attend_back(
        query, self_attn, self_attn_grad, self_logs, self_keys, plain_places
    )
    query_grad, own_pair_grad, other_pair_grad = tie(
        cross_chains, query_grad, own_pair_grad, other_pair_grad
    )
    for chain in cross_chains:
        chain.advance()
    pair_grad = (
        own_pair_grad.astype(FLOAT) + cross(other_pair_grad, core_link()).astype(FLOAT)
    ).astype(BFLOAT)
    last_chains = [
        scatter_chain(
            outer((self_input, query_grad), (self_attn, self_out_grad)), "last", False
        ),
        scatter_chain(outer((self_input, pair_grad)), "last", True),
    ]
    query_grad, pair_grad = tie(cross_chains + last_chains, query_grad, pair_grad)
    for chain in cross_chains + last_chains:
        chain.advance()
    in_grad_normed = nt(query_grad, w_query) + nt(pair_grad, w_key_value)
    self_back = jax.vjp(modulate, inputs, shift_self, scale_self)[1]
    input_res_grad, shift_self_grad, scale_self_grad = self_back(in_grad_normed)
    input_grad = (self_res_grad + input_res_grad).astype(BFLOAT)
    input_grad, shift_self_grad, scale_self_grad = tie(
        cross_chains + last_chains, input_grad, shift_self_grad, scale_self_grad
    )
    for chain in cross_chains + last_chains:
        chain.advance()

    modulation_grad = jnp.concatenate(
        [
            shift_self_grad,
            scale_self_grad,
            gate_self_grad,
            shift_mlp_grad,
            scale_mlp_grad,
            gate_mlp_grad,
        ],
        axis=-1,
    )
    modulation_grad = modulation_grad + cross(modulation_grad, core_link())
    modulation_grad, block_out, input_grad = tie(
        cross_chains + last_chains, modulation_grad, block_out, input_grad
    )
    block_out, input_grad = swap_place(jnp.stack([block_out, input_grad]))
    modulation_grad = modulation_grad.reshape((1,) * dp_bits() + (6 * D,))
    for link in far_links()[::-1] + [row_link()]:
        other = cross(modulation_grad, link)
        upper = bit_of(link) == 1
        dim = dp_bits() - 1 if link[0] == "head" else dp_bits() - link[1].bit_length()
        modulation_grad = jnp.concatenate(
            [
                jnp.where(upper, other, modulation_grad),
                jnp.where(upper, modulation_grad, other),
            ],
            axis=dim,
        )
    ada_raw = jnp.einsum(
        "cr,cx->rx",
        condition.astype(FLOAT),
        modulation_grad.reshape(clips, 6 * D),
        precision=PRECISE,
    )

    cross_raw, ckv_raw = [chain.finish() for chain in cross_chains]
    query_out_raw, pair_raw = [chain.finish() for chain in last_chains]

    place = jnp.stack([data_at, head_at]).astype(jnp.int32)
    raw_grads = [ada_raw, query_out_raw, pair_raw, cross_raw, ckv_raw, mlp_raw]
    (statistics,) = whole_call(
        statistics_kernel, [(STAT_LINES, LINE)], place, weight_squares, *raw_grads, places=1
    )
    sums = sum_all(statistics)
    shapes = [master.shape for master in masters]
    line = (1, LINE)
    row_new, col_new, norm, update_squares, *rest = whole_call(
        update_kernel,
        [(ROW_LINES, LINE), (COL_LINES, LINE), line, line] + shapes + shapes,
        place,
        sums,
        row_state.reshape(ROW_LINES, LINE),
        col_state.reshape(COL_LINES, LINE),
        *raw_grads,
        places=1,
    )
    clipped, updates = list(rest[:8]), rest[8:]
    updated = whole_call(
        apply_kernel,
        shapes,
        sum_all(update_squares),
        sums[STAT_LINES - 2 : STAT_LINES - 1],
        *masters,
        *updates,
    )
    updated = list(updated)
    clipped[5] = clipped[5].reshape(w_ckv.shape)
    updated[5] = updated[5].reshape(w_ckv.shape)
    clipped[7] = clipped[7].T
    updated[7] = updated[7].T
    return (
        block_out[None],
        input_grad[None],
        norm[0, 0],
        row_new.reshape(-1),
        col_new.reshape(-1),
        *clipped,
        *updated,
    )


def solution(mesh):
    return jax.shard_map(
        per_device,
        mesh=mesh,
        in_specs=(
            P("dp", "head", None),
            P("dp", None, None),
            P("dp"),
            P("dp", None),
            P("dp", None),
            P("dp", "head", None),
            P(("dp", "head"), None),
            P(("dp", "head"), None),
            P(("dp", "head"), None),
            P(("dp", "head"), None),
            P(("dp", "head"), None),
            P("dp", None, "head"),
            P("dp", "head"),
            P("head", "dp"),
            P(),
            P(),
        ),
        out_specs=(
            P("dp", "head", None),
            P("dp", "head", None),
            P(),
            P(),
            P(),
            P(("dp", "head"), None),
            P(("dp", "head"), None),
            P(("dp", "head"), None),
            P(("dp", "head"), None),
            P(("dp", "head"), None),
            P("dp", None, "head"),
            P("dp", "head"),
            P("head", "dp"),
            P(("dp", "head"), None),
            P(("dp", "head"), None),
            P(("dp", "head"), None),
            P(("dp", "head"), None),
            P(("dp", "head"), None),
            P("dp", None, "head"),
            P("dp", "head"),
            P("head", "dp"),
        ),
        check_vma=False,
    )
```

```python
import functools

import jax
import jax.numpy as jnp
from jax import lax
from jax.experimental import pallas as pl
from jax.experimental.pallas import tpu as pltpu
from jax.sharding import PartitionSpec as P

D = 768
FF = 3072
DT = 1024
HD = 64
HALF = FF // 2

PRECISE = lax.Precision.HIGHEST
FLOAT = jnp.float32
BFLOAT = jnp.bfloat16
EPS_NORM = 1e-06
EPS_FACTOR = 1e-30
CLIP_NORM = 1.0
CLIP_UPDATE = 0.25
DECAY_RATE = 0.5
RELATIVE_RATE = 4.0
SCALE_FLOOR = 0.001
SCORE_SCALE = 0.125
MASKED_SCORE = -1e30
DP = ("far", "near", "core")
ALL = DP + ("head",)
HEAD = ("head",)
PAIR = 2 * HD
PAIRS = D // PAIR


def embed_part(steps, first, count):
    halfway = D // 2
    place = first + jnp.arange(count)
    freqs = jnp.exp(-jnp.log(10000.0) * (place % halfway).astype(FLOAT) / halfway)
    angles = steps.astype(FLOAT)[:, None] * freqs
    waves = jnp.where(place < halfway, jnp.cos(angles), jnp.sin(angles))
    return jax.nn.silu(waves).astype(BFLOAT)


def layer_norm(values):
    centered = values - jnp.mean(values, axis=-1, keepdims=True)
    variance = jnp.mean(centered * centered, axis=-1, keepdims=True)
    return centered * lax.rsqrt(variance + EPS_NORM)


def modulate(values, shift, scale):
    return layer_norm(values) * (1.0 + scale) + shift


def core_link():
    return (DP, 1)


def row_link():
    return (HEAD, 1)


def far_links():
    masks, mask = [], 2
    while mask < lax.axis_size(DP):
        masks.append(mask)
        mask = mask * 2
    return [(DP, mask) for mask in masks]


def dp_bits():
    return lax.axis_size(DP).bit_length() - 1


def bit_of(link):
    return (lax.axis_index(link[0]) // link[1]) % 2


def cross(values, link):
    pairs = [(place, place ^ link[1]) for place in range(lax.axis_size(link[0]))]
    return lax.ppermute(values, link[0], pairs)


def dim_of(link, head):
    if link[0] == HEAD:
        return {"first": 0, "last": dp_bits(), "columns": dp_bits() + 1}[head]
    return (1 if head == "first" else 0) + dp_bits() - link[1].bit_length()


def leading(head):
    return dp_bits() + (0 if head == "columns" else 1)


def grow(block, link, head):
    other = cross(block, link)
    upper = bit_of(link) == 1
    low = jnp.where(upper, other, block)
    high = jnp.where(upper, block, other)
    return jnp.concatenate([low, high], axis=dim_of(link, head))


def shrink(block, link, head, kind=BFLOAT):
    dim, bit = dim_of(link, head), bit_of(link)
    half = block.shape[dim] // 2
    kept = lax.dynamic_slice_in_dim(block, bit * half, half, axis=dim)
    sent = lax.dynamic_slice_in_dim(block, (1 - bit) * half, half, axis=dim)
    return (kept.astype(FLOAT) + cross(sent.astype(BFLOAT), link).astype(FLOAT)).astype(kind)


class Chain:
    def __init__(self, state, steps):
        self.state, self.steps = state, list(steps)

    def advance(self, count=1):
        for _ in range(min(count, len(self.steps))):
            self.state = self.steps.pop(0)(self.state)
        return self

    def finish(self):
        return self.advance(len(self.steps)).state


def tie(chains, *values):
    states, values = lax.optimization_barrier(([chain.state for chain in chains], values))
    for chain, state in zip(chains, states):
        chain.state = state
    return values


def gather_chain(block, head, links):
    return Chain(block, [lambda state, link=link: grow(state, link, head) for link in links])


def with_bits(shard, head):
    return shard.reshape((1,) * leading(head) + shard.shape)


def scatter_chain(matrix, head, row_early):
    bits = leading(head)
    rows, columns = matrix.shape[-2:]
    split = dp_bits() if head == "first" else bits
    block = matrix.reshape((2,) * bits + (rows // 2**split, columns))
    far = far_links()
    plane = [far[0], row_link()] if row_early else [row_link(), far[0]]
    order = [core_link()] + plane + far[:0:-1]
    kinds = [BFLOAT] * (len(order) - 1) + [FLOAT]
    steps = [
        lambda state, link=link, kind=kind: shrink(state, link, head, kind)
        for link, kind in zip(order, kinds)
    ]
    return Chain(block, steps + [lambda state: state.reshape(state.shape[bits:])])


def sum_all(values):
    for link in [core_link(), row_link()] + far_links():
        values = values + cross(values, link)
    return values


def on_own_chip():
    return bit_of(core_link()) == bit_of(row_link())


def swap_only(values):
    pairs = []
    for place in range(lax.axis_size(DP)):
        for head in range(2):
            if place & 1 != head:
                pairs.append((place * 2 + head, ((place & ~1) | head) * 2 + (place & 1)))
    return lax.ppermute(values, ALL, pairs)


def swap_place(values):
    return jnp.where(on_own_chip(), values, swap_only(values))


def from_clip_core(values):
    pairs = []
    for place in range(0, lax.axis_size(DP), 2):
        for head in range(2):
            pairs.append(((place + head) * 2 + head, (place + 1 - head) * 2 + head))
    return jnp.where(on_own_chip(), values, lax.ppermute(values, ALL, pairs))


def nt(left, right):
    return lax.dot_general(left, right, (((1,), (1,)), ((), ())), preferred_element_type=FLOAT)


def nn(left, right):
    return lax.dot_general(left, right, (((1,), (0,)), ((), ())), preferred_element_type=FLOAT)


def lanes_of(length):
    return lax.broadcasted_iota(jnp.int32, (length, PAIR), 1)


def with_spare(pair, head, spare):
    lane = lanes_of(pair.shape[0])
    rest = jnp.where(lane == HD * (1 - head), spare, jnp.zeros_like(pair))
    return jnp.where(lane // HD == head, pair, rest)


def attend_kernel(blocks, *refs):
    query_ref = refs[0]
    key_refs, value_refs, bias_refs = refs[1 : 1 + 3 * blocks : 3], refs[2 : 2 + 3 * blocks : 3], refs[3 : 3 + 3 * blocks : 3]
    out_ref, log_ref = refs[1 + 3 * blocks :]
    queries = query_ref[...] * jnp.asarray(SCORE_SCALE, BFLOAT)
    one = jnp.ones((1, 1), BFLOAT)
    values_t = [ref[...].T for ref in value_refs]
    results, logs = [], []
    for head in range(2):
        query = with_spare(queries, head, one)
        scores = [
            nt(with_spare(key_ref[...], head, bias_ref[...]), query)
            for key_ref, bias_ref in zip(key_refs, bias_refs)
        ]
        peak = functools.reduce(
            jnp.maximum, [jnp.max(score, axis=0, keepdims=True) for score in scores]
        )
        total = None
        for score, value_t in zip(scores, values_t):
            probs = jnp.exp(score - peak).astype(BFLOAT)
            row = lax.broadcasted_iota(jnp.int32, value_t.shape, 0)
            term = nn(jnp.where(row // HD == head, value_t, one), probs)
            total = term if total is None else total + term
        weight = total[HD * (1 - head) : HD * (1 - head) + 1, :]
        results.append(total[HD * head : HD * (head + 1), :] / weight)
        logs.append(peak + jnp.log(weight))
    out_ref[...] = jnp.concatenate(results, axis=0).T.astype(BFLOAT)
    log_ref[0] = jnp.concatenate(logs, axis=0)


def back_kernel(blocks, places, *refs):
    query_ref, out_ref, grad_ref, log_ref = refs[:4]
    ins = refs[4 : 4 + 3 * blocks]
    key_refs, value_refs, bias_refs = ins[0::3], ins[1::3], ins[2::3]
    query_grad_ref = refs[4 + 3 * blocks]
    pair_grad_refs = refs[5 + 3 * blocks :]
    queries = query_ref[...] * jnp.asarray(SCORE_SCALE, BFLOAT)
    out_grad = grad_ref[...]
    zero = jnp.zeros((1, 1), BFLOAT)
    one = jnp.ones((1, 1), BFLOAT)
    product = out_ref[...].astype(FLOAT) * out_grad.astype(FLOAT)
    chooser = (
        lax.broadcasted_iota(jnp.int32, (8, PAIR), 1) // HD
        == lax.broadcasted_iota(jnp.int32, (8, PAIR), 0)
    ).astype(FLOAT)
    inner = lax.dot_general(
        chooser, product, (((1,), (1,)), ((), ())), precision=PRECISE, preferred_element_type=FLOAT
    )
    keys_t = [ref[...].T for ref in key_refs]
    query_parts = [None, None]
    for block in range(blocks):
        key_grad, value_grad = None, None
        for head in range(2):
            grad_here = with_spare(out_grad, head, zero)
            score = nt(
                with_spare(key_refs[block][...], head, bias_refs[block][...]),
                with_spare(queries, head, one),
            )
            probs = jnp.exp(score - log_ref[0, head : head + 1, :])
            prob_grad = nt(value_refs[block][...], grad_here)
            score_grad = (probs * (prob_grad - inner[head : head + 1, :])).astype(BFLOAT)
            value_term = nn(probs.astype(BFLOAT), grad_here)
            key_term = nn(score_grad, with_spare(queries, head, zero))
            query_term = nn(keys_t[block][HD * head : HD * (head + 1), :], score_grad)
            value_grad = value_term if value_grad is None else value_grad + value_term
            key_grad = key_term if key_grad is None else key_grad + key_term
            query_parts[head] = (
                query_term if query_parts[head] is None else query_parts[head] + query_term
            )
        key_at, value_at = places(pl.program_id(0))
        key_at = pl.multiple_of(key_at * PAIR, PAIR)
        value_at = pl.multiple_of(value_at * PAIR, PAIR)
        pair_grad_refs[block][:, pl.ds(key_at, PAIR)] = key_grad.astype(BFLOAT)
        pair_grad_refs[block][:, pl.ds(value_at, PAIR)] = value_grad.astype(BFLOAT)
    joined = jnp.concatenate(query_parts, axis=0) * SCORE_SCALE
    query_grad_ref[...] = joined.T.astype(BFLOAT)


def column_block(length):
    return pl.BlockSpec((length, PAIR), lambda pair: (0, pair))


def plain_places(pair):
    return pair, pair + PAIRS


def half_places(pair):
    half, part = pair // (PAIRS // 2), pair % (PAIRS // 2)
    return half * PAIRS + part, half * PAIRS + PAIRS // 2 + part


def whole_block(shape):
    return pl.BlockSpec(shape, lambda pair: (0,) * len(shape))


def log_block(frames):
    return pl.BlockSpec((1, 2, frames), lambda pair: (pair, 0, 0))


def key_specs(key_values, places):
    specs, operands = [], []
    for joint, bias in key_values:
        length = joint.shape[0]
        specs += [
            pl.BlockSpec((length, PAIR), lambda pair: (0, places(pair)[0])),
            pl.BlockSpec((length, PAIR), lambda pair: (0, places(pair)[1])),
            whole_block((length, PAIR)),
        ]
        operands += [joint, joint, bias]
    return specs, operands


KERNEL = pltpu.CompilerParams(vmem_limit_bytes=48 * 1024 * 1024)
LIGHT = pl.CostEstimate(flops=1000, bytes_accessed=1000, transcendentals=0)


def attend(queries, key_values, places):
    frames, blocks = queries.shape[0], len(key_values)
    specs, operands = key_specs(key_values, places)
    return pl.pallas_call(
        functools.partial(attend_kernel, blocks),
        grid=(PAIRS,),
        in_specs=[column_block(frames)] + specs,
        out_specs=[column_block(frames), log_block(frames)],
        out_shape=[
            jax.ShapeDtypeStruct((frames, D), BFLOAT),
            jax.ShapeDtypeStruct((PAIRS, 2, frames), FLOAT),
        ],
        compiler_params=KERNEL,
        cost_estimate=LIGHT,
    )(queries, *operands)


def attend_back(queries, out, out_grad, logs, key_values, places):
    frames, blocks = queries.shape[0], len(key_values)
    specs, operands = key_specs(key_values, places)
    return pl.pallas_call(
        functools.partial(back_kernel, blocks, places),
        grid=(PAIRS,),
        in_specs=[column_block(frames)] * 3 + [log_block(frames)] + specs,
        out_specs=[column_block(frames)] + [whole_block(joint.shape) for joint, _ in key_values],
        out_shape=[jax.ShapeDtypeStruct((frames, D), BFLOAT)]
        + [jax.ShapeDtypeStruct(joint.shape, BFLOAT) for joint, _ in key_values],
        compiler_params=KERNEL,
        cost_estimate=LIGHT,
    )(queries, out, out_grad, logs, *operands)


def outer_kernel(*refs):
    out_ref, count = refs[-1], len(refs) // 2
    at = 0
    for place in range(count):
        left, right = refs[2 * place], refs[2 * place + 1]
        width = right.shape[1]
        product = lax.dot_general(
            left[...], right[...], (((0,), (0,)), ((), ())), preferred_element_type=FLOAT
        )
        out_ref[:, at : at + width] = product.astype(BFLOAT)
        at += width


def outer(*pairs):
    operands = [matrix for pair in pairs for matrix in pair]
    shape = (pairs[0][0].shape[1], sum(right.shape[1] for _, right in pairs))
    return pl.pallas_call(
        outer_kernel,
        out_shape=jax.ShapeDtypeStruct(shape, BFLOAT),
        compiler_params=KERNEL,
        cost_estimate=LIGHT,
    )(*operands)


def bias_of(allowed):
    column = jnp.where(allowed > 0, 0.0, MASKED_SCORE).astype(BFLOAT)
    return jnp.broadcast_to(column[:, None], (allowed.shape[0], PAIR))


LINE = 128
ROW_SIZES = [D, D, D, D, D, DT, D, FF]
COL_SIZES = [6 * D, 3 * D, D, D, D, 2 * D, FF, D]
ROW_LINES = sum(ROW_SIZES) // LINE
COL_LINES = sum(COL_SIZES) // LINE
STAT_LINES = ROW_LINES + COL_LINES + 2


def starts_of(sizes, first):
    starts = []
    for size in sizes:
        starts.append(first)
        first += size // LINE
    return starts


ROW_STARTS = starts_of(ROW_SIZES, 0)
COL_STARTS = starts_of(COL_SIZES, ROW_LINES)


def lines_at(line, shape):
    return lax.broadcasted_iota(jnp.int32, shape, 1) + line * LINE


def down_lines(column, offset, lines):
    shape = (column.shape[0], LINE)
    wanted = lax.broadcasted_iota(jnp.int32, shape, 0) + offset
    return [
        jnp.sum(jnp.where(lines_at(line, shape) == wanted, column, 0.0), axis=0, keepdims=True)
        for line in range(lines)
    ]


def from_lines(lines, offset, count):
    shape = (count, LINE)
    wanted = lax.broadcasted_iota(jnp.int32, shape, 0) + offset
    total = jnp.zeros(shape, FLOAT)
    for line in range(lines.shape[0]):
        here = jnp.where(lines_at(line, shape) == wanted, lines[line : line + 1, :], 0.0)
        total = total + here
    return jnp.sum(total, axis=1, keepdims=True)


def pieces_of(grad_refs):
    ada, query_out, key_value, cross_pair, text_pair, mlp = grad_refs
    return [
        [(ada, 0, 6 * D)],
        [(query_out, 0, D), (key_value, 0, 2 * D)],
        [(query_out, D, D)],
        [(cross_pair, 0, D)],
        [(cross_pair, D, D)],
        [(text_pair, 0, D)],
        [(mlp.at[0], 0, HALF)],
        [(mlp.at[1], 0, HALF)],
    ]


def joined_pieces(refs):
    square, text_pair, mlp = refs
    parts, at = [], 0
    for place in range(5):
        parts.append((square, at, COL_SIZES[place]))
        at += COL_SIZES[place]
    return parts + [(text_pair, 0, D), (mlp, 0, HALF), (mlp, HALF, HALF)]


def statistics_kernel(place_ref, weight_ref, *refs):
    grad_refs, out_ref = refs[:6], refs[6]
    data_at, head_at = place_ref[0], place_ref[1]
    flat_at = data_at * 2 + head_at
    out_ref[STAT_LINES - 2 : STAT_LINES - 1, :] = weight_ref[...]
    out_ref[STAT_LINES - 1 : STAT_LINES, :] = jnp.zeros((1, LINE), FLOAT)
    for place, parts in enumerate(pieces_of(grad_refs)):
        across, down = 0.0, []
        for ref, first, columns in parts:
            rows = ref.shape[0]
            wide = jnp.zeros((rows, LINE), FLOAT)
            for line in range(columns // LINE):
                piece = ref[:, first + line * LINE : first + (line + 1) * LINE]
                square = piece * piece
                wide = wide + square
                down.append(jnp.sum(square, axis=0, keepdims=True))
            across = across + jnp.sum(wide, axis=1, keepdims=True)
        offset = (flat_at if place < 5 else data_at) * rows
        row_start, col_start = ROW_STARTS[place], COL_STARTS[place]
        if place == 7:
            row_start, col_start = col_start, row_start
        row_lines = (COL_SIZES if place == 7 else ROW_SIZES)[place] // LINE
        for line, entry in enumerate(down_lines(across, offset, row_lines)):
            out_ref[row_start + line : row_start + line + 1, :] = entry
        groups = {5: 2}.get(place, 1)
        size = len(down) // groups
        for line, entry in enumerate(down):
            if place < 5:
                out_ref[col_start + line : col_start + line + 1, :] = entry
            else:
                for half in range(2):
                    at = col_start + (line // size * 2 + half) * size + line % size
                    out_ref[at : at + 1, :] = jnp.where(head_at == half, entry, 0.0)


def lane_of(lines, lane):
    shape = (1, LINE)
    here = lax.broadcasted_iota(jnp.int32, shape, 1) == lane
    return jnp.sum(jnp.where(here, lines, 0.0), axis=1, keepdims=True)


def update_kernel(place_ref, sums_ref, row_ref, col_ref, *refs):
    grad_refs, outs = refs[:6], refs[6:]
    row_out, col_out, norm_out, total_out = outs[:4]
    clipped_refs, update_refs = outs[4:12], joined_pieces(outs[12:15])
    data_at, head_at = place_ref[0], place_ref[1]
    flat_at = data_at * 2 + head_at
    row_sums = sums_ref[0:ROW_LINES, :]
    square_total = jnp.sum(jnp.sum(row_sums, axis=0, keepdims=True), axis=1, keepdims=True)
    norm = jnp.sqrt(square_total)
    factor = 1.0 / jnp.maximum(1.0, norm / CLIP_NORM)
    norm_out[...] = jnp.broadcast_to(norm, (1, LINE))
    square_factor = factor * factor
    lane = lax.broadcasted_iota(jnp.int32, (1, LINE), 1)
    totals = jnp.zeros((1, LINE), FLOAT)
    for place, parts in enumerate(pieces_of(grad_refs)):
        rows_len, cols_len = ROW_SIZES[place], COL_SIZES[place]
        row_from, row_to = ROW_STARTS[place], ROW_STARTS[place] + rows_len // LINE
        col_from, col_to = COL_STARTS[place], COL_STARTS[place] + cols_len // LINE
        new_row = DECAY_RATE * row_ref[row_from:row_to, :] + (1.0 - DECAY_RATE) * (
            square_factor * sums_ref[row_from:row_to, :] / float(cols_len) + EPS_FACTOR
        )
        col_from, col_to = col_from - ROW_LINES, col_to - ROW_LINES
        new_col = DECAY_RATE * col_ref[col_from:col_to, :] + (1.0 - DECAY_RATE) * (
            square_factor
            * sums_ref[ROW_LINES + col_from : ROW_LINES + col_to, :]
            / float(rows_len)
            + EPS_FACTOR
        )
        row_out[row_from:row_to, :] = new_row
        col_out[col_from:col_to, :] = new_col
        row_mean = (
            jnp.sum(jnp.sum(new_row, axis=0, keepdims=True), axis=1, keepdims=True) / rows_len
        )
        rows = parts[0][0].shape[0]
        offset = (flat_at if place < 5 else data_at) * rows
        if place == 7:
            down = lax.rsqrt(from_lines(new_col, offset, rows))
            across = jnp.where(head_at == 0, new_row[:12], new_row[12:])
            across = lax.rsqrt(across / row_mean)
        else:
            down = lax.rsqrt(from_lines(new_row, offset, rows) / row_mean)
            if place == 5:
                keys = jnp.where(head_at == 0, new_col[0:3], new_col[3:6])
                values = jnp.where(head_at == 0, new_col[6:9], new_col[9:12])
                across = lax.rsqrt(jnp.concatenate([keys, values], axis=0))
            elif place == 6:
                across = lax.rsqrt(jnp.where(head_at == 0, new_col[:12], new_col[12:]))
            else:
                across = lax.rsqrt(new_col)
        square = jnp.zeros((rows, LINE), FLOAT)
        line_at = 0
        for ref, first, columns in parts:
            for line in range(columns // LINE):
                piece = ref[:, first + line * LINE : first + (line + 1) * LINE] * factor
                update = piece * (down * across[line_at : line_at + 1, :])
                clipped_refs[place][:, line_at * LINE : (line_at + 1) * LINE] = piece
                update_ref, update_at, _ = update_refs[place]
                update_at += line_at * LINE
                update_ref[:, update_at : update_at + LINE] = update
                square = square + update * update
                line_at += 1
        total = jnp.sum(jnp.sum(square, axis=0, keepdims=True), axis=1, keepdims=True)
        totals = jnp.where(lane == place, total, totals)
    total_out[...] = totals


def apply_kernel(total_ref, weight_ref, *refs):
    master_refs, update_refs = joined_pieces(refs[:3]), joined_pieces(refs[3:6])
    for place in range(8):
        entries = float(ROW_SIZES[place] * COL_SIZES[place])
        total = lane_of(total_ref[...], place)
        weight = lane_of(weight_ref[...], place)
        limit = jnp.maximum(1.0, jnp.sqrt(total / entries) / CLIP_UPDATE)
        rate = RELATIVE_RATE * jnp.maximum(SCALE_FLOOR, jnp.sqrt(weight / entries))
        scale = rate / limit
        ref, at, columns = master_refs[place]
        update = update_refs[place][0][:, at : at + columns]
        refs[6 + place][...] = ref[:, at : at + columns] - scale * update


def weight_kernel(*refs):
    lane = lax.broadcasted_iota(jnp.int32, (1, LINE), 1)
    totals = jnp.zeros((1, LINE), FLOAT)
    for place in range(8):
        ref, at, columns = joined_pieces(refs[:3])[place]
        matrix = ref[:, at : at + columns]
        total = jnp.sum(jnp.sum(matrix * matrix, axis=0, keepdims=True), axis=1, keepdims=True)
        totals = jnp.where(lane == place, total, totals)
    refs[3][...] = totals


def whole_call(kernel, shapes, *operands, places=0):
    memory = [pl.BlockSpec(memory_space=pltpu.SMEM)] * places
    memory += [pl.BlockSpec(memory_space=pltpu.VMEM)] * (len(operands) - places)
    return pl.pallas_call(
        kernel,
        in_specs=memory,
        out_specs=[pl.BlockSpec(memory_space=pltpu.VMEM)] * len(shapes),
        out_shape=[jax.ShapeDtypeStruct(shape, FLOAT) for shape in shapes],
        compiler_params=KERNEL,
        cost_estimate=LIGHT,
    )(*operands)


GELU_WIDTH = 0.7978845608028654
GELU_CUBE = 0.044715


def gelu_parts(values):
    square = values * values
    bend = jnp.tanh(values * (GELU_WIDTH + GELU_WIDTH * GELU_CUBE * square))
    half = 0.5 + 0.5 * bend
    slope = GELU_WIDTH + 3.0 * GELU_WIDTH * GELU_CUBE * square
    return values * half, half + (0.5 * values) * (1.0 - bend * bend) * slope


def mlp_kernel(
    input_ref, grad_ref, fc1_ref, fc2_ref, branch_ref, in_grad_ref, part_ref, input_t, grad_t
):
    step = pl.program_id(0) * pl.num_programs(1) + pl.program_id(1)

    @pl.when(step == 0)
    def _():
        input_t[...] = input_ref[...].T
        grad_t[...] = grad_ref[...].T

    fc1, fc2 = fc1_ref[0], fc2_ref[0]
    act, slope = gelu_parts(nn(input_ref[...], fc1))
    act = act.astype(BFLOAT)
    pre_grad = (nn(grad_ref[...], fc2) * slope).astype(BFLOAT)
    branch, in_grad = nt(act, fc2), nt(pre_grad, fc1)

    @pl.when(step == 0)
    def _():
        branch_ref[...] = branch
        in_grad_ref[...] = in_grad

    @pl.when(step > 0)
    def _():
        branch_ref[...] += branch
        in_grad_ref[...] += in_grad

    far, rows = part_ref.shape[2], part_ref.shape[4]
    for kind, product in enumerate((nn(input_t[...], pre_grad), nn(grad_t[...], act))):
        product = product.astype(BFLOAT)
        for place in range(4 * far):
            part_ref[0, place % 4, place // 4, kind] = product[place * rows : (place + 1) * rows]


MLP_TILE = 512


def mlp_both(mlp_input, mlp_grad, weights):
    frames = mlp_input.shape[0]
    far = lax.axis_size("far")
    rows = D // (4 * far)
    tiles = HALF // MLP_TILE
    whole = pl.BlockSpec((frames, D), lambda half, tile: (0, 0))
    return pl.pallas_call(
        mlp_kernel,
        grid=(2, tiles),
        in_specs=[
            whole,
            whole,
            pl.BlockSpec((1, D, MLP_TILE), lambda half, tile: (half, 0, tile)),
            pl.BlockSpec((1, D, MLP_TILE), lambda half, tile: (half, 0, tile + tiles)),
        ],
        out_specs=[
            whole,
            whole,
            pl.BlockSpec(
                (1, 4, far, 2, rows, MLP_TILE), lambda half, tile: (half, 0, 0, 0, 0, tile)
            ),
        ],
        out_shape=[
            jax.ShapeDtypeStruct((frames, D), FLOAT),
            jax.ShapeDtypeStruct((frames, D), FLOAT),
            jax.ShapeDtypeStruct((2, 4, far, 2, rows, HALF), BFLOAT),
        ],
        scratch_shapes=[pltpu.VMEM((D, frames), BFLOAT), pltpu.VMEM((D, frames), BFLOAT)],
        compiler_params=KERNEL,
        cost_estimate=LIGHT,
    )(mlp_input, mlp_grad, weights, weights)


def per_device(
    block_in,
    text,
    timesteps,
    frame_mask,
    text_mask,
    cotangent,
    w_ada,
    w_qkv,
    w_out,
    w_cq,
    w_cout,
    w_ckv,
    w_fc1,
    w_fc2,
    row_state,
    col_state,
):
    clips = lax.axis_size(DP)
    devices = clips * 2
    data_at = lax.axis_index(DP)
    head_at = lax.axis_index("head")
    flat_at = data_at * 2 + head_at
    frames = block_in.shape[1]
    rows = w_qkv.shape[0]

    far = far_links()
    x_first = [far[0], row_link(), core_link()]
    y_first = [row_link(), far[0], core_link()]
    first = [
        gather_chain(
            with_bits(
                jnp.concatenate([w_qkv[:, :D], w_out, w_qkv[:, D:]], axis=1).astype(BFLOAT), "last"
            ),
            "last",
            far[1:],
        )
    ]
    second = [
        gather_chain(
            with_bits(jnp.concatenate([w_cq, w_cout], axis=1).astype(BFLOAT), "last"),
            "last",
            far[1:] + x_first,
        ),
        gather_chain(
            with_bits(w_ckv.astype(BFLOAT).reshape(w_ckv.shape[0], D), "columns"),
            "columns",
            far[1:] + y_first,
        ),
    ]
    masters = [
        jnp.concatenate([w_ada, w_qkv, w_out, w_cq, w_cout], axis=1),
        w_ckv.reshape(w_ckv.shape[0], D),
        jnp.concatenate([w_fc1, w_fc2.T], axis=1),
    ]
    mlp_shard = jnp.concatenate([w_fc1.astype(BFLOAT), w_fc2.T.astype(BFLOAT)], axis=1)
    inputs = swap_place(block_in[0])
    joint_mask = jnp.concatenate([frame_mask[0], text_mask[0]])

    def add_step(link):
        return lambda state: state + cross(state, link)

    def project(steps):
        condition = embed_part(steps, flat_at * rows, rows)
        product = jnp.dot(condition, w_ada.astype(BFLOAT), preferred_element_type=FLOAT)
        return condition, product.reshape(clips // 2, 2, 6 * D)

    def keep_step(link):
        def step(state):
            condition, product = state
            bit = bit_of(link)
            product = product.reshape(-1, 2, 6 * D)
            kept = lax.dynamic_slice_in_dim(product, bit, 1, axis=1)
            sent = lax.dynamic_slice_in_dim(product, 1 - bit, 1, axis=1)
            return condition, (kept + cross(sent, link)).reshape(-1, 6 * D)

        return step

    def last_step(state):
        condition, product = state
        return condition, product + cross(product, core_link())

    steps = lax.dynamic_update_slice(jnp.zeros((clips,), jnp.int32), timesteps, (data_at,))
    timing = Chain(
        steps,
        [add_step(link) for link in [core_link()] + far_links()[1:] + far_links()[:1]]
        + [lambda steps: keep_step(row_link())(project(steps))]
        + [keep_step(link) for link in far_links()]
        + [last_step],
    )
    far_count = len(far) - 1
    slots = far_count + 3
    for slot in range(slots):
        timing.advance({0: 1 + far_count, 1: 3, 2: far_count, 3: 1}.get(slot, 0))
        if slot == far_count:
            joint = first[0].state
            first = [
                gather_chain(joint[..., : 2 * D], "last", x_first),
                gather_chain(joint[..., 2 * D :], "last", y_first),
            ]
        for chain in first:
            chain.advance()
        if slot >= 2:
            for chain in second:
                chain.advance()
        if slot == far_count - 1:
            inputs, mlp_shard, joint_mask, text = tie(
                [timing] + first + second, inputs, mlp_shard, joint_mask, text
            )
            mlp_all = lax.all_gather(mlp_shard, HEAD + DP, axis=0, tiled=True)
            masks = from_clip_core(joint_mask)
            clip_text = from_clip_core(text[0])
        elif slot < slots - 1:
            tie([timing] + first + second)
        else:
            masters = tie([timing] + first, *masters)
            (weight_squares,) = whole_call(weight_kernel, [(1, LINE)], *masters)
    condition, modulation = timing.finish()
    query_out, w_key_value = [chain.finish().reshape(D, 2 * D) for chain in first]
    w_query, w_project = query_out[:, :D], query_out[:, D:]

    inputs = inputs.astype(FLOAT)
    core_at = data_at % 2
    own_allowed = lax.dynamic_slice_in_dim(masks, core_at * frames, frames)
    other_allowed = lax.dynamic_slice_in_dim(masks, (1 - core_at) * frames, frames)
    own_bias, other_bias = bias_of(own_allowed), bias_of(other_allowed)
    text_bias = bias_of(masks[2 * frames :])
    shift_self, scale_self, gate_self, shift_mlp, scale_mlp, gate_mlp = jnp.split(
        modulation, 6, axis=-1
    )

    self_input = modulate(inputs, shift_self, scale_self).astype(BFLOAT)
    key_value = nn(self_input, w_key_value).astype(BFLOAT)
    query = nn(self_input, w_query).astype(BFLOAT)
    other_key_value = cross(key_value, core_link())
    query, other_key_value = tie(second, query, other_key_value)
    for chain in second:
        chain.advance()

    self_keys = [(key_value, own_bias), (other_key_value, other_bias)]
    self_attn, self_logs = attend(query, self_keys, plain_places)
    self_attn, cotangent = tie(second, self_attn, cotangent)
    out_grad = swap_place(cotangent[0])
    cross_pair, w_text = [chain.finish() for chain in second]
    cross_pair, w_text = cross_pair.reshape(D, 2 * D), w_text.reshape(DT, 2 * D)
    w_cross_query, w_cross_project = cross_pair[:, :D], cross_pair[:, D:]
    self_branch = nn(self_attn, w_project)
    after_self = inputs + gate_self * self_branch

    text_pair = nn(clip_text, w_text).astype(BFLOAT)
    cross_input = layer_norm(after_self).astype(BFLOAT)
    cross_query = nn(cross_input, w_cross_query).astype(BFLOAT)
    text_keys = [(text_pair, text_bias)]
    cross_attn, cross_logs = attend(cross_query, text_keys, half_places)
    after_cross = after_self + nn(cross_attn, w_cross_project)

    mlp_input = modulate(after_cross, shift_mlp, scale_mlp).astype(BFLOAT)
    mlp_input, out_grad = tie([], mlp_input, out_grad)
    out_grad = out_grad.astype(FLOAT)
    mlp_grad = (gate_mlp * out_grad).astype(BFLOAT)
    mlp_branch, mlp_in_grad, mlp_part = mlp_both(
        mlp_input, mlp_grad, mlp_all.reshape(2, D, 2 * HALF)
    )
    mlp_part = lax.psum_scatter(
        mlp_part.reshape((8,) + mlp_part.shape[2:]),
        HEAD + ("near", "core"),
        scatter_dimension=0,
        tiled=False,
    )
    block_out = (after_cross + gate_mlp * mlp_branch).astype(BFLOAT)
    gate_mlp_grad = jnp.sum(out_grad * mlp_branch, axis=0, keepdims=True)
    mlp_back = jax.vjp(modulate, after_cross, shift_mlp, scale_mlp)[1]
    cross_res_grad, shift_mlp_grad, scale_mlp_grad = mlp_back(mlp_in_grad)
    cross_res_grad = out_grad + cross_res_grad
    cross_res_grad, block_out, gate_mlp_grad = tie([], cross_res_grad, block_out, gate_mlp_grad)

    cross_out_grad = cross_res_grad.astype(BFLOAT)
    cross_attn_grad = nt(cross_out_grad, w_cross_project).astype(BFLOAT)
    cross_query_grad, text_pair_grad = attend_back(
        cross_query, cross_attn, cross_attn_grad, cross_logs, text_keys, half_places
    )
    cross_chains = [
        scatter_chain(
            outer((cross_input, cross_query_grad), (cross_attn, cross_out_grad)), "last", False
        ),
        scatter_chain(outer((clip_text, text_pair_grad)), "columns", True),
    ]
    (cross_query_grad,) = tie(cross_chains, cross_query_grad)
    for chain in cross_chains:
        chain.advance()
    cross_in_grad = nt(cross_query_grad, w_cross_query)
    norm_back = jax.vjp(layer_norm, after_self)[1]
    self_res_grad = cross_res_grad + norm_back(cross_in_grad)[0]

    gate_self_grad = jnp.sum(self_res_grad * self_branch, axis=0, keepdims=True)
    self_out_grad = (gate_self * self_res_grad).astype(BFLOAT)
    self_attn_grad = nt(self_out_grad, w_project).astype(BFLOAT)
    self_attn_grad, self_out_grad = tie(cross_chains, self_attn_grad, self_out_grad)
    for chain in cross_chains:
        chain.advance()
    query_grad, own_pair_grad, other_pair_grad = attend_back(
        query, self_attn, self_attn_grad, self_logs, self_keys, plain_places
    )
    query_grad, own_pair_grad, other_pair_grad = tie(
        cross_chains, query_grad, own_pair_grad, other_pair_grad
    )
    for chain in cross_chains:
        chain.advance()
    pair_grad = (
        own_pair_grad.astype(FLOAT) + cross(other_pair_grad, core_link()).astype(FLOAT)
    ).astype(BFLOAT)
    last_chains = [
        scatter_chain(
            outer((self_input, query_grad), (self_attn, self_out_grad)), "last", False
        ),
        scatter_chain(outer((self_input, pair_grad)), "last", True),
    ]
    query_grad, pair_grad = tie(cross_chains + last_chains, query_grad, pair_grad)
    for chain in cross_chains + last_chains:
        chain.advance()
    in_grad_normed = nt(query_grad, w_query) + nt(pair_grad, w_key_value)
    self_back = jax.vjp(modulate, inputs, shift_self, scale_self)[1]
    input_res_grad, shift_self_grad, scale_self_grad = self_back(in_grad_normed)
    input_grad = (self_res_grad + input_res_grad).astype(BFLOAT)
    modulation_grad = jnp.concatenate(
        [
            shift_self_grad,
            scale_self_grad,
            gate_self_grad,
            shift_mlp_grad,
            scale_mlp_grad,
            gate_mlp_grad,
        ],
        axis=-1,
    )

    def join_step(link):
        def step(state):
            other = cross(state, link)
            upper = bit_of(link) == 1
            dim = dp_bits() - 1 if link[0] == HEAD else dp_bits() - link[1].bit_length()
            low, high = jnp.where(upper, other, state), jnp.where(upper, state, other)
            return jnp.concatenate([low, high], axis=dim)

        return step

    far = far_links()
    shape = (1,) * dp_bits() + (6 * D,)
    joining = Chain(
        modulation_grad,
        [lambda state: (state + cross(state, core_link())).reshape(shape)]
        + [join_step(link) for link in far[::-1] + [row_link()]],
    )
    joining.advance(2)
    block_out, input_grad, mlp_part = tie(
        [joining] + cross_chains + last_chains, block_out, input_grad, mlp_part
    )
    mlp_raw = lax.psum_scatter(mlp_part, "far", scatter_dimension=0, tiled=False).astype(FLOAT)
    for count in (len(far) - 2, 2):
        for chain in cross_chains + last_chains:
            chain.advance()
        joining.advance(count)
        block_out, input_grad = tie(
            [joining] + cross_chains + last_chains, block_out, input_grad
        )
    mlp_raw, block_out, input_grad = tie(last_chains, mlp_raw, block_out, input_grad)
    own_results = jnp.stack([block_out, input_grad])
    swapped_results = swap_only(own_results)
    modulation_grad = joining.finish()
    ada_raw = jnp.einsum(
        "cr,cx->rx",
        condition.astype(FLOAT),
        modulation_grad.reshape(clips, 6 * D),
        precision=PRECISE,
    )

    cross_raw, ckv_raw = [chain.finish() for chain in cross_chains]
    query_out_raw, pair_raw = [chain.finish() for chain in last_chains]

    place = jnp.stack([data_at, head_at]).astype(jnp.int32)
    raw_grads = [ada_raw, query_out_raw, pair_raw, cross_raw, ckv_raw, mlp_raw]
    (statistics,) = whole_call(
        statistics_kernel, [(STAT_LINES, LINE)], place, weight_squares, *raw_grads, places=1
    )
    sums = sum_all(statistics)
    shapes = [(rows, columns) for columns in COL_SIZES[:5]]
    shapes += [masters[1].shape] + [(rows * 2, HALF)] * 2
    line = (1, LINE)
    row_new, col_new, norm, update_squares, *rest = whole_call(
        update_kernel,
        [(ROW_LINES, LINE), (COL_LINES, LINE), line, line]
        + shapes
        + [master.shape for master in masters],
        place,
        sums,
        row_state.reshape(ROW_LINES, LINE),
        col_state.reshape(COL_LINES, LINE),
        *raw_grads,
        places=1,
    )
    clipped, updates = list(rest[:8]), rest[8:]
    updated = whole_call(
        apply_kernel,
        shapes,
        sum_all(update_squares),
        sums[STAT_LINES - 2 : STAT_LINES - 1],
        *masters,
        *updates,
    )
    updated = list(updated)
    (own,) = tie([], own_results)
    late, _ = tie([], on_own_chip(), update_squares)
    block_out, input_grad = jnp.where(late, own, swapped_results)
    clipped[5] = clipped[5].reshape(w_ckv.shape)
    updated[5] = updated[5].reshape(w_ckv.shape)
    clipped[7] = clipped[7].T
    updated[7] = updated[7].T
    return (
        block_out[None],
        input_grad[None],
        norm[0, 0],
        row_new.reshape(-1),
        col_new.reshape(-1),
        *clipped,
        *updated,
    )


def solution(mesh):
    devices = mesh.devices
    refined = jax.sharding.Mesh(devices.reshape(devices.shape[0] // 4, 2, 2, 2), ALL)
    return jax.shard_map(
        per_device,
        mesh=refined,
        in_specs=(
            P(DP, "head", None),
            P(DP, None, None),
            P(DP),
            P(DP, None),
            P(DP, None),
            P(DP, "head", None),
            P(ALL, None),
            P(ALL, None),
            P(ALL, None),
            P(ALL, None),
            P(ALL, None),
            P(DP, None, "head"),
            P(DP, "head"),
            P("head", DP),
            P(),
            P(),
        ),
        out_specs=(
            P(DP, "head", None),
            P(DP, "head", None),
            P(),
            P(),
            P(),
            P(ALL, None),
            P(ALL, None),
            P(ALL, None),
            P(ALL, None),
            P(ALL, None),
            P(DP, None, "head"),
            P(DP, "head"),
            P("head", DP),
            P(ALL, None),
            P(ALL, None),
            P(ALL, None),
            P(ALL, None),
            P(ALL, None),
            P(DP, None, "head"),
            P(DP, "head"),
            P("head", DP),
        ),
        check_vma=False,
    )
```

```python
import functools

import jax
import jax.numpy as jnp
from jax import lax
from jax.experimental import pallas as pl
from jax.experimental.pallas import tpu as pltpu
from jax.sharding import PartitionSpec as P

D = 768
FF = 3072
DT = 1024
HD = 64
HALF = FF // 2

PRECISE = lax.Precision.HIGHEST
FLOAT = jnp.float32
BFLOAT = jnp.bfloat16
EPS_NORM = 1e-06
EPS_FACTOR = 1e-30
CLIP_NORM = 1.0
CLIP_UPDATE = 0.25
DECAY_RATE = 0.5
RELATIVE_RATE = 4.0
SCALE_FLOOR = 0.001
SCORE_SCALE = 0.125
MASKED_SCORE = -1e30
DP = ("far", "near", "core")
ALL = DP + ("head",)
HEAD = ("head",)
PAIR = 2 * HD
PAIRS = D // PAIR


def embed_part(steps, first, count):
    halfway = D // 2
    place = first + jnp.arange(count)
    freqs = jnp.exp(-jnp.log(10000.0) * (place % halfway).astype(FLOAT) / halfway)
    angles = steps.astype(FLOAT)[:, None] * freqs
    waves = jnp.where(place < halfway, jnp.cos(angles), jnp.sin(angles))
    return jax.nn.silu(waves).astype(BFLOAT)


def core_link():
    return (DP, 1)


def row_link():
    return (HEAD, 1)


def far_links():
    masks, mask = [], 2
    while mask < lax.axis_size(DP):
        masks.append(mask)
        mask = mask * 2
    return [(DP, mask) for mask in masks]


def dp_bits():
    return lax.axis_size(DP).bit_length() - 1


def bit_of(link):
    return (lax.axis_index(link[0]) // link[1]) % 2


def cross(values, link):
    pairs = [(place, place ^ link[1]) for place in range(lax.axis_size(link[0]))]
    return lax.ppermute(values, link[0], pairs)


def dim_of(link, head):
    if link[0] == HEAD:
        return {"first": 0, "last": dp_bits(), "columns": dp_bits() + 1}[head]
    return (1 if head == "first" else 0) + dp_bits() - link[1].bit_length()


def leading(head):
    return dp_bits() + (0 if head == "columns" else 1)


def grow(block, link, head):
    other = cross(block, link)
    upper = bit_of(link) == 1
    low = jnp.where(upper, other, block)
    high = jnp.where(upper, block, other)
    return jnp.concatenate([low, high], axis=dim_of(link, head))


def shrink(block, link, head, kind=BFLOAT):
    dim, bit = dim_of(link, head), bit_of(link)
    half = block.shape[dim] // 2
    kept = lax.dynamic_slice_in_dim(block, bit * half, half, axis=dim)
    sent = lax.dynamic_slice_in_dim(block, (1 - bit) * half, half, axis=dim)
    return (kept.astype(FLOAT) + cross(sent.astype(BFLOAT), link).astype(FLOAT)).astype(kind)


class Chain:
    def __init__(self, state, steps):
        self.state, self.steps = state, list(steps)

    def advance(self, count=1):
        for _ in range(min(count, len(self.steps))):
            self.state = self.steps.pop(0)(self.state)
        return self

    def finish(self):
        return self.advance(len(self.steps)).state


def tie(chains, *values):
    states, values = lax.optimization_barrier(([chain.state for chain in chains], values))
    for chain, state in zip(chains, states):
        chain.state = state
    return values


def gather_chain(block, head, links):
    return Chain(block, [lambda state, link=link: grow(state, link, head) for link in links])


def with_bits(shard, head):
    return shard.reshape((1,) * leading(head) + shard.shape)


def scatter_chain(matrix, head, row_early):
    bits = leading(head)
    rows, columns = matrix.shape[-2:]
    split = dp_bits() if head == "first" else bits
    block = matrix.reshape((2,) * bits + (rows // 2**split, columns))
    far = far_links()
    plane = [far[0], row_link()] if row_early else [row_link(), far[0]]
    order = [core_link()] + plane + far[1:]
    kinds = [BFLOAT] * (len(order) - 1) + [FLOAT]
    steps = [
        lambda state, link=link, kind=kind: shrink(state, link, head, kind)
        for link, kind in zip(order, kinds)
    ]
    return Chain(block, steps + [lambda state: state.reshape(state.shape[bits:])])


def sum_all(values):
    for link in [core_link(), row_link()] + far_links():
        values = values + cross(values, link)
    return values


def on_own_chip():
    return bit_of(core_link()) == bit_of(row_link())


def swap_only(values):
    pairs = []
    for place in range(lax.axis_size(DP)):
        for head in range(2):
            if place & 1 != head:
                pairs.append((place * 2 + head, ((place & ~1) | head) * 2 + (place & 1)))
    return lax.ppermute(values, ALL, pairs)


def swap_place(values):
    return jnp.where(on_own_chip(), values, swap_only(values))


def from_clip_core(values):
    pairs = []
    for place in range(0, lax.axis_size(DP), 2):
        for head in range(2):
            pairs.append(((place + head) * 2 + head, (place + 1 - head) * 2 + head))
    return jnp.where(on_own_chip(), values, lax.ppermute(values, ALL, pairs))


def nt(left, right):
    return lax.dot_general(left, right, (((1,), (1,)), ((), ())), preferred_element_type=FLOAT)


def nn(left, right):
    return lax.dot_general(left, right, (((1,), (0,)), ((), ())), preferred_element_type=FLOAT)


def lanes_of(length):
    return lax.broadcasted_iota(jnp.int32, (length, PAIR), 1)


def with_spare(pair, head, spare):
    lane = lanes_of(pair.shape[0])
    rest = jnp.where(lane == HD * (1 - head), spare, jnp.zeros_like(pair))
    return jnp.where(lane // HD == head, pair, rest)


def attend_kernel(blocks, *refs):
    query_ref = refs[0]
    key_refs, value_refs, bias_refs = refs[1 : 1 + 3 * blocks : 3], refs[2 : 2 + 3 * blocks : 3], refs[3 : 3 + 3 * blocks : 3]
    out_ref, log_ref = refs[1 + 3 * blocks :]
    queries = query_ref[...] * jnp.asarray(SCORE_SCALE, BFLOAT)
    one = jnp.ones((1, 1), BFLOAT)
    values_t = [ref[...].T for ref in value_refs]
    results, logs = [], []
    for head in range(2):
        query = with_spare(queries, head, one)
        scores = [
            nt(with_spare(key_ref[...], head, bias_ref[...]), query)
            for key_ref, bias_ref in zip(key_refs, bias_refs)
        ]
        peak = functools.reduce(
            jnp.maximum, [jnp.max(score, axis=0, keepdims=True) for score in scores]
        )
        total = None
        for score, value_t in zip(scores, values_t):
            probs = jnp.exp(score - peak).astype(BFLOAT)
            row = lax.broadcasted_iota(jnp.int32, value_t.shape, 0)
            term = nn(jnp.where(row // HD == head, value_t, one), probs)
            total = term if total is None else total + term
        weight = total[HD * (1 - head) : HD * (1 - head) + 1, :]
        results.append(total[HD * head : HD * (head + 1), :] / weight)
        logs.append(peak + jnp.log(weight))
    out_ref[...] = jnp.concatenate(results, axis=0).T.astype(BFLOAT)
    log_ref[0] = jnp.concatenate(logs, axis=0)


def back_kernel(blocks, places, *refs):
    query_ref, out_ref, grad_ref, log_ref = refs[:4]
    ins = refs[4 : 4 + 3 * blocks]
    key_refs, value_refs, bias_refs = ins[0::3], ins[1::3], ins[2::3]
    query_grad_ref = refs[4 + 3 * blocks]
    pair_grad_refs = refs[5 + 3 * blocks :]
    queries = query_ref[...] * jnp.asarray(SCORE_SCALE, BFLOAT)
    out_grad = grad_ref[...]
    zero = jnp.zeros((1, 1), BFLOAT)
    one = jnp.ones((1, 1), BFLOAT)
    product = out_ref[...].astype(FLOAT) * out_grad.astype(FLOAT)
    chooser = (
        lax.broadcasted_iota(jnp.int32, (8, PAIR), 1) // HD
        == lax.broadcasted_iota(jnp.int32, (8, PAIR), 0)
    ).astype(FLOAT)
    inner = lax.dot_general(
        chooser, product, (((1,), (1,)), ((), ())), precision=PRECISE, preferred_element_type=FLOAT
    )
    keys_t = [ref[...].T for ref in key_refs]
    query_parts = [None, None]
    for block in range(blocks):
        key_grad, value_grad = None, None
        for head in range(2):
            grad_here = with_spare(out_grad, head, zero)
            score = nt(
                with_spare(key_refs[block][...], head, bias_refs[block][...]),
                with_spare(queries, head, one),
            )
            probs = jnp.exp(score - log_ref[0, head : head + 1, :])
            prob_grad = nt(value_refs[block][...], grad_here)
            score_grad = (probs * (prob_grad - inner[head : head + 1, :])).astype(BFLOAT)
            value_term = nn(probs.astype(BFLOAT), grad_here)
            key_term = nn(score_grad, with_spare(queries, head, zero))
            query_term = nn(keys_t[block][HD * head : HD * (head + 1), :], score_grad)
            value_grad = value_term if value_grad is None else value_grad + value_term
            key_grad = key_term if key_grad is None else key_grad + key_term
            query_parts[head] = (
                query_term if query_parts[head] is None else query_parts[head] + query_term
            )
        key_at, value_at = places(pl.program_id(0))
        key_at = pl.multiple_of(key_at * PAIR, PAIR)
        value_at = pl.multiple_of(value_at * PAIR, PAIR)
        pair_grad_refs[block][:, pl.ds(key_at, PAIR)] = key_grad.astype(BFLOAT)
        pair_grad_refs[block][:, pl.ds(value_at, PAIR)] = value_grad.astype(BFLOAT)
    joined = jnp.concatenate(query_parts, axis=0) * SCORE_SCALE
    query_grad_ref[...] = joined.T.astype(BFLOAT)


def column_block(length):
    return pl.BlockSpec((length, PAIR), lambda pair: (0, pair))


def plain_places(pair):
    return pair, pair + PAIRS


def half_places(pair):
    half, part = pair // (PAIRS // 2), pair % (PAIRS // 2)
    return half * PAIRS + part, half * PAIRS + PAIRS // 2 + part


def whole_block(shape):
    return pl.BlockSpec(shape, lambda pair: (0,) * len(shape))


def log_block(frames):
    return pl.BlockSpec((1, 2, frames), lambda pair: (pair, 0, 0))


def key_specs(key_values, places):
    specs, operands = [], []
    for joint, bias in key_values:
        length = joint.shape[0]
        specs += [
            pl.BlockSpec((length, PAIR), lambda pair: (0, places(pair)[0])),
            pl.BlockSpec((length, PAIR), lambda pair: (0, places(pair)[1])),
            whole_block((length, PAIR)),
        ]
        operands += [joint, joint, bias]
    return specs, operands


def room(mebibytes):
    return pltpu.CompilerParams(vmem_limit_bytes=mebibytes * 1024 * 1024)


LIGHT = pl.CostEstimate(flops=1000, bytes_accessed=1000, transcendentals=0)


def attend(queries, key_values, places):
    frames, blocks = queries.shape[0], len(key_values)
    specs, operands = key_specs(key_values, places)
    return pl.pallas_call(
        functools.partial(attend_kernel, blocks),
        grid=(PAIRS,),
        in_specs=[column_block(frames)] + specs,
        out_specs=[column_block(frames), log_block(frames)],
        out_shape=[
            jax.ShapeDtypeStruct((frames, D), BFLOAT),
            jax.ShapeDtypeStruct((PAIRS, 2, frames), FLOAT),
        ],
        compiler_params=room(48),
        cost_estimate=LIGHT,
    )(queries, *operands)


def attend_back(queries, out, out_grad, logs, key_values, places):
    frames, blocks = queries.shape[0], len(key_values)
    specs, operands = key_specs(key_values, places)
    return pl.pallas_call(
        functools.partial(back_kernel, blocks, places),
        grid=(PAIRS,),
        in_specs=[column_block(frames)] * 3 + [log_block(frames)] + specs,
        out_specs=[column_block(frames)] + [whole_block(joint.shape) for joint, _ in key_values],
        out_shape=[jax.ShapeDtypeStruct((frames, D), BFLOAT)]
        + [jax.ShapeDtypeStruct(joint.shape, BFLOAT) for joint, _ in key_values],
        compiler_params=room(48),
        cost_estimate=LIGHT,
    )(queries, out, out_grad, logs, *operands)


def outer_kernel(*refs):
    out_ref, count = refs[-1], len(refs) // 2
    at = 0
    for place in range(count):
        left, right = refs[2 * place], refs[2 * place + 1]
        width = right.shape[1]
        product = lax.dot_general(
            left[...], right[...], (((0,), (0,)), ((), ())), preferred_element_type=FLOAT
        )
        out_ref[:, at : at + width] = product.astype(BFLOAT)
        at += width


def outer(*pairs):
    operands = [matrix for pair in pairs for matrix in pair]
    shape = (pairs[0][0].shape[1], sum(right.shape[1] for _, right in pairs))
    return pl.pallas_call(
        outer_kernel,
        out_shape=jax.ShapeDtypeStruct(shape, BFLOAT),
        compiler_params=room(48),
        cost_estimate=LIGHT,
    )(*operands)


def bias_of(allowed):
    column = jnp.where(allowed > 0, 0.0, MASKED_SCORE).astype(BFLOAT)
    return jnp.broadcast_to(column[:, None], (allowed.shape[0], PAIR))


LINE = 128
ROW_SIZES = [D, D, D, D, D, DT, D, FF]
COL_SIZES = [6 * D, 3 * D, D, D, D, 2 * D, FF, D]
ROW_LINES = sum(ROW_SIZES) // LINE
COL_LINES = sum(COL_SIZES) // LINE
STAT_LINES = ROW_LINES + COL_LINES + 2


def starts_of(sizes, first):
    starts = []
    for size in sizes:
        starts.append(first)
        first += size // LINE
    return starts


ROW_STARTS = starts_of(ROW_SIZES, 0)
COL_STARTS = starts_of(COL_SIZES, ROW_LINES)


def lines_at(line, shape):
    return lax.broadcasted_iota(jnp.int32, shape, 1) + line * LINE


def down_lines(column, offset, lines):
    shape = (column.shape[0], LINE)
    wanted = lax.broadcasted_iota(jnp.int32, shape, 0) + offset
    return [
        jnp.sum(jnp.where(lines_at(line, shape) == wanted, column, 0.0), axis=0, keepdims=True)
        for line in range(lines)
    ]


def from_lines(lines, offset, count):
    shape = (count, LINE)
    wanted = lax.broadcasted_iota(jnp.int32, shape, 0) + offset
    total = jnp.zeros(shape, FLOAT)
    for line in range(lines.shape[0]):
        here = jnp.where(lines_at(line, shape) == wanted, lines[line : line + 1, :], 0.0)
        total = total + here
    return jnp.sum(total, axis=1, keepdims=True)


def pieces_of(grad_refs):
    ada, query_out, key_value, cross_pair, text_pair, mlp = grad_refs
    return [
        [(ada, 0, 6 * D)],
        [(query_out, 0, D), (key_value, 0, 2 * D)],
        [(query_out, D, D)],
        [(cross_pair, 0, D)],
        [(cross_pair, D, D)],
        [(text_pair, 0, D)],
        [(mlp.at[0], 0, HALF)],
        [(mlp.at[1], 0, HALF)],
    ]


def joined_pieces(refs):
    square, text_pair, mlp = refs
    parts, at = [], 0
    for place in range(5):
        parts.append((square, at, COL_SIZES[place]))
        at += COL_SIZES[place]
    return parts + [(text_pair, 0, D), (mlp, 0, HALF), (mlp, HALF, HALF)]


def statistics_kernel(place_ref, weight_ref, *refs):
    grad_refs, out_ref = refs[:6], refs[6]
    data_at, head_at = place_ref[0], place_ref[1]
    flat_at = data_at * 2 + head_at
    out_ref[STAT_LINES - 2 : STAT_LINES - 1, :] = weight_ref[...]
    out_ref[STAT_LINES - 1 : STAT_LINES, :] = jnp.zeros((1, LINE), FLOAT)
    for place, parts in enumerate(pieces_of(grad_refs)):
        across, down = 0.0, []
        for ref, first, columns in parts:
            rows = ref.shape[0]
            wide = jnp.zeros((rows, LINE), FLOAT)
            for line in range(columns // LINE):
                piece = ref[:, first + line * LINE : first + (line + 1) * LINE]
                square = piece * piece
                wide = wide + square
                down.append(jnp.sum(square, axis=0, keepdims=True))
            across = across + jnp.sum(wide, axis=1, keepdims=True)
        offset = (flat_at if place < 5 else data_at) * rows
        row_start, col_start = ROW_STARTS[place], COL_STARTS[place]
        if place == 7:
            row_start, col_start = col_start, row_start
        row_lines = (COL_SIZES if place == 7 else ROW_SIZES)[place] // LINE
        for line, entry in enumerate(down_lines(across, offset, row_lines)):
            out_ref[row_start + line : row_start + line + 1, :] = entry
        groups = {5: 2}.get(place, 1)
        size = len(down) // groups
        for line, entry in enumerate(down):
            if place < 5:
                out_ref[col_start + line : col_start + line + 1, :] = entry
            else:
                for half in range(2):
                    at = col_start + (line // size * 2 + half) * size + line % size
                    out_ref[at : at + 1, :] = jnp.where(head_at == half, entry, 0.0)


def lane_of(lines, lane):
    shape = (1, LINE)
    here = lax.broadcasted_iota(jnp.int32, shape, 1) == lane
    return jnp.sum(jnp.where(here, lines, 0.0), axis=1, keepdims=True)


def update_kernel(place_ref, sums_ref, row_ref, col_ref, *refs):
    grad_refs, outs = refs[:6], refs[6:]
    row_out, col_out, norm_out, total_out = outs[:4]
    clipped_refs, update_refs = outs[4:12], joined_pieces(outs[12:15])
    data_at, head_at = place_ref[0], place_ref[1]
    flat_at = data_at * 2 + head_at
    row_sums = sums_ref[0:ROW_LINES, :]
    square_total = jnp.sum(jnp.sum(row_sums, axis=0, keepdims=True), axis=1, keepdims=True)
    norm = jnp.sqrt(square_total)
    factor = 1.0 / jnp.maximum(1.0, norm / CLIP_NORM)
    norm_out[...] = jnp.broadcast_to(norm, (1, LINE))
    square_factor = factor * factor
    lane = lax.broadcasted_iota(jnp.int32, (1, LINE), 1)
    totals = jnp.zeros((1, LINE), FLOAT)
    for place, parts in enumerate(pieces_of(grad_refs)):
        rows_len, cols_len = ROW_SIZES[place], COL_SIZES[place]
        row_from, row_to = ROW_STARTS[place], ROW_STARTS[place] + rows_len // LINE
        col_from, col_to = COL_STARTS[place], COL_STARTS[place] + cols_len // LINE
        new_row = DECAY_RATE * row_ref[row_from:row_to, :] + (1.0 - DECAY_RATE) * (
            square_factor * sums_ref[row_from:row_to, :] / float(cols_len) + EPS_FACTOR
        )
        col_from, col_to = col_from - ROW_LINES, col_to - ROW_LINES
        new_col = DECAY_RATE * col_ref[col_from:col_to, :] + (1.0 - DECAY_RATE) * (
            square_factor
            * sums_ref[ROW_LINES + col_from : ROW_LINES + col_to, :]
            / float(rows_len)
            + EPS_FACTOR
        )
        row_out[row_from:row_to, :] = new_row
        col_out[col_from:col_to, :] = new_col
        row_mean = (
            jnp.sum(jnp.sum(new_row, axis=0, keepdims=True), axis=1, keepdims=True) / rows_len
        )
        rows = parts[0][0].shape[0]
        offset = (flat_at if place < 5 else data_at) * rows
        if place == 7:
            down = lax.rsqrt(from_lines(new_col, offset, rows))
            across = jnp.where(head_at == 0, new_row[:12], new_row[12:])
            across = lax.rsqrt(across / row_mean)
        else:
            down = lax.rsqrt(from_lines(new_row, offset, rows) / row_mean)
            if place == 5:
                keys = jnp.where(head_at == 0, new_col[0:3], new_col[3:6])
                values = jnp.where(head_at == 0, new_col[6:9], new_col[9:12])
                across = lax.rsqrt(jnp.concatenate([keys, values], axis=0))
            elif place == 6:
                across = lax.rsqrt(jnp.where(head_at == 0, new_col[:12], new_col[12:]))
            else:
                across = lax.rsqrt(new_col)
        square = jnp.zeros((rows, LINE), FLOAT)
        line_at = 0
        for ref, first, columns in parts:
            for line in range(columns // LINE):
                piece = ref[:, first + line * LINE : first + (line + 1) * LINE] * factor
                update = piece * (down * across[line_at : line_at + 1, :])
                clipped_refs[place][:, line_at * LINE : (line_at + 1) * LINE] = piece
                update_ref, update_at, _ = update_refs[place]
                update_at += line_at * LINE
                update_ref[:, update_at : update_at + LINE] = update
                square = square + update * update
                line_at += 1
        total = jnp.sum(jnp.sum(square, axis=0, keepdims=True), axis=1, keepdims=True)
        totals = jnp.where(lane == place, total, totals)
    total_out[...] = totals


def apply_kernel(total_ref, weight_ref, *refs):
    master_refs, update_refs = joined_pieces(refs[:3]), joined_pieces(refs[3:6])
    for place in range(8):
        entries = float(ROW_SIZES[place] * COL_SIZES[place])
        total = lane_of(total_ref[...], place)
        weight = lane_of(weight_ref[...], place)
        limit = jnp.maximum(1.0, jnp.sqrt(total / entries) / CLIP_UPDATE)
        rate = RELATIVE_RATE * jnp.maximum(SCALE_FLOOR, jnp.sqrt(weight / entries))
        scale = rate / limit
        ref, at, columns = master_refs[place]
        update = update_refs[place][0][:, at : at + columns]
        refs[6 + place][...] = ref[:, at : at + columns] - scale * update


def weight_kernel(*refs):
    lane = lax.broadcasted_iota(jnp.int32, (1, LINE), 1)
    totals = jnp.zeros((1, LINE), FLOAT)
    for place in range(8):
        ref, at, columns = joined_pieces(refs[:3])[place]
        matrix = ref[:, at : at + columns]
        total = jnp.sum(jnp.sum(matrix * matrix, axis=0, keepdims=True), axis=1, keepdims=True)
        totals = jnp.where(lane == place, total, totals)
    refs[3][...] = totals


def whole_call(kernel, shapes, *operands, places=0):
    memory = [pl.BlockSpec(memory_space=pltpu.SMEM)] * places
    memory += [pl.BlockSpec(memory_space=pltpu.VMEM)] * (len(operands) - places)
    return pl.pallas_call(
        kernel,
        in_specs=memory,
        out_specs=[pl.BlockSpec(memory_space=pltpu.VMEM)] * len(shapes),
        out_shape=[jax.ShapeDtypeStruct(shape, FLOAT) for shape in shapes],
        compiler_params=room(48),
        cost_estimate=LIGHT,
    )(*operands)


GELU_WIDTH = 0.7978845608028654
GELU_CUBE = 0.044715


def gelu_parts(values):
    square = values * values
    bend = jnp.tanh(values * (GELU_WIDTH + GELU_WIDTH * GELU_CUBE * square))
    half = 0.5 + 0.5 * bend
    slope = GELU_WIDTH + 3.0 * GELU_WIDTH * GELU_CUBE * square
    return values * half, half + (0.5 * values) * (1.0 - bend * bend) * slope


ROWS = 512
SHIFT_SELF, SCALE_SELF, GATE_SELF, SHIFT_MLP, SCALE_MLP, GATE_MLP = range(6)


def block_of(modulation_ref, place):
    return modulation_ref[:, place * D : (place + 1) * D]


def over_rows(frames, body, start=None):
    def step(place, carry):
        return body(pl.ds(pl.multiple_of(place * ROWS, ROWS), ROWS), carry)

    return lax.fori_loop(0, frames // ROWS, step, start)


def normed(values):
    centered = values - jnp.mean(values, axis=-1, keepdims=True)
    rate = lax.rsqrt(jnp.mean(centered * centered, axis=-1, keepdims=True) + EPS_NORM)
    return centered * rate, rate


def normed_back(grad, norm, rate):
    inner = jnp.mean(grad * norm, axis=-1, keepdims=True)
    return rate * (grad - jnp.mean(grad, axis=-1, keepdims=True) - norm * inner)


def down(values):
    return jnp.sum(values, axis=0, keepdims=True)


def no_sums(count):
    return (jnp.zeros((1, D), FLOAT),) * count


def first_kernel(
    in_ref, modulation_ref, query_weight_ref, pair_weight_ref, self_input_ref, query_ref, pair_ref
):
    shift = block_of(modulation_ref, SHIFT_SELF)
    scale = 1.0 + block_of(modulation_ref, SCALE_SELF)

    def some(rows, carry):
        norm, _ = normed(in_ref[rows, :].astype(FLOAT))
        self_input_ref[rows, :] = (norm * scale + shift).astype(BFLOAT)
        return carry

    over_rows(in_ref.shape[0], some)
    pair_ref[...] = nn(self_input_ref[...], pair_weight_ref[...]).astype(BFLOAT)
    query_ref[...] = nn(self_input_ref[...], query_weight_ref[...]).astype(BFLOAT)


def between_kernel(
    attn_ref,
    project_ref,
    in_ref,
    modulation_ref,
    query_weight_ref,
    branch_ref,
    after_ref,
    cross_input_ref,
    query_ref,
):
    branch_ref[...] = nn(attn_ref[...], project_ref[...])
    gate = block_of(modulation_ref, GATE_SELF)

    def some(rows, carry):
        after = in_ref[rows, :].astype(FLOAT) + gate * branch_ref[rows, :]
        after_ref[rows, :] = after
        norm, _ = normed(after)
        cross_input_ref[rows, :] = norm.astype(BFLOAT)
        return carry

    over_rows(in_ref.shape[0], some)
    query_ref[...] = nn(cross_input_ref[...], query_weight_ref[...]).astype(BFLOAT)


def mlp_kernel(
    attn_ref,
    project_ref,
    after_ref,
    modulation_ref,
    out_grad_ref,
    fc1_ref,
    fc2_ref,
    out_ref,
    res_grad_ref,
    cross_out_grad_ref,
    attn_grad_ref,
    sums_ref,
    part_ref,
    input_ref,
    grad_ref,
    input_t,
    grad_t,
    joined_ref,
    branch_ref,
    in_grad_ref,
):
    step = pl.program_id(0) * pl.num_programs(1) + pl.program_id(1)
    last = pl.num_programs(0) * pl.num_programs(1) - 1
    frames = attn_ref.shape[0]
    gate = block_of(modulation_ref, GATE_MLP)
    scale = 1.0 + block_of(modulation_ref, SCALE_MLP)

    @pl.when(step == 0)
    def _():
        shift = block_of(modulation_ref, SHIFT_MLP)
        joined_ref[...] = after_ref[...] + nn(attn_ref[...], project_ref[...])

        def some(rows, carry):
            norm, _ = normed(joined_ref[rows, :])
            input_ref[rows, :] = (norm * scale + shift).astype(BFLOAT)
            grad_ref[rows, :] = (gate * out_grad_ref[rows, :].astype(FLOAT)).astype(BFLOAT)
            return carry

        over_rows(frames, some)
        input_t[...] = input_ref[...].T
        grad_t[...] = grad_ref[...].T

    fc1, fc2 = fc1_ref[0], fc2_ref[0]
    act, slope = gelu_parts(nn(input_ref[...], fc1))
    act = act.astype(BFLOAT)
    pre_grad = (nn(grad_ref[...], fc2) * slope).astype(BFLOAT)
    branch, in_grad = nt(act, fc2), nt(pre_grad, fc1)

    @pl.when(step == 0)
    def _():
        branch_ref[...] = branch
        in_grad_ref[...] = in_grad

    @pl.when(step > 0)
    def _():
        branch_ref[...] += branch
        in_grad_ref[...] += in_grad

    far, size = part_ref.shape[2], part_ref.shape[4]
    for kind, product in enumerate((nn(input_t[...], pre_grad), nn(grad_t[...], act))):
        product = product.astype(BFLOAT)
        for place in range(4 * far):
            part_ref[0, place % 4, place // 4, kind] = product[place * size : (place + 1) * size]

    @pl.when(step == last)
    def _():
        def some(rows, carry):
            gate_sum, shift_sum, scale_sum = carry
            joined, branch_here = joined_ref[rows, :], branch_ref[rows, :]
            out_grad, in_grad_here = out_grad_ref[rows, :].astype(FLOAT), in_grad_ref[rows, :]
            out_ref[rows, :] = (joined + gate * branch_here).astype(BFLOAT)
            norm, rate = normed(joined)
            res_grad = out_grad + normed_back(in_grad_here * scale, norm, rate)
            res_grad_ref[rows, :] = res_grad
            cross_out_grad_ref[rows, :] = res_grad.astype(BFLOAT)
            return (
                gate_sum + down(out_grad * branch_here),
                shift_sum + down(in_grad_here),
                scale_sum + down(in_grad_here * norm),
            )

        gate_sum, shift_sum, scale_sum = over_rows(frames, some, no_sums(3))
        sums_ref[:, :D] = shift_sum
        sums_ref[:, D : 2 * D] = scale_sum
        sums_ref[:, 2 * D :] = gate_sum
        attn_grad_ref[...] = nt(cross_out_grad_ref[...], project_ref[...]).astype(BFLOAT)


def between_back_kernel(
    query_grad_ref,
    query_weight_ref,
    after_ref,
    res_grad_ref,
    branch_ref,
    modulation_ref,
    project_ref,
    self_res_ref,
    out_grad_ref,
    attn_grad_ref,
    sums_ref,
    in_grad_ref,
):
    in_grad_ref[...] = nt(query_grad_ref[...], query_weight_ref[...])
    gate = block_of(modulation_ref, GATE_SELF)

    def some(rows, carry):
        norm, rate = normed(after_ref[rows, :])
        res_grad = res_grad_ref[rows, :] + normed_back(in_grad_ref[rows, :], norm, rate)
        self_res_ref[rows, :] = res_grad
        out_grad_ref[rows, :] = (gate * res_grad).astype(BFLOAT)
        return (carry[0] + down(res_grad * branch_ref[rows, :]),)

    (sums_ref[...],) = over_rows(after_ref.shape[0], some, no_sums(1))
    attn_grad_ref[...] = nt(out_grad_ref[...], project_ref[...]).astype(BFLOAT)


def first_back_kernel(
    query_grad_ref,
    pair_grad_ref,
    query_weight_ref,
    pair_weight_ref,
    in_ref,
    modulation_ref,
    self_res_ref,
    out_ref,
    sums_ref,
    in_grad_ref,
):
    in_grad_ref[...] = nt(query_grad_ref[...], query_weight_ref[...]) + nt(
        pair_grad_ref[...], pair_weight_ref[...]
    )
    scale = 1.0 + block_of(modulation_ref, SCALE_SELF)

    def some(rows, carry):
        norm, rate = normed(in_ref[rows, :].astype(FLOAT))
        grad = in_grad_ref[rows, :]
        res_grad = self_res_ref[rows, :] + normed_back(grad * scale, norm, rate)
        out_ref[rows, :] = res_grad.astype(BFLOAT)
        return carry[0] + down(grad), carry[1] + down(grad * norm)

    shift_sum, scale_sum = over_rows(in_ref.shape[0], some, no_sums(2))
    sums_ref[:, :D] = shift_sum
    sums_ref[:, D:] = scale_sum


def left_half(weights):
    return weights, pl.BlockSpec((D, D), lambda step: (0, 0))


def right_half(weights):
    return weights, pl.BlockSpec((D, D), lambda step: (0, 1))


def frame_call(kernel, results, *operands, scratch=()):
    specs, arrays = [], []
    for operand in operands:
        if isinstance(operand, tuple):
            arrays.append(operand[0])
            specs.append(operand[1])
        else:
            arrays.append(operand)
            specs.append(whole_block(operand.shape))
    return pl.pallas_call(
        kernel,
        grid=(1,),
        in_specs=specs,
        out_specs=[whole_block(shape) for shape, _ in results],
        out_shape=[jax.ShapeDtypeStruct(shape, kind) for shape, kind in results],
        scratch_shapes=[pltpu.VMEM(shape, kind) for shape, kind in scratch],
        compiler_params=room(48),
        cost_estimate=LIGHT,
    )(*arrays)


MLP_TILE = 512


def mlp_both(cross_attn, project, after_self, modulation, out_grad, weights):
    frames = cross_attn.shape[0]
    far = lax.axis_size("far")
    rows = D // (4 * far)
    tiles = HALF // MLP_TILE
    once = dict(pipeline_mode=pl.Buffered(1))
    whole = pl.BlockSpec((frames, D), lambda half, tile: (0, 0), **once)
    square = (frames, D)
    return pl.pallas_call(
        mlp_kernel,
        grid=(2, tiles),
        in_specs=[
            whole,
            pl.BlockSpec((D, D), lambda half, tile: (0, 1), **once),
            whole,
            pl.BlockSpec((1, 6 * D), lambda half, tile: (0, 0)),
            whole,
            pl.BlockSpec((1, D, MLP_TILE), lambda half, tile: (half, 0, tile)),
            pl.BlockSpec((1, D, MLP_TILE), lambda half, tile: (half, 0, tile + tiles)),
        ],
        out_specs=[whole] * 4
        + [
            pl.BlockSpec((1, 3 * D), lambda half, tile: (0, 0)),
            pl.BlockSpec(
                (1, 4, far, 2, rows, MLP_TILE), lambda half, tile: (half, 0, 0, 0, 0, tile)
            ),
        ],
        out_shape=[
            jax.ShapeDtypeStruct(square, BFLOAT),
            jax.ShapeDtypeStruct(square, FLOAT),
            jax.ShapeDtypeStruct(square, BFLOAT),
            jax.ShapeDtypeStruct(square, BFLOAT),
            jax.ShapeDtypeStruct((1, 3 * D), FLOAT),
            jax.ShapeDtypeStruct((2, 4, far, 2, rows, HALF), BFLOAT),
        ],
        scratch_shapes=[
            pltpu.VMEM(square, BFLOAT),
            pltpu.VMEM(square, BFLOAT),
            pltpu.VMEM((D, frames), BFLOAT),
            pltpu.VMEM((D, frames), BFLOAT),
            pltpu.VMEM(square, FLOAT),
            pltpu.VMEM(square, FLOAT),
            pltpu.VMEM(square, FLOAT),
        ],
        compiler_params=room(48),
        cost_estimate=LIGHT,
    )(cross_attn, project, after_self, modulation, out_grad, weights, weights)


def per_device(
    block_in,
    text,
    timesteps,
    frame_mask,
    text_mask,
    cotangent,
    w_ada,
    w_qkv,
    w_out,
    w_cq,
    w_cout,
    w_ckv,
    w_fc1,
    w_fc2,
    row_state,
    col_state,
):
    clips = lax.axis_size(DP)
    devices = clips * 2
    data_at = lax.axis_index(DP)
    head_at = lax.axis_index("head")
    flat_at = data_at * 2 + head_at
    frames = block_in.shape[1]
    rows = w_qkv.shape[0]

    far = far_links()
    x_first = [far[0], row_link(), core_link()]
    y_first = [row_link(), far[0], core_link()]
    first = [
        gather_chain(
            with_bits(
                jnp.concatenate([w_qkv[:, :D], w_out, w_qkv[:, D:]], axis=1).astype(BFLOAT), "last"
            ),
            "last",
            far[:0:-1],
        )
    ]
    second = [
        gather_chain(
            with_bits(jnp.concatenate([w_cq, w_cout], axis=1).astype(BFLOAT), "last"),
            "last",
            far[:0:-1] + x_first,
        ),
        gather_chain(
            with_bits(w_ckv.astype(BFLOAT).reshape(w_ckv.shape[0], D), "columns"),
            "columns",
            far[:0:-1] + y_first,
        ),
    ]
    mlp_shard = jnp.concatenate([w_fc1.astype(BFLOAT), w_fc2.T.astype(BFLOAT)], axis=1)
    inputs = swap_place(block_in[0])
    joint_mask = jnp.concatenate([frame_mask[0], text_mask[0]])

    def add_step(link):
        return lambda state: state + cross(state, link)

    def project(steps):
        condition = embed_part(steps, flat_at * rows, rows)
        product = jnp.dot(condition, w_ada.astype(BFLOAT), preferred_element_type=FLOAT)
        return condition, product.reshape(clips // 2, 2, 6 * D)

    def keep_step(link):
        def step(state):
            condition, product = state
            bit = bit_of(link)
            dim = 1 if link == row_link() else dp_bits() - link[1].bit_length()
            kept = lax.dynamic_slice_in_dim(product, bit, 1, axis=dim)
            sent = lax.dynamic_slice_in_dim(product, 1 - bit, 1, axis=dim)
            product = kept + cross(sent, link)
            if link == row_link():
                product = product.reshape((2,) * (dp_bits() - 1) + (6 * D,))
            return condition, product

        return step

    def last_step(state):
        condition, product = state
        return condition, (product + cross(product, core_link())).reshape(1, 6 * D)

    steps = lax.dynamic_update_slice(jnp.zeros((clips,), jnp.int32), timesteps, (data_at,))
    timing = Chain(
        steps,
        [add_step(link) for link in [core_link()] + far_links()[1:] + far_links()[:1]]
        + [lambda steps: keep_step(row_link())(project(steps))]
        + [keep_step(link) for link in far_links()[1:] + far_links()[:1]]
        + [last_step],
    )
    far_count = len(far) - 1
    slots = far_count + 3
    for slot in range(slots):
        if slot < far_count:
            timing.advance(1 + (slot == 0) + (slot == far_count - 1))
        else:
            timing.advance((1, far_count, 2)[slot - far_count])
        if slot == far_count:
            joint = first[0].state
            first = [
                gather_chain(joint[..., : 2 * D], "last", x_first),
                gather_chain(joint[..., 2 * D :], "last", y_first),
            ]
        for chain in first:
            chain.advance()
        if slot >= 2:
            for chain in second:
                chain.advance()
        if slot == far_count - 1:
            inputs, mlp_shard, joint_mask, text = tie(
                [timing] + first + second, inputs, mlp_shard, joint_mask, text
            )
            mlp_all = lax.all_gather(mlp_shard, HEAD + DP, axis=0, tiled=True)
            masks = from_clip_core(joint_mask)
            clip_text = from_clip_core(text[0])
        elif slot < slots - 1:
            tie([timing] + first + second)
        else:
            wide = tie([timing] + first, w_ada, w_qkv, w_out, w_cq, w_cout, w_fc1, w_fc2)
            masters = [
                jnp.concatenate(wide[:5], axis=1),
                w_ckv.reshape(w_ckv.shape[0], D),
                jnp.concatenate([wide[5], wide[6].T], axis=1),
            ]
            (weight_squares,) = whole_call(weight_kernel, [(1, LINE)], *masters)
    condition, modulation = timing.finish()
    query_out, w_key_value = [chain.finish().reshape(D, 2 * D) for chain in first]
    square = (frames, D)
    core_at = data_at % 2
    own_allowed = lax.dynamic_slice_in_dim(masks, core_at * frames, frames)
    other_allowed = lax.dynamic_slice_in_dim(masks, (1 - core_at) * frames, frames)
    own_bias, other_bias = bias_of(own_allowed), bias_of(other_allowed)
    text_bias = bias_of(masks[2 * frames :])

    self_input, query, key_value = frame_call(
        first_kernel,
        [(square, BFLOAT), (square, BFLOAT), ((frames, 2 * D), BFLOAT)],
        inputs,
        modulation,
        left_half(query_out),
        w_key_value,
    )
    other_key_value = cross(key_value, core_link())
    query, other_key_value = tie(second, query, other_key_value)
    for chain in second:
        chain.advance()

    self_keys = [(key_value, own_bias), (other_key_value, other_bias)]
    self_attn, self_logs = attend(query, self_keys, plain_places)
    self_attn, cotangent = tie(second, self_attn, cotangent)
    swapped_cotangent = swap_only(cotangent[0])
    cross_pair, w_text = [chain.finish() for chain in second]
    cross_pair, w_text = cross_pair.reshape(D, 2 * D), w_text.reshape(DT, 2 * D)
    self_branch, after_self, cross_input, cross_query = frame_call(
        between_kernel,
        [(square, FLOAT), (square, FLOAT), (square, BFLOAT), (square, BFLOAT)],
        self_attn,
        right_half(query_out),
        inputs,
        modulation,
        left_half(cross_pair),
    )

    text_pair = nn(clip_text, w_text).astype(BFLOAT)
    text_keys = [(text_pair, text_bias)]
    cross_attn, cross_logs = attend(cross_query, text_keys, half_places)

    cross_attn, own, cotangent = tie([], cross_attn, on_own_chip(), cotangent)
    out_grad = jnp.where(own, cotangent[0], swapped_cotangent)
    block_out, cross_res_grad, cross_out_grad, cross_attn_grad, mlp_sums, mlp_part = mlp_both(
        cross_attn,
        cross_pair,
        after_self,
        modulation,
        out_grad,
        mlp_all.reshape(2, D, 2 * HALF),
    )
    mlp_part = lax.psum_scatter(
        mlp_part.reshape((8,) + mlp_part.shape[2:]),
        HEAD + ("near", "core"),
        scatter_dimension=0,
        tiled=False,
    )

    cross_query_grad, text_pair_grad = attend_back(
        cross_query, cross_attn, cross_attn_grad, cross_logs, text_keys, half_places
    )
    self_res_grad, self_out_grad, self_attn_grad, gate_self_grad = frame_call(
        between_back_kernel,
        [(square, FLOAT), (square, BFLOAT), (square, BFLOAT), ((1, D), FLOAT)],
        cross_query_grad,
        left_half(cross_pair),
        after_self,
        cross_res_grad,
        self_branch,
        modulation,
        right_half(query_out),
        scratch=[(square, FLOAT)],
    )

    query_grad, own_pair_grad, other_pair_grad = attend_back(
        query, self_attn, self_attn_grad, self_logs, self_keys, plain_places
    )
    pair_grad = (
        own_pair_grad.astype(FLOAT) + cross(other_pair_grad, core_link()).astype(FLOAT)
    ).astype(BFLOAT)
    last_chains = [
        scatter_chain(
            outer((self_input, query_grad), (self_attn, self_out_grad)), "last", False
        ),
        scatter_chain(outer((self_input, pair_grad)), "last", True),
    ]
    cross_query_grad, text_pair_grad = tie(last_chains, cross_query_grad, text_pair_grad)
    for chain in last_chains:
        chain.advance()
    cross_chains = [
        scatter_chain(
            outer((cross_input, cross_query_grad), (cross_attn, cross_out_grad)), "last", False
        ),
        scatter_chain(outer((clip_text, text_pair_grad)), "columns", True),
    ]
    query_grad, pair_grad = tie(cross_chains + last_chains, query_grad, pair_grad)
    for chain in last_chains + cross_chains:
        chain.advance()
    input_grad, self_sums = frame_call(
        first_back_kernel,
        [(square, BFLOAT), ((1, 2 * D), FLOAT)],
        query_grad,
        pair_grad,
        left_half(query_out),
        w_key_value,
        inputs,
        modulation,
        self_res_grad,
        scratch=[(square, FLOAT)],
    )
    modulation_grad = jnp.concatenate([self_sums, gate_self_grad, mlp_sums], axis=-1)

    def join_step(link):
        def step(state):
            other = cross(state, link)
            upper = bit_of(link) == 1
            dim = dp_bits() - 1 if link[0] == HEAD else dp_bits() - link[1].bit_length()
            low, high = jnp.where(upper, other, state), jnp.where(upper, state, other)
            return jnp.concatenate([low, high], axis=dim)

        return step

    far = far_links()
    shape = (1,) * dp_bits() + (6 * D,)
    joining = Chain(
        modulation_grad,
        [lambda state: (state + cross(state, core_link())).reshape(shape)]
        + [join_step(link) for link in far[:0:-1] + [far[0], row_link()]],
    )

    chains = last_chains + cross_chains
    joining.advance()
    block_out, input_grad, mlp_part = tie([joining] + chains, block_out, input_grad, mlp_part)
    mlp_raw = lax.psum_scatter(mlp_part, "far", scatter_dimension=0, tiled=False).astype(FLOAT)
    for chain in chains:
        chain.advance()
    joining.advance(len(far) - 1)
    block_out, input_grad = tie([joining] + chains, block_out, input_grad)
    for chain in chains:
        chain.advance()
    joining.advance(2)
    block_out, input_grad, mlp_raw = tie([joining] + chains, block_out, input_grad, mlp_raw)
    for chain in chains:
        chain.advance()
    block_out, input_grad = tie(chains, block_out, input_grad)
    own_results = jnp.stack([block_out, input_grad])
    swapped_results = swap_only(own_results)
    for chain in cross_chains:
        chain.advance()
    (swapped_results,) = tie(cross_chains, swapped_results)
    modulation_grad = joining.finish()
    ada_raw = jnp.einsum(
        "cr,cx->rx",
        condition.astype(FLOAT),
        modulation_grad.reshape(clips, 6 * D),
        precision=PRECISE,
    )

    cross_raw, ckv_raw = [chain.finish() for chain in cross_chains]
    query_out_raw, pair_raw = [chain.finish() for chain in last_chains]

    place = jnp.stack([data_at, head_at]).astype(jnp.int32)
    raw_grads = [ada_raw, query_out_raw, pair_raw, cross_raw, ckv_raw, mlp_raw]
    (statistics,) = whole_call(
        statistics_kernel, [(STAT_LINES, LINE)], place, weight_squares, *raw_grads, places=1
    )
    sums = sum_all(statistics)
    shapes = [(rows, columns) for columns in COL_SIZES[:5]]
    shapes += [masters[1].shape] + [(rows * 2, HALF)] * 2
    line = (1, LINE)
    row_new, col_new, norm, update_squares, *rest = whole_call(
        update_kernel,
        [(ROW_LINES, LINE), (COL_LINES, LINE), line, line]
        + shapes
        + [master.shape for master in masters],
        place,
        sums,
        row_state.reshape(ROW_LINES, LINE),
        col_state.reshape(COL_LINES, LINE),
        *raw_grads,
        places=1,
    )
    clipped, updates = list(rest[:8]), rest[8:]
    updated = whole_call(
        apply_kernel,
        shapes,
        sum_all(update_squares),
        sums[STAT_LINES - 2 : STAT_LINES - 1],
        *masters,
        *updates,
    )
    updated = list(updated)
    (own,) = tie([], own_results)
    late, _ = tie([], on_own_chip(), update_squares)
    block_out, input_grad = jnp.where(late, own, swapped_results)
    clipped[5] = clipped[5].reshape(w_ckv.shape)
    updated[5] = updated[5].reshape(w_ckv.shape)
    clipped[7] = clipped[7].T
    updated[7] = updated[7].T
    return (
        block_out[None],
        input_grad[None],
        norm[0, 0],
        row_new.reshape(-1),
        col_new.reshape(-1),
        *clipped,
        *updated,
    )


def solution(mesh):
    devices = mesh.devices
    refined = jax.sharding.Mesh(devices.reshape(devices.shape[0] // 4, 2, 2, 2), ALL)
    return jax.shard_map(
        per_device,
        mesh=refined,
        in_specs=(
            P(DP, "head", None),
            P(DP, None, None),
            P(DP),
            P(DP, None),
            P(DP, None),
            P(DP, "head", None),
            P(ALL, None),
            P(ALL, None),
            P(ALL, None),
            P(ALL, None),
            P(ALL, None),
            P(DP, None, "head"),
            P(DP, "head"),
            P("head", DP),
            P(),
            P(),
        ),
        out_specs=(
            P(DP, "head", None),
            P(DP, "head", None),
            P(),
            P(),
            P(),
            P(ALL, None),
            P(ALL, None),
            P(ALL, None),
            P(ALL, None),
            P(ALL, None),
            P(DP, None, "head"),
            P(DP, "head"),
            P("head", DP),
            P(ALL, None),
            P(ALL, None),
            P(ALL, None),
            P(ALL, None),
            P(ALL, None),
            P(DP, None, "head"),
            P(DP, "head"),
            P("head", DP),
        ),
        check_vma=False,
    )
```

```python
import functools

import jax
import jax.numpy as jnp
from jax import lax
from jax.experimental import pallas as pl
from jax.experimental.pallas import tpu as pltpu
from jax.sharding import PartitionSpec as P

D = 768
FF = 3072
DT = 1024
HD = 64
HALF = FF // 2

PRECISE = lax.Precision.HIGHEST
FLOAT = jnp.float32
BFLOAT = jnp.bfloat16
EPS_NORM = 1e-06
EPS_FACTOR = 1e-30
CLIP_NORM = 1.0
CLIP_UPDATE = 0.25
DECAY_RATE = 0.5
RELATIVE_RATE = 4.0
SCALE_FLOOR = 0.001
SCORE_SCALE = 0.125
MASKED_SCORE = -1e30
DP = ("far", "near", "core")
ALL = DP + ("head",)
HEAD = ("head",)
PAIR = 2 * HD
PAIRS = D // PAIR


def embed_part(steps, first, count):
    halfway = D // 2
    place = first + jnp.arange(count)
    freqs = jnp.exp(-jnp.log(10000.0) * (place % halfway).astype(FLOAT) / halfway)
    angles = steps.astype(FLOAT)[:, None] * freqs
    waves = jnp.where(place < halfway, jnp.cos(angles), jnp.sin(angles))
    return jax.nn.silu(waves).astype(BFLOAT)


def core_link():
    return (DP, 1)


def row_link():
    return (HEAD, 1)


def far_links():
    masks, mask = [], 2
    while mask < lax.axis_size(DP):
        masks.append(mask)
        mask = mask * 2
    return [(DP, mask) for mask in masks]


def dp_bits():
    return lax.axis_size(DP).bit_length() - 1


def bit_of(link):
    return (lax.axis_index(link[0]) // link[1]) % 2


def cross(values, link):
    pairs = [(place, place ^ link[1]) for place in range(lax.axis_size(link[0]))]
    return lax.ppermute(values, link[0], pairs)


def dim_of(link, head):
    if link[0] == HEAD:
        return {"first": 0, "last": dp_bits(), "columns": dp_bits() + 1}[head]
    return (1 if head == "first" else 0) + dp_bits() - link[1].bit_length()


def leading(head):
    return dp_bits() + (0 if head == "columns" else 1)


def grow(block, link, head):
    other = cross(block, link)
    upper = bit_of(link) == 1
    low = jnp.where(upper, other, block)
    high = jnp.where(upper, block, other)
    return jnp.concatenate([low, high], axis=dim_of(link, head))


def shrink(block, link, head, kind=BFLOAT):
    dim, bit = dim_of(link, head), bit_of(link)
    half = block.shape[dim] // 2
    kept = lax.dynamic_slice_in_dim(block, bit * half, half, axis=dim)
    sent = lax.dynamic_slice_in_dim(block, (1 - bit) * half, half, axis=dim)
    return (kept.astype(FLOAT) + cross(sent.astype(BFLOAT), link).astype(FLOAT)).astype(kind)


class Chain:
    def __init__(self, state, steps):
        self.state, self.steps = state, list(steps)

    def advance(self, count=1):
        for _ in range(min(count, len(self.steps))):
            self.state = self.steps.pop(0)(self.state)
        return self

    def finish(self):
        return self.advance(len(self.steps)).state


def tie(chains, *values):
    states, values = lax.optimization_barrier(([chain.state for chain in chains], values))
    for chain, state in zip(chains, states):
        chain.state = state
    return values


def gather_chain(block, head, links):
    return Chain(block, [lambda state, link=link: grow(state, link, head) for link in links])


def with_bits(shard, head):
    return shard.reshape((1,) * leading(head) + shard.shape)


def scatter_chain(matrix, head, row_early):
    bits = leading(head)
    rows, columns = matrix.shape[-2:]
    split = dp_bits() if head == "first" else bits
    block = matrix.reshape((2,) * bits + (rows // 2**split, columns))
    far = far_links()
    plane = [far[0], row_link()] if row_early else [row_link(), far[0]]
    order = [core_link()] + plane + far[1:]
    kinds = [BFLOAT] * (len(order) - 1) + [FLOAT]
    steps = [
        lambda state, link=link, kind=kind: shrink(state, link, head, kind)
        for link, kind in zip(order, kinds)
    ]
    return Chain(block, steps + [lambda state: state.reshape(state.shape[bits:])])


def sum_all(values):
    for link in [core_link(), row_link()] + far_links():
        values = values + cross(values, link)
    return values


def on_own_chip():
    return bit_of(core_link()) == bit_of(row_link())


def swap_only(values):
    pairs = []
    for place in range(lax.axis_size(DP)):
        for head in range(2):
            if place & 1 != head:
                pairs.append((place * 2 + head, ((place & ~1) | head) * 2 + (place & 1)))
    return lax.ppermute(values, ALL, pairs)


def swap_place(values):
    return jnp.where(on_own_chip(), values, swap_only(values))


def from_clip_core(values):
    pairs = []
    for place in range(0, lax.axis_size(DP), 2):
        for head in range(2):
            pairs.append(((place + head) * 2 + head, (place + 1 - head) * 2 + head))
    return jnp.where(on_own_chip(), values, lax.ppermute(values, ALL, pairs))


def nt(left, right):
    return lax.dot_general(left, right, (((1,), (1,)), ((), ())), preferred_element_type=FLOAT)


def nn(left, right):
    return lax.dot_general(left, right, (((1,), (0,)), ((), ())), preferred_element_type=FLOAT)


def lanes_of(length):
    return lax.broadcasted_iota(jnp.int32, (length, PAIR), 1)


def with_spare(pair, head, spare):
    lane = lanes_of(pair.shape[0])
    rest = jnp.where(lane == HD * (1 - head), spare, jnp.zeros_like(pair))
    return jnp.where(lane // HD == head, pair, rest)


def attend_kernel(blocks, *refs):
    query_ref = refs[0]
    key_refs, value_refs, bias_refs = refs[1 : 1 + 3 * blocks : 3], refs[2 : 2 + 3 * blocks : 3], refs[3 : 3 + 3 * blocks : 3]
    out_ref, log_ref = refs[1 + 3 * blocks :]
    queries = query_ref[...] * jnp.asarray(SCORE_SCALE, BFLOAT)
    one = jnp.ones((1, 1), BFLOAT)
    values_t = [ref[...].T for ref in value_refs]
    results, logs = [], []
    for head in range(2):
        query = with_spare(queries, head, one)
        scores = [
            nt(with_spare(key_ref[...], head, bias_ref[...]), query)
            for key_ref, bias_ref in zip(key_refs, bias_refs)
        ]
        peak = functools.reduce(
            jnp.maximum, [jnp.max(score, axis=0, keepdims=True) for score in scores]
        )
        total = None
        for score, value_t in zip(scores, values_t):
            probs = jnp.exp(score - peak).astype(BFLOAT)
            row = lax.broadcasted_iota(jnp.int32, value_t.shape, 0)
            term = nn(jnp.where(row // HD == head, value_t, one), probs)
            total = term if total is None else total + term
        weight = total[HD * (1 - head) : HD * (1 - head) + 1, :]
        results.append(total[HD * head : HD * (head + 1), :] / weight)
        logs.append(peak + jnp.log(weight))
    out_ref[...] = jnp.concatenate(results, axis=0).T.astype(BFLOAT)
    log_ref[0] = jnp.concatenate(logs, axis=0)


def back_kernel(blocks, places, *refs):
    query_ref, out_ref, grad_ref, log_ref = refs[:4]
    ins = refs[4 : 4 + 3 * blocks]
    key_refs, value_refs, bias_refs = ins[0::3], ins[1::3], ins[2::3]
    query_grad_ref = refs[4 + 3 * blocks]
    pair_grad_refs = refs[5 + 3 * blocks :]
    queries = query_ref[...] * jnp.asarray(SCORE_SCALE, BFLOAT)
    out_grad = grad_ref[...]
    zero = jnp.zeros((1, 1), BFLOAT)
    one = jnp.ones((1, 1), BFLOAT)
    product = out_ref[...].astype(FLOAT) * out_grad.astype(FLOAT)
    chooser = (
        lax.broadcasted_iota(jnp.int32, (8, PAIR), 1) // HD
        == lax.broadcasted_iota(jnp.int32, (8, PAIR), 0)
    ).astype(FLOAT)
    inner = lax.dot_general(
        chooser, product, (((1,), (1,)), ((), ())), precision=PRECISE, preferred_element_type=FLOAT
    )
    keys_t = [ref[...].T for ref in key_refs]
    query_parts = [None, None]
    for block in range(blocks):
        key_grad, value_grad = None, None
        for head in range(2):
            grad_here = with_spare(out_grad, head, zero)
            score = nt(
                with_spare(key_refs[block][...], head, bias_refs[block][...]),
                with_spare(queries, head, one),
            )
            probs = jnp.exp(score - log_ref[0, head : head + 1, :])
            prob_grad = nt(value_refs[block][...], grad_here)
            score_grad = (probs * (prob_grad - inner[head : head + 1, :])).astype(BFLOAT)
            value_term = nn(probs.astype(BFLOAT), grad_here)
            key_term = nn(score_grad, with_spare(queries, head, zero))
            query_term = nn(keys_t[block][HD * head : HD * (head + 1), :], score_grad)
            value_grad = value_term if value_grad is None else value_grad + value_term
            key_grad = key_term if key_grad is None else key_grad + key_term
            query_parts[head] = (
                query_term if query_parts[head] is None else query_parts[head] + query_term
            )
        key_at, value_at = places(pl.program_id(0))
        key_at = pl.multiple_of(key_at * PAIR, PAIR)
        value_at = pl.multiple_of(value_at * PAIR, PAIR)
        pair_grad_refs[block][:, pl.ds(key_at, PAIR)] = key_grad.astype(BFLOAT)
        pair_grad_refs[block][:, pl.ds(value_at, PAIR)] = value_grad.astype(BFLOAT)
    joined = jnp.concatenate(query_parts, axis=0) * SCORE_SCALE
    query_grad_ref[...] = joined.T.astype(BFLOAT)


def column_block(length):
    return pl.BlockSpec((length, PAIR), lambda pair: (0, pair))


def plain_places(pair):
    return pair, pair + PAIRS


def half_places(pair):
    half, part = pair // (PAIRS // 2), pair % (PAIRS // 2)
    return half * PAIRS + part, half * PAIRS + PAIRS // 2 + part


def whole_block(shape):
    return pl.BlockSpec(shape, lambda pair: (0,) * len(shape))


def log_block(frames):
    return pl.BlockSpec((1, 2, frames), lambda pair: (pair, 0, 0))


def key_specs(key_values, places):
    specs, operands = [], []
    for joint, bias in key_values:
        length = joint.shape[0]
        specs += [
            pl.BlockSpec((length, PAIR), lambda pair: (0, places(pair)[0])),
            pl.BlockSpec((length, PAIR), lambda pair: (0, places(pair)[1])),
            whole_block((length, PAIR)),
        ]
        operands += [joint, joint, bias]
    return specs, operands


def room(mebibytes):
    return pltpu.CompilerParams(vmem_limit_bytes=mebibytes * 1024 * 1024)


LIGHT = pl.CostEstimate(flops=1000, bytes_accessed=1000, transcendentals=0)


def attend(queries, key_values, places):
    frames, blocks = queries.shape[0], len(key_values)
    specs, operands = key_specs(key_values, places)
    return pl.pallas_call(
        functools.partial(attend_kernel, blocks),
        grid=(PAIRS,),
        in_specs=[column_block(frames)] + specs,
        out_specs=[column_block(frames), log_block(frames)],
        out_shape=[
            jax.ShapeDtypeStruct((frames, D), BFLOAT),
            jax.ShapeDtypeStruct((PAIRS, 2, frames), FLOAT),
        ],
        compiler_params=room(48),
        cost_estimate=LIGHT,
    )(queries, *operands)


def attend_back(queries, out, out_grad, logs, key_values, places):
    frames, blocks = queries.shape[0], len(key_values)
    specs, operands = key_specs(key_values, places)
    return pl.pallas_call(
        functools.partial(back_kernel, blocks, places),
        grid=(PAIRS,),
        in_specs=[column_block(frames)] * 3 + [log_block(frames)] + specs,
        out_specs=[column_block(frames)] + [whole_block(joint.shape) for joint, _ in key_values],
        out_shape=[jax.ShapeDtypeStruct((frames, D), BFLOAT)]
        + [jax.ShapeDtypeStruct(joint.shape, BFLOAT) for joint, _ in key_values],
        compiler_params=room(48),
        cost_estimate=LIGHT,
    )(queries, out, out_grad, logs, *operands)


def outer_kernel(*refs):
    out_ref, count = refs[-1], len(refs) // 2
    at = 0
    for place in range(count):
        left, right = refs[2 * place], refs[2 * place + 1]
        width = right.shape[1]
        product = lax.dot_general(
            left[...], right[...], (((0,), (0,)), ((), ())), preferred_element_type=FLOAT
        )
        out_ref[:, at : at + width] = product.astype(BFLOAT)
        at += width


def outer(*pairs):
    operands = [matrix for pair in pairs for matrix in pair]
    shape = (pairs[0][0].shape[1], sum(right.shape[1] for _, right in pairs))
    return pl.pallas_call(
        outer_kernel,
        out_shape=jax.ShapeDtypeStruct(shape, BFLOAT),
        compiler_params=room(48),
        cost_estimate=LIGHT,
    )(*operands)


def bias_of(allowed):
    column = jnp.where(allowed > 0, 0.0, MASKED_SCORE).astype(BFLOAT)
    return jnp.broadcast_to(column[:, None], (allowed.shape[0], PAIR))


LINE = 128
ROW_SIZES = [D, D, D, D, D, DT, D, FF]
COL_SIZES = [6 * D, 3 * D, D, D, D, 2 * D, FF, D]
ROW_LINES = sum(ROW_SIZES) // LINE
COL_LINES = sum(COL_SIZES) // LINE
STAT_LINES = ROW_LINES + COL_LINES + 2


def starts_of(sizes, first):
    starts = []
    for size in sizes:
        starts.append(first)
        first += size // LINE
    return starts


ROW_STARTS = starts_of(ROW_SIZES, 0)
COL_STARTS = starts_of(COL_SIZES, ROW_LINES)


def lines_at(line, shape):
    return lax.broadcasted_iota(jnp.int32, shape, 1) + line * LINE


def down_lines(column, offset, lines):
    shape = (column.shape[0], LINE)
    wanted = lax.broadcasted_iota(jnp.int32, shape, 0) + offset
    return [
        jnp.sum(jnp.where(lines_at(line, shape) == wanted, column, 0.0), axis=0, keepdims=True)
        for line in range(lines)
    ]


def from_lines(lines, offset, count):
    shape = (count, LINE)
    wanted = lax.broadcasted_iota(jnp.int32, shape, 0) + offset
    total = jnp.zeros(shape, FLOAT)
    for line in range(lines.shape[0]):
        here = jnp.where(lines_at(line, shape) == wanted, lines[line : line + 1, :], 0.0)
        total = total + here
    return jnp.sum(total, axis=1, keepdims=True)


def pieces_of(grad_refs):
    ada, query_out, key_value, cross_pair, text_pair, mlp = grad_refs
    return [
        [(ada, 0, 6 * D)],
        [(query_out, 0, D), (key_value, 0, 2 * D)],
        [(query_out, D, D)],
        [(cross_pair, 0, D)],
        [(cross_pair, D, D)],
        [(text_pair, 0, D)],
        [(mlp.at[0], 0, HALF)],
        [(mlp.at[1], 0, HALF)],
    ]


def joined_pieces(refs):
    square, text_pair, mlp = refs
    parts, at = [], 0
    for place in range(5):
        parts.append((square, at, COL_SIZES[place]))
        at += COL_SIZES[place]
    return parts + [(text_pair, 0, D), (mlp, 0, HALF), (mlp, HALF, HALF)]


def statistics_kernel(place_ref, weight_ref, *refs):
    grad_refs, out_ref = refs[:6], refs[6]
    data_at, head_at = place_ref[0], place_ref[1]
    flat_at = data_at * 2 + head_at
    out_ref[STAT_LINES - 2 : STAT_LINES - 1, :] = weight_ref[...]
    out_ref[STAT_LINES - 1 : STAT_LINES, :] = jnp.zeros((1, LINE), FLOAT)
    for place, parts in enumerate(pieces_of(grad_refs)):
        across, down = 0.0, []
        for ref, first, columns in parts:
            rows = ref.shape[0]
            wide = jnp.zeros((rows, LINE), FLOAT)
            for line in range(columns // LINE):
                piece = ref[:, first + line * LINE : first + (line + 1) * LINE]
                square = piece * piece
                wide = wide + square
                down.append(jnp.sum(square, axis=0, keepdims=True))
            across = across + jnp.sum(wide, axis=1, keepdims=True)
        offset = (flat_at if place < 5 else data_at) * rows
        row_start, col_start = ROW_STARTS[place], COL_STARTS[place]
        if place == 7:
            row_start, col_start = col_start, row_start
        row_lines = (COL_SIZES if place == 7 else ROW_SIZES)[place] // LINE
        for line, entry in enumerate(down_lines(across, offset, row_lines)):
            out_ref[row_start + line : row_start + line + 1, :] = entry
        groups = {5: 2}.get(place, 1)
        size = len(down) // groups
        for line, entry in enumerate(down):
            if place < 5:
                out_ref[col_start + line : col_start + line + 1, :] = entry
            else:
                for half in range(2):
                    at = col_start + (line // size * 2 + half) * size + line % size
                    out_ref[at : at + 1, :] = jnp.where(head_at == half, entry, 0.0)


def lane_of(lines, lane):
    shape = (1, LINE)
    here = lax.broadcasted_iota(jnp.int32, shape, 1) == lane
    return jnp.sum(jnp.where(here, lines, 0.0), axis=1, keepdims=True)


def update_kernel(place_ref, sums_ref, row_ref, col_ref, *refs):
    grad_refs, outs = refs[:6], refs[6:]
    row_out, col_out, norm_out, total_out = outs[:4]
    clipped_refs, update_refs = outs[4:12], joined_pieces(outs[12:15])
    data_at, head_at = place_ref[0], place_ref[1]
    flat_at = data_at * 2 + head_at
    row_sums = sums_ref[0:ROW_LINES, :]
    square_total = jnp.sum(jnp.sum(row_sums, axis=0, keepdims=True), axis=1, keepdims=True)
    norm = jnp.sqrt(square_total)
    factor = 1.0 / jnp.maximum(1.0, norm / CLIP_NORM)
    norm_out[...] = jnp.broadcast_to(norm, (1, LINE))
    square_factor = factor * factor
    lane = lax.broadcasted_iota(jnp.int32, (1, LINE), 1)
    totals = jnp.zeros((1, LINE), FLOAT)
    for place, parts in enumerate(pieces_of(grad_refs)):
        rows_len, cols_len = ROW_SIZES[place], COL_SIZES[place]
        row_from, row_to = ROW_STARTS[place], ROW_STARTS[place] + rows_len // LINE
        col_from, col_to = COL_STARTS[place], COL_STARTS[place] + cols_len // LINE
        new_row = DECAY_RATE * row_ref[row_from:row_to, :] + (1.0 - DECAY_RATE) * (
            square_factor * sums_ref[row_from:row_to, :] / float(cols_len) + EPS_FACTOR
        )
        col_from, col_to = col_from - ROW_LINES, col_to - ROW_LINES
        new_col = DECAY_RATE * col_ref[col_from:col_to, :] + (1.0 - DECAY_RATE) * (
            square_factor
            * sums_ref[ROW_LINES + col_from : ROW_LINES + col_to, :]
            / float(rows_len)
            + EPS_FACTOR
        )
        row_out[row_from:row_to, :] = new_row
        col_out[col_from:col_to, :] = new_col
        row_mean = (
            jnp.sum(jnp.sum(new_row, axis=0, keepdims=True), axis=1, keepdims=True) / rows_len
        )
        rows = parts[0][0].shape[0]
        offset = (flat_at if place < 5 else data_at) * rows
        if place == 7:
            down = lax.rsqrt(from_lines(new_col, offset, rows))
            across = jnp.where(head_at == 0, new_row[:12], new_row[12:])
            across = lax.rsqrt(across / row_mean)
        else:
            down = lax.rsqrt(from_lines(new_row, offset, rows) / row_mean)
            if place == 5:
                keys = jnp.where(head_at == 0, new_col[0:3], new_col[3:6])
                values = jnp.where(head_at == 0, new_col[6:9], new_col[9:12])
                across = lax.rsqrt(jnp.concatenate([keys, values], axis=0))
            elif place == 6:
                across = lax.rsqrt(jnp.where(head_at == 0, new_col[:12], new_col[12:]))
            else:
                across = lax.rsqrt(new_col)
        square = jnp.zeros((rows, LINE), FLOAT)
        line_at = 0
        for ref, first, columns in parts:
            for line in range(columns // LINE):
                piece = ref[:, first + line * LINE : first + (line + 1) * LINE] * factor
                update = piece * (down * across[line_at : line_at + 1, :])
                clipped_refs[place][:, line_at * LINE : (line_at + 1) * LINE] = piece
                update_ref, update_at, _ = update_refs[place]
                update_at += line_at * LINE
                update_ref[:, update_at : update_at + LINE] = update
                square = square + update * update
                line_at += 1
        total = jnp.sum(jnp.sum(square, axis=0, keepdims=True), axis=1, keepdims=True)
        totals = jnp.where(lane == place, total, totals)
    total_out[...] = totals


def apply_kernel(total_ref, weight_ref, *refs):
    master_refs, update_refs = joined_pieces(refs[:3]), joined_pieces(refs[3:6])
    for place in range(8):
        entries = float(ROW_SIZES[place] * COL_SIZES[place])
        total = lane_of(total_ref[...], place)
        weight = lane_of(weight_ref[...], place)
        limit = jnp.maximum(1.0, jnp.sqrt(total / entries) / CLIP_UPDATE)
        rate = RELATIVE_RATE * jnp.maximum(SCALE_FLOOR, jnp.sqrt(weight / entries))
        scale = rate / limit
        ref, at, columns = master_refs[place]
        update = update_refs[place][0][:, at : at + columns]
        refs[6 + place][...] = ref[:, at : at + columns] - scale * update


def weight_kernel(*refs):
    lane = lax.broadcasted_iota(jnp.int32, (1, LINE), 1)
    totals = jnp.zeros((1, LINE), FLOAT)
    for place in range(8):
        ref, at, columns = joined_pieces(refs[:3])[place]
        matrix = ref[:, at : at + columns]
        total = jnp.sum(jnp.sum(matrix * matrix, axis=0, keepdims=True), axis=1, keepdims=True)
        totals = jnp.where(lane == place, total, totals)
    refs[3][...] = totals


def whole_call(kernel, shapes, *operands, places=0):
    memory = [pl.BlockSpec(memory_space=pltpu.SMEM)] * places
    memory += [pl.BlockSpec(memory_space=pltpu.VMEM)] * (len(operands) - places)
    return pl.pallas_call(
        kernel,
        in_specs=memory,
        out_specs=[pl.BlockSpec(memory_space=pltpu.VMEM)] * len(shapes),
        out_shape=[jax.ShapeDtypeStruct(shape, FLOAT) for shape in shapes],
        compiler_params=room(48),
        cost_estimate=LIGHT,
    )(*operands)


GELU_WIDTH = 0.7978845608028654
GELU_CUBE = 0.044715


def gelu_parts(values):
    square = values * values
    bend = jnp.tanh(values * (GELU_WIDTH + GELU_WIDTH * GELU_CUBE * square))
    half = 0.5 + 0.5 * bend
    slope = GELU_WIDTH + 3.0 * GELU_WIDTH * GELU_CUBE * square
    return values * half, half + (0.5 * values) * (1.0 - bend * bend) * slope


ROWS = 512
SHIFT_SELF, SCALE_SELF, GATE_SELF, SHIFT_MLP, SCALE_MLP, GATE_MLP = range(6)


def block_of(modulation_ref, place):
    return modulation_ref[:, place * D : (place + 1) * D]


def over_rows(frames, body, start=None):
    def step(place, carry):
        return body(pl.ds(pl.multiple_of(place * ROWS, ROWS), ROWS), carry)

    return lax.fori_loop(0, frames // ROWS, step, start)


def normed(values):
    centered = values - jnp.mean(values, axis=-1, keepdims=True)
    rate = lax.rsqrt(jnp.mean(centered * centered, axis=-1, keepdims=True) + EPS_NORM)
    return centered * rate, rate


def normed_back(grad, norm, rate):
    inner = jnp.mean(grad * norm, axis=-1, keepdims=True)
    return rate * (grad - jnp.mean(grad, axis=-1, keepdims=True) - norm * inner)


def down(values):
    return jnp.sum(values, axis=0, keepdims=True)


def no_sums(count):
    return (jnp.zeros((1, D), FLOAT),) * count


def first_kernel(
    in_ref, modulation_ref, query_weight_ref, pair_weight_ref, self_input_ref, query_ref, pair_ref
):
    shift = block_of(modulation_ref, SHIFT_SELF)
    scale = 1.0 + block_of(modulation_ref, SCALE_SELF)

    def some(rows, carry):
        norm, _ = normed(in_ref[rows, :].astype(FLOAT))
        self_input_ref[rows, :] = (norm * scale + shift).astype(BFLOAT)
        return carry

    over_rows(in_ref.shape[0], some)
    pair_ref[...] = nn(self_input_ref[...], pair_weight_ref[...]).astype(BFLOAT)
    query_ref[...] = nn(self_input_ref[...], query_weight_ref[...]).astype(BFLOAT)


def between_kernel(
    attn_ref,
    project_ref,
    in_ref,
    modulation_ref,
    query_weight_ref,
    branch_ref,
    after_ref,
    cross_input_ref,
    query_ref,
):
    branch_ref[...] = nn(attn_ref[...], project_ref[...])
    gate = block_of(modulation_ref, GATE_SELF)

    def some(rows, carry):
        after = in_ref[rows, :].astype(FLOAT) + gate * branch_ref[rows, :]
        after_ref[rows, :] = after
        norm, _ = normed(after)
        cross_input_ref[rows, :] = norm.astype(BFLOAT)
        return carry

    over_rows(in_ref.shape[0], some)
    query_ref[...] = nn(cross_input_ref[...], query_weight_ref[...]).astype(BFLOAT)


def mlp_kernel(
    attn_ref,
    project_ref,
    after_ref,
    modulation_ref,
    out_grad_ref,
    fc1_ref,
    fc2_ref,
    out_ref,
    res_grad_ref,
    cross_out_grad_ref,
    attn_grad_ref,
    sums_ref,
    part_ref,
    input_ref,
    grad_ref,
    input_t,
    grad_t,
    joined_ref,
    branch_ref,
    in_grad_ref,
):
    step = pl.program_id(0) * pl.num_programs(1) + pl.program_id(1)
    last = pl.num_programs(0) * pl.num_programs(1) - 1
    frames = attn_ref.shape[0]
    gate = block_of(modulation_ref, GATE_MLP)
    scale = 1.0 + block_of(modulation_ref, SCALE_MLP)

    @pl.when(step == 0)
    def _():
        shift = block_of(modulation_ref, SHIFT_MLP)
        joined_ref[...] = after_ref[...] + nn(attn_ref[...], project_ref[...])

        def some(rows, carry):
            norm, _ = normed(joined_ref[rows, :])
            input_ref[rows, :] = (norm * scale + shift).astype(BFLOAT)
            grad_ref[rows, :] = (gate * out_grad_ref[rows, :].astype(FLOAT)).astype(BFLOAT)
            return carry

        over_rows(frames, some)
        input_t[...] = input_ref[...].T
        grad_t[...] = grad_ref[...].T

    fc1, fc2 = fc1_ref[0], fc2_ref[0]
    act, slope = gelu_parts(nn(input_ref[...], fc1))
    act = act.astype(BFLOAT)
    pre_grad = (nn(grad_ref[...], fc2) * slope).astype(BFLOAT)
    branch, in_grad = nt(act, fc2), nt(pre_grad, fc1)

    @pl.when(step == 0)
    def _():
        branch_ref[...] = branch
        in_grad_ref[...] = in_grad

    @pl.when(step > 0)
    def _():
        branch_ref[...] += branch
        in_grad_ref[...] += in_grad

    far, size = part_ref.shape[2], part_ref.shape[4]
    for kind, product in enumerate((nn(input_t[...], pre_grad), nn(grad_t[...], act))):
        product = product.astype(BFLOAT)
        for place in range(4 * far):
            part_ref[0, place % 4, place // 4, kind] = product[place * size : (place + 1) * size]

    @pl.when(step == last)
    def _():
        def some(rows, carry):
            gate_sum, shift_sum, scale_sum = carry
            joined, branch_here = joined_ref[rows, :], branch_ref[rows, :]
            out_grad, in_grad_here = out_grad_ref[rows, :].astype(FLOAT), in_grad_ref[rows, :]
            out_ref[rows, :] = (joined + gate * branch_here).astype(BFLOAT)
            norm, rate = normed(joined)
            res_grad = out_grad + normed_back(in_grad_here * scale, norm, rate)
            res_grad_ref[rows, :] = res_grad
            cross_out_grad_ref[rows, :] = res_grad.astype(BFLOAT)
            return (
                gate_sum + down(out_grad * branch_here),
                shift_sum + down(in_grad_here),
                scale_sum + down(in_grad_here * norm),
            )

        gate_sum, shift_sum, scale_sum = over_rows(frames, some, no_sums(3))
        sums_ref[:, :D] = shift_sum
        sums_ref[:, D : 2 * D] = scale_sum
        sums_ref[:, 2 * D :] = gate_sum
        attn_grad_ref[...] = nt(cross_out_grad_ref[...], project_ref[...]).astype(BFLOAT)


def between_back_kernel(
    query_grad_ref,
    query_weight_ref,
    after_ref,
    res_grad_ref,
    branch_ref,
    modulation_ref,
    project_ref,
    self_res_ref,
    out_grad_ref,
    attn_grad_ref,
    sums_ref,
    in_grad_ref,
):
    in_grad_ref[...] = nt(query_grad_ref[...], query_weight_ref[...])
    gate = block_of(modulation_ref, GATE_SELF)

    def some(rows, carry):
        norm, rate = normed(after_ref[rows, :])
        res_grad = res_grad_ref[rows, :] + normed_back(in_grad_ref[rows, :], norm, rate)
        self_res_ref[rows, :] = res_grad
        out_grad_ref[rows, :] = (gate * res_grad).astype(BFLOAT)
        return (carry[0] + down(res_grad * branch_ref[rows, :]),)

    (sums_ref[...],) = over_rows(after_ref.shape[0], some, no_sums(1))
    attn_grad_ref[...] = nt(out_grad_ref[...], project_ref[...]).astype(BFLOAT)


def first_back_kernel(
    query_grad_ref,
    pair_grad_ref,
    query_weight_ref,
    pair_weight_ref,
    in_ref,
    modulation_ref,
    self_res_ref,
    out_ref,
    sums_ref,
    in_grad_ref,
):
    in_grad_ref[...] = nt(query_grad_ref[...], query_weight_ref[...]) + nt(
        pair_grad_ref[...], pair_weight_ref[...]
    )
    scale = 1.0 + block_of(modulation_ref, SCALE_SELF)

    def some(rows, carry):
        norm, rate = normed(in_ref[rows, :].astype(FLOAT))
        grad = in_grad_ref[rows, :]
        res_grad = self_res_ref[rows, :] + normed_back(grad * scale, norm, rate)
        out_ref[rows, :] = res_grad.astype(BFLOAT)
        return carry[0] + down(grad), carry[1] + down(grad * norm)

    shift_sum, scale_sum = over_rows(in_ref.shape[0], some, no_sums(2))
    sums_ref[:, :D] = shift_sum
    sums_ref[:, D:] = scale_sum


def left_half(weights):
    return weights, pl.BlockSpec((D, D), lambda step: (0, 0))


def right_half(weights):
    return weights, pl.BlockSpec((D, D), lambda step: (0, 1))


def frame_call(kernel, results, *operands, scratch=()):
    specs, arrays = [], []
    for operand in operands:
        if isinstance(operand, tuple):
            arrays.append(operand[0])
            specs.append(operand[1])
        else:
            arrays.append(operand)
            specs.append(whole_block(operand.shape))
    return pl.pallas_call(
        kernel,
        grid=(1,),
        in_specs=specs,
        out_specs=[whole_block(shape) for shape, _ in results],
        out_shape=[jax.ShapeDtypeStruct(shape, kind) for shape, kind in results],
        scratch_shapes=[pltpu.VMEM(shape, kind) for shape, kind in scratch],
        compiler_params=room(48),
        cost_estimate=LIGHT,
    )(*arrays)


MLP_TILE = 768


def mlp_both(cross_attn, project, after_self, modulation, out_grad, weights):
    frames = cross_attn.shape[0]
    far = lax.axis_size("far")
    rows = D // (4 * far)
    tiles = HALF // MLP_TILE
    once = dict(pipeline_mode=pl.Buffered(1))
    whole = pl.BlockSpec((frames, D), lambda half, tile: (0, 0), **once)
    square = (frames, D)
    return pl.pallas_call(
        mlp_kernel,
        grid=(2, tiles),
        in_specs=[
            whole,
            pl.BlockSpec((D, D), lambda half, tile: (0, 1), **once),
            whole,
            pl.BlockSpec((1, 6 * D), lambda half, tile: (0, 0)),
            whole,
            pl.BlockSpec((1, D, MLP_TILE), lambda half, tile: (half, 0, tile)),
            pl.BlockSpec((1, D, MLP_TILE), lambda half, tile: (half, 0, tile + tiles)),
        ],
        out_specs=[whole] * 4
        + [
            pl.BlockSpec((1, 3 * D), lambda half, tile: (0, 0)),
            pl.BlockSpec(
                (1, 4, far, 2, rows, MLP_TILE), lambda half, tile: (half, 0, 0, 0, 0, tile)
            ),
        ],
        out_shape=[
            jax.ShapeDtypeStruct(square, BFLOAT),
            jax.ShapeDtypeStruct(square, FLOAT),
            jax.ShapeDtypeStruct(square, BFLOAT),
            jax.ShapeDtypeStruct(square, BFLOAT),
            jax.ShapeDtypeStruct((1, 3 * D), FLOAT),
            jax.ShapeDtypeStruct((2, 4, far, 2, rows, HALF), BFLOAT),
        ],
        scratch_shapes=[
            pltpu.VMEM(square, BFLOAT),
            pltpu.VMEM(square, BFLOAT),
            pltpu.VMEM((D, frames), BFLOAT),
            pltpu.VMEM((D, frames), BFLOAT),
            pltpu.VMEM(square, FLOAT),
            pltpu.VMEM(square, FLOAT),
            pltpu.VMEM(square, FLOAT),
        ],
        compiler_params=room(48),
        cost_estimate=LIGHT,
    )(cross_attn, project, after_self, modulation, out_grad, weights, weights)


def per_device(
    block_in,
    text,
    timesteps,
    frame_mask,
    text_mask,
    cotangent,
    w_ada,
    w_qkv,
    w_out,
    w_cq,
    w_cout,
    w_ckv,
    w_fc1,
    w_fc2,
    row_state,
    col_state,
):
    clips = lax.axis_size(DP)
    devices = clips * 2
    data_at = lax.axis_index(DP)
    head_at = lax.axis_index("head")
    flat_at = data_at * 2 + head_at
    frames = block_in.shape[1]
    rows = w_qkv.shape[0]

    far = far_links()
    x_first = [far[0], row_link(), core_link()]
    y_first = [row_link(), far[0], core_link()]
    first = [
        gather_chain(
            with_bits(
                jnp.concatenate([w_qkv[:, :D], w_out, w_qkv[:, D:]], axis=1).astype(BFLOAT), "last"
            ),
            "last",
            far[:0:-1],
        )
    ]
    second = [
        gather_chain(
            with_bits(jnp.concatenate([w_cq, w_cout], axis=1).astype(BFLOAT), "last"),
            "last",
            far[:0:-1] + x_first,
        ),
        gather_chain(
            with_bits(w_ckv.astype(BFLOAT).reshape(w_ckv.shape[0], D), "columns"),
            "columns",
            far[:0:-1] + y_first,
        ),
    ]
    mlp_shard = jnp.concatenate([w_fc1.astype(BFLOAT), w_fc2.T.astype(BFLOAT)], axis=1)
    inputs = swap_place(block_in[0])
    joint_mask = jnp.concatenate([frame_mask[0], text_mask[0]])

    def add_step(link):
        return lambda state: state + cross(state, link)

    def project(steps):
        condition = embed_part(steps, flat_at * rows, rows)
        product = jnp.dot(condition, w_ada.astype(BFLOAT), preferred_element_type=FLOAT)
        return condition, product.reshape(clips // 2, 2, 6 * D)

    def keep_step(link):
        def step(state):
            condition, product = state
            bit = bit_of(link)
            dim = 1 if link == row_link() else dp_bits() - link[1].bit_length()
            kept = lax.dynamic_slice_in_dim(product, bit, 1, axis=dim)
            sent = lax.dynamic_slice_in_dim(product, 1 - bit, 1, axis=dim)
            product = kept + cross(sent, link)
            if link == row_link():
                product = product.reshape((2,) * (dp_bits() - 1) + (6 * D,))
            return condition, product

        return step

    def last_step(state):
        condition, product = state
        return condition, (product + cross(product, core_link())).reshape(1, 6 * D)

    steps = lax.dynamic_update_slice(jnp.zeros((clips,), jnp.int32), timesteps, (data_at,))
    timing = Chain(
        steps,
        [add_step(link) for link in [core_link()] + far_links()[1:] + far_links()[:1]]
        + [lambda steps: keep_step(row_link())(project(steps))]
        + [keep_step(link) for link in far_links()[1:] + far_links()[:1]]
        + [last_step],
    )
    far_count = len(far) - 1
    slots = far_count + 3
    for slot in range(slots):
        if slot < far_count:
            timing.advance(1 + (slot == 0) + (slot == far_count - 1))
        else:
            timing.advance((1, far_count, 2)[slot - far_count])
        if slot == far_count:
            joint = first[0].state
            first = [
                gather_chain(joint[..., : 2 * D], "last", x_first),
                gather_chain(joint[..., 2 * D :], "last", y_first),
            ]
        for chain in first:
            chain.advance()
        if slot >= 2:
            for chain in second:
                chain.advance()
        if slot == far_count - 1:
            inputs, mlp_shard, joint_mask, text = tie(
                [timing] + first + second, inputs, mlp_shard, joint_mask, text
            )
            mlp_all = lax.all_gather(mlp_shard, HEAD + DP, axis=0, tiled=True)
            masks = from_clip_core(joint_mask)
            clip_text = from_clip_core(text[0])
        elif slot < slots - 1:
            tie([timing] + first + second)
        else:
            wide = tie([timing] + first, w_ada, w_qkv, w_out, w_cq, w_cout, w_fc1, w_fc2)
            masters = [
                jnp.concatenate(wide[:5], axis=1),
                w_ckv.reshape(w_ckv.shape[0], D),
                jnp.concatenate([wide[5], wide[6].T], axis=1),
            ]
            (weight_squares,) = whole_call(weight_kernel, [(1, LINE)], *masters)
    condition, modulation = timing.finish()
    query_out, w_key_value = [chain.finish().reshape(D, 2 * D) for chain in first]
    square = (frames, D)
    core_at = data_at % 2
    own_allowed = lax.dynamic_slice_in_dim(masks, core_at * frames, frames)
    other_allowed = lax.dynamic_slice_in_dim(masks, (1 - core_at) * frames, frames)
    own_bias, other_bias = bias_of(own_allowed), bias_of(other_allowed)
    text_bias = bias_of(masks[2 * frames :])

    self_input, query, key_value = frame_call(
        first_kernel,
        [(square, BFLOAT), (square, BFLOAT), ((frames, 2 * D), BFLOAT)],
        inputs,
        modulation,
        left_half(query_out),
        w_key_value,
    )
    other_key_value = cross(key_value, core_link())
    query, other_key_value = tie(second, query, other_key_value)
    for chain in second:
        chain.advance()

    self_keys = [(key_value, own_bias), (other_key_value, other_bias)]
    self_attn, self_logs = attend(query, self_keys, plain_places)
    self_attn, cotangent = tie(second, self_attn, cotangent)
    swapped_cotangent = swap_only(cotangent[0])
    cross_pair, w_text = [chain.finish() for chain in second]
    cross_pair, w_text = cross_pair.reshape(D, 2 * D), w_text.reshape(DT, 2 * D)
    self_branch, after_self, cross_input, cross_query = frame_call(
        between_kernel,
        [(square, FLOAT), (square, FLOAT), (square, BFLOAT), (square, BFLOAT)],
        self_attn,
        right_half(query_out),
        inputs,
        modulation,
        left_half(cross_pair),
    )

    text_pair = nn(clip_text, w_text).astype(BFLOAT)
    text_keys = [(text_pair, text_bias)]
    cross_attn, cross_logs = attend(cross_query, text_keys, half_places)

    cross_attn, own, cotangent = tie([], cross_attn, on_own_chip(), cotangent)
    out_grad = jnp.where(own, cotangent[0], swapped_cotangent)
    block_out, cross_res_grad, cross_out_grad, cross_attn_grad, mlp_sums, mlp_part = mlp_both(
        cross_attn,
        cross_pair,
        after_self,
        modulation,
        out_grad,
        mlp_all.reshape(2, D, 2 * HALF),
    )
    mlp_part = lax.psum_scatter(
        mlp_part.reshape((8,) + mlp_part.shape[2:]),
        HEAD + ("near", "core"),
        scatter_dimension=0,
        tiled=False,
    )

    cross_query_grad, text_pair_grad = attend_back(
        cross_query, cross_attn, cross_attn_grad, cross_logs, text_keys, half_places
    )
    self_res_grad, self_out_grad, self_attn_grad, gate_self_grad = frame_call(
        between_back_kernel,
        [(square, FLOAT), (square, BFLOAT), (square, BFLOAT), ((1, D), FLOAT)],
        cross_query_grad,
        left_half(cross_pair),
        after_self,
        cross_res_grad,
        self_branch,
        modulation,
        right_half(query_out),
        scratch=[(square, FLOAT)],
    )

    query_grad, own_pair_grad, other_pair_grad = attend_back(
        query, self_attn, self_attn_grad, self_logs, self_keys, plain_places
    )
    pair_grad = (
        own_pair_grad.astype(FLOAT) + cross(other_pair_grad, core_link()).astype(FLOAT)
    ).astype(BFLOAT)
    last_chains = [
        scatter_chain(
            outer((self_input, query_grad), (self_attn, self_out_grad)), "last", False
        ),
        scatter_chain(outer((self_input, pair_grad)), "last", True),
    ]
    cross_query_grad, text_pair_grad = tie(last_chains, cross_query_grad, text_pair_grad)
    for chain in last_chains:
        chain.advance()
    cross_chains = [
        scatter_chain(
            outer((cross_input, cross_query_grad), (cross_attn, cross_out_grad)), "last", False
        ),
        scatter_chain(outer((clip_text, text_pair_grad)), "columns", True),
    ]
    query_grad, pair_grad = tie(cross_chains + last_chains, query_grad, pair_grad)
    for chain in last_chains + cross_chains:
        chain.advance()
    input_grad, self_sums = frame_call(
        first_back_kernel,
        [(square, BFLOAT), ((1, 2 * D), FLOAT)],
        query_grad,
        pair_grad,
        left_half(query_out),
        w_key_value,
        inputs,
        modulation,
        self_res_grad,
        scratch=[(square, FLOAT)],
    )
    modulation_grad = jnp.concatenate([self_sums, gate_self_grad, mlp_sums], axis=-1)

    def join_step(link):
        def step(state):
            other = cross(state, link)
            upper = bit_of(link) == 1
            dim = dp_bits() - 1 if link[0] == HEAD else dp_bits() - link[1].bit_length()
            low, high = jnp.where(upper, other, state), jnp.where(upper, state, other)
            return jnp.concatenate([low, high], axis=dim)

        return step

    far = far_links()
    shape = (1,) * dp_bits() + (6 * D,)
    joining = Chain(
        modulation_grad,
        [lambda state: (state + cross(state, core_link())).reshape(shape)]
        + [join_step(link) for link in far[:0:-1] + [far[0], row_link()]],
    )

    chains = last_chains + cross_chains
    joining.advance()
    block_out, input_grad, mlp_part = tie([joining] + chains, block_out, input_grad, mlp_part)
    mlp_raw = lax.psum_scatter(mlp_part, "far", scatter_dimension=0, tiled=False).astype(FLOAT)
    for chain in chains:
        chain.advance()
    joining.advance(len(far) - 1)
    block_out, input_grad = tie([joining] + chains, block_out, input_grad)
    for chain in chains:
        chain.advance()
    joining.advance(2)
    block_out, input_grad, mlp_raw = tie([joining] + chains, block_out, input_grad, mlp_raw)
    for chain in chains:
        chain.advance()
    block_out, input_grad = tie(chains, block_out, input_grad)
    own_results = jnp.stack([block_out, input_grad])
    swapped_results = swap_only(own_results)
    for chain in cross_chains:
        chain.advance()
    (swapped_results,) = tie(cross_chains, swapped_results)
    modulation_grad = joining.finish()
    ada_raw = jnp.einsum(
        "cr,cx->rx",
        condition.astype(FLOAT),
        modulation_grad.reshape(clips, 6 * D),
        precision=PRECISE,
    )

    cross_raw, ckv_raw = [chain.finish() for chain in cross_chains]
    query_out_raw, pair_raw = [chain.finish() for chain in last_chains]

    place = jnp.stack([data_at, head_at]).astype(jnp.int32)
    raw_grads = [ada_raw, query_out_raw, pair_raw, cross_raw, ckv_raw, mlp_raw]
    (statistics,) = whole_call(
        statistics_kernel, [(STAT_LINES, LINE)], place, weight_squares, *raw_grads, places=1
    )
    sums = sum_all(statistics)
    shapes = [(rows, columns) for columns in COL_SIZES[:5]]
    shapes += [masters[1].shape] + [(rows * 2, HALF)] * 2
    line = (1, LINE)
    row_new, col_new, norm, update_squares, *rest = whole_call(
        update_kernel,
        [(ROW_LINES, LINE), (COL_LINES, LINE), line, line]
        + shapes
        + [master.shape for master in masters],
        place,
        sums,
        row_state.reshape(ROW_LINES, LINE),
        col_state.reshape(COL_LINES, LINE),
        *raw_grads,
        places=1,
    )
    clipped, updates = list(rest[:8]), rest[8:]
    updated = whole_call(
        apply_kernel,
        shapes,
        sum_all(update_squares),
        sums[STAT_LINES - 2 : STAT_LINES - 1],
        *masters,
        *updates,
    )
    updated = list(updated)
    (own,) = tie([], own_results)
    late, _ = tie([], on_own_chip(), update_squares)
    block_out, input_grad = jnp.where(late, own, swapped_results)
    clipped[5] = clipped[5].reshape(w_ckv.shape)
    updated[5] = updated[5].reshape(w_ckv.shape)
    clipped[7] = clipped[7].T
    updated[7] = updated[7].T
    return (
        block_out[None],
        input_grad[None],
        norm[0, 0],
        row_new.reshape(-1),
        col_new.reshape(-1),
        *clipped,
        *updated,
    )


def solution(mesh):
    devices = mesh.devices
    refined = jax.sharding.Mesh(devices.reshape(devices.shape[0] // 4, 2, 2, 2), ALL)
    return jax.shard_map(
        per_device,
        mesh=refined,
        in_specs=(
            P(DP, "head", None),
            P(DP, None, None),
            P(DP),
            P(DP, None),
            P(DP, None),
            P(DP, "head", None),
            P(ALL, None),
            P(ALL, None),
            P(ALL, None),
            P(ALL, None),
            P(ALL, None),
            P(DP, None, "head"),
            P(DP, "head"),
            P("head", DP),
            P(),
            P(),
        ),
        out_specs=(
            P(DP, "head", None),
            P(DP, "head", None),
            P(),
            P(),
            P(),
            P(ALL, None),
            P(ALL, None),
            P(ALL, None),
            P(ALL, None),
            P(ALL, None),
            P(DP, None, "head"),
            P(DP, "head"),
            P("head", DP),
            P(ALL, None),
            P(ALL, None),
            P(ALL, None),
            P(ALL, None),
            P(ALL, None),
            P(DP, None, "head"),
            P(DP, "head"),
            P("head", DP),
        ),
        check_vma=False,
    )
```

```python
import functools

import jax
import jax.numpy as jnp
from jax import lax
from jax.experimental import pallas as pl
from jax.experimental.pallas import tpu as pltpu
from jax.sharding import PartitionSpec as P

D = 768
FF = 3072
DT = 1024
HD = 64
HALF = FF // 2

PRECISE = lax.Precision.HIGHEST
FLOAT = jnp.float32
BFLOAT = jnp.bfloat16
EPS_NORM = 1e-06
EPS_FACTOR = 1e-30
CLIP_NORM = 1.0
CLIP_UPDATE = 0.25
DECAY_RATE = 0.5
RELATIVE_RATE = 4.0
SCALE_FLOOR = 0.001
SCORE_SCALE = 0.125
MASKED_SCORE = -1e30
DP = ("far", "near", "core")
ALL = DP + ("head",)
HEAD = ("head",)
PAIR = 2 * HD
PAIRS = D // PAIR


def embed_part(steps, first, count):
    halfway = D // 2
    place = first + jnp.arange(count)
    freqs = jnp.exp(-jnp.log(10000.0) * (place % halfway).astype(FLOAT) / halfway)
    angles = steps.astype(FLOAT)[:, None] * freqs
    waves = jnp.where(place < halfway, jnp.cos(angles), jnp.sin(angles))
    return jax.nn.silu(waves).astype(BFLOAT)


def core_link():
    return (DP, 1)


def row_link():
    return (HEAD, 1)


def far_links():
    masks, mask = [], 2
    while mask < lax.axis_size(DP):
        masks.append(mask)
        mask = mask * 2
    return [(DP, mask) for mask in masks]


def dp_bits():
    return lax.axis_size(DP).bit_length() - 1


def bit_of(link):
    return (lax.axis_index(link[0]) // link[1]) % 2


def cross(values, link):
    pairs = [(place, place ^ link[1]) for place in range(lax.axis_size(link[0]))]
    return lax.ppermute(values, link[0], pairs)


def dim_of(link, head):
    if link[0] == HEAD:
        return {"first": 0, "last": dp_bits(), "columns": dp_bits() + 1}[head]
    return (1 if head == "first" else 0) + dp_bits() - link[1].bit_length()


def leading(head):
    return dp_bits() + (0 if head == "columns" else 1)


def grow(block, link, head):
    other = cross(block, link)
    upper = bit_of(link) == 1
    low = jnp.where(upper, other, block)
    high = jnp.where(upper, block, other)
    return jnp.concatenate([low, high], axis=dim_of(link, head))


def shrink(block, link, head, kind=BFLOAT):
    dim, bit = dim_of(link, head), bit_of(link)
    half = block.shape[dim] // 2
    kept = lax.dynamic_slice_in_dim(block, bit * half, half, axis=dim)
    sent = lax.dynamic_slice_in_dim(block, (1 - bit) * half, half, axis=dim)
    return (kept.astype(FLOAT) + cross(sent.astype(BFLOAT), link).astype(FLOAT)).astype(kind)


class Chain:
    def __init__(self, state, steps):
        self.state, self.steps = state, list(steps)

    def advance(self, count=1):
        for _ in range(min(count, len(self.steps))):
            self.state = self.steps.pop(0)(self.state)
        return self

    def finish(self):
        return self.advance(len(self.steps)).state


def tie(chains, *values):
    states, values = lax.optimization_barrier(([chain.state for chain in chains], values))
    for chain, state in zip(chains, states):
        chain.state = state
    return values


def gather_chain(block, head, links):
    return Chain(block, [lambda state, link=link: grow(state, link, head) for link in links])


def with_bits(shard, head):
    return shard.reshape((1,) * leading(head) + shard.shape)


def scatter_chain(matrix, head, row_early):
    bits = leading(head)
    rows, columns = matrix.shape[-2:]
    split = dp_bits() if head == "first" else bits
    block = matrix.reshape((2,) * bits + (rows // 2**split, columns))
    far = far_links()
    plane = [far[0], row_link()] if row_early else [row_link(), far[0]]
    order = [core_link()] + plane + far[1:]
    kinds = [BFLOAT] * (len(order) - 1) + [FLOAT]
    steps = [
        lambda state, link=link, kind=kind: shrink(state, link, head, kind)
        for link, kind in zip(order, kinds)
    ]
    return Chain(block, steps + [lambda state: state.reshape(state.shape[bits:])])


def sum_all(values):
    for link in [core_link()] + far_links() + [row_link()]:
        values = values + cross(values, link)
    return values


def on_own_chip():
    return bit_of(core_link()) == bit_of(row_link())


def swap_only(values):
    pairs = []
    for place in range(lax.axis_size(DP)):
        for head in range(2):
            if place & 1 != head:
                pairs.append((place * 2 + head, ((place & ~1) | head) * 2 + (place & 1)))
    return lax.ppermute(values, ALL, pairs)


def swap_place(values):
    return jnp.where(on_own_chip(), values, swap_only(values))


def from_clip_core(values):
    pairs = []
    for place in range(0, lax.axis_size(DP), 2):
        for head in range(2):
            pairs.append(((place + head) * 2 + head, (place + 1 - head) * 2 + head))
    return jnp.where(on_own_chip(), values, lax.ppermute(values, ALL, pairs))


def nt(left, right):
    return lax.dot_general(left, right, (((1,), (1,)), ((), ())), preferred_element_type=FLOAT)


def nn(left, right):
    return lax.dot_general(left, right, (((1,), (0,)), ((), ())), preferred_element_type=FLOAT)


def lanes_of(length):
    return lax.broadcasted_iota(jnp.int32, (length, PAIR), 1)


def with_spare(pair, head, spare):
    lane = lanes_of(pair.shape[0])
    rest = jnp.where(lane == HD * (1 - head), spare, jnp.zeros_like(pair))
    return jnp.where(lane // HD == head, pair, rest)


def attend_kernel(blocks, *refs):
    query_ref = refs[0]
    key_refs, value_refs, bias_refs = refs[1 : 1 + 3 * blocks : 3], refs[2 : 2 + 3 * blocks : 3], refs[3 : 3 + 3 * blocks : 3]
    out_ref, log_ref = refs[1 + 3 * blocks :]
    queries = query_ref[...] * jnp.asarray(SCORE_SCALE, BFLOAT)
    one = jnp.ones((1, 1), BFLOAT)
    values_t = [ref[...].T for ref in value_refs]
    results, logs = [], []
    for head in range(2):
        query = with_spare(queries, head, one)
        scores = [
            nt(with_spare(key_ref[...], head, bias_ref[...]), query)
            for key_ref, bias_ref in zip(key_refs, bias_refs)
        ]
        peak = functools.reduce(
            jnp.maximum, [jnp.max(score, axis=0, keepdims=True) for score in scores]
        )
        total = None
        for score, value_t in zip(scores, values_t):
            probs = jnp.exp(score - peak).astype(BFLOAT)
            row = lax.broadcasted_iota(jnp.int32, value_t.shape, 0)
            term = nn(jnp.where(row // HD == head, value_t, one), probs)
            total = term if total is None else total + term
        weight = total[HD * (1 - head) : HD * (1 - head) + 1, :]
        results.append(total[HD * head : HD * (head + 1), :] / weight)
        logs.append(peak + jnp.log(weight))
    out_ref[...] = jnp.concatenate(results, axis=0).T.astype(BFLOAT)
    log_ref[0] = jnp.concatenate(logs, axis=0)


def back_kernel(blocks, places, *refs):
    query_ref, out_ref, grad_ref, log_ref = refs[:4]
    ins = refs[4 : 4 + 3 * blocks]
    key_refs, value_refs, bias_refs = ins[0::3], ins[1::3], ins[2::3]
    query_grad_ref = refs[4 + 3 * blocks]
    pair_grad_refs = refs[5 + 3 * blocks :]
    queries = query_ref[...] * jnp.asarray(SCORE_SCALE, BFLOAT)
    out_grad = grad_ref[...]
    zero = jnp.zeros((1, 1), BFLOAT)
    one = jnp.ones((1, 1), BFLOAT)
    product = out_ref[...].astype(FLOAT) * out_grad.astype(FLOAT)
    chooser = (
        lax.broadcasted_iota(jnp.int32, (8, PAIR), 1) // HD
        == lax.broadcasted_iota(jnp.int32, (8, PAIR), 0)
    ).astype(FLOAT)
    inner = lax.dot_general(
        chooser, product, (((1,), (1,)), ((), ())), precision=PRECISE, preferred_element_type=FLOAT
    )
    keys_t = [ref[...].T for ref in key_refs]
    query_parts = [None, None]
    for block in range(blocks):
        key_grad, value_grad = None, None
        for head in range(2):
            grad_here = with_spare(out_grad, head, zero)
            score = nt(
                with_spare(key_refs[block][...], head, bias_refs[block][...]),
                with_spare(queries, head, one),
            )
            probs = jnp.exp(score - log_ref[0, head : head + 1, :])
            prob_grad = nt(value_refs[block][...], grad_here)
            score_grad = (probs * (prob_grad - inner[head : head + 1, :])).astype(BFLOAT)
            value_term = nn(probs.astype(BFLOAT), grad_here)
            key_term = nn(score_grad, with_spare(queries, head, zero))
            query_term = nn(keys_t[block][HD * head : HD * (head + 1), :], score_grad)
            value_grad = value_term if value_grad is None else value_grad + value_term
            key_grad = key_term if key_grad is None else key_grad + key_term
            query_parts[head] = (
                query_term if query_parts[head] is None else query_parts[head] + query_term
            )
        key_at, value_at = places(pl.program_id(0))
        key_at = pl.multiple_of(key_at * PAIR, PAIR)
        value_at = pl.multiple_of(value_at * PAIR, PAIR)
        pair_grad_refs[block][:, pl.ds(key_at, PAIR)] = key_grad.astype(BFLOAT)
        pair_grad_refs[block][:, pl.ds(value_at, PAIR)] = value_grad.astype(BFLOAT)
    joined = jnp.concatenate(query_parts, axis=0) * SCORE_SCALE
    query_grad_ref[...] = joined.T.astype(BFLOAT)


def column_block(length):
    return pl.BlockSpec((length, PAIR), lambda pair: (0, pair))


def plain_places(pair):
    return pair, pair + PAIRS


def half_places(pair):
    half, part = pair // (PAIRS // 2), pair % (PAIRS // 2)
    return half * PAIRS + part, half * PAIRS + PAIRS // 2 + part


def whole_block(shape):
    return pl.BlockSpec(shape, lambda pair: (0,) * len(shape))


def log_block(frames):
    return pl.BlockSpec((1, 2, frames), lambda pair: (pair, 0, 0))


def key_specs(key_values, places):
    specs, operands = [], []
    for joint, bias in key_values:
        length = joint.shape[0]
        specs += [
            pl.BlockSpec((length, PAIR), lambda pair: (0, places(pair)[0])),
            pl.BlockSpec((length, PAIR), lambda pair: (0, places(pair)[1])),
            whole_block((length, PAIR)),
        ]
        operands += [joint, joint, bias]
    return specs, operands


def room(mebibytes):
    return pltpu.CompilerParams(vmem_limit_bytes=mebibytes * 1024 * 1024)


LIGHT = pl.CostEstimate(flops=1000, bytes_accessed=1000, transcendentals=0)


def attend(queries, key_values, places):
    frames, blocks = queries.shape[0], len(key_values)
    specs, operands = key_specs(key_values, places)
    return pl.pallas_call(
        functools.partial(attend_kernel, blocks),
        grid=(PAIRS,),
        in_specs=[column_block(frames)] + specs,
        out_specs=[column_block(frames), log_block(frames)],
        out_shape=[
            jax.ShapeDtypeStruct((frames, D), BFLOAT),
            jax.ShapeDtypeStruct((PAIRS, 2, frames), FLOAT),
        ],
        compiler_params=room(48),
        cost_estimate=LIGHT,
    )(queries, *operands)


def attend_back(queries, out, out_grad, logs, key_values, places):
    frames, blocks = queries.shape[0], len(key_values)
    specs, operands = key_specs(key_values, places)
    return pl.pallas_call(
        functools.partial(back_kernel, blocks, places),
        grid=(PAIRS,),
        in_specs=[column_block(frames)] * 3 + [log_block(frames)] + specs,
        out_specs=[column_block(frames)] + [whole_block(joint.shape) for joint, _ in key_values],
        out_shape=[jax.ShapeDtypeStruct((frames, D), BFLOAT)]
        + [jax.ShapeDtypeStruct(joint.shape, BFLOAT) for joint, _ in key_values],
        compiler_params=room(48),
        cost_estimate=LIGHT,
    )(queries, out, out_grad, logs, *operands)


def outer_kernel(*refs):
    out_ref, count = refs[-1], len(refs) // 2
    at = 0
    for place in range(count):
        left, right = refs[2 * place], refs[2 * place + 1]
        width = right.shape[1]
        product = lax.dot_general(
            left[...], right[...], (((0,), (0,)), ((), ())), preferred_element_type=FLOAT
        )
        out_ref[:, at : at + width] = product.astype(BFLOAT)
        at += width


def outer(*pairs):
    operands = [matrix for pair in pairs for matrix in pair]
    shape = (pairs[0][0].shape[1], sum(right.shape[1] for _, right in pairs))
    return pl.pallas_call(
        outer_kernel,
        out_shape=jax.ShapeDtypeStruct(shape, BFLOAT),
        compiler_params=room(48),
        cost_estimate=LIGHT,
    )(*operands)


def bias_of(allowed):
    column = jnp.where(allowed > 0, 0.0, MASKED_SCORE).astype(BFLOAT)
    return jnp.broadcast_to(column[:, None], (allowed.shape[0], PAIR))


LINE = 128
ROW_SIZES = [D, D, D, D, D, DT, D, FF]
COL_SIZES = [6 * D, 3 * D, D, D, D, 2 * D, FF, D]
ROW_LINES = sum(ROW_SIZES) // LINE
COL_LINES = sum(COL_SIZES) // LINE
STAT_LINES = ROW_LINES + COL_LINES + 2


def starts_of(sizes, first):
    starts = []
    for size in sizes:
        starts.append(first)
        first += size // LINE
    return starts


ROW_STARTS = starts_of(ROW_SIZES, 0)
COL_STARTS = starts_of(COL_SIZES, ROW_LINES)


def lines_at(line, shape):
    return lax.broadcasted_iota(jnp.int32, shape, 1) + line * LINE


def down_lines(column, offset, lines):
    shape = (column.shape[0], LINE)
    wanted = lax.broadcasted_iota(jnp.int32, shape, 0) + offset
    return [
        jnp.sum(jnp.where(lines_at(line, shape) == wanted, column, 0.0), axis=0, keepdims=True)
        for line in range(lines)
    ]


def from_lines(lines, offset, count):
    shape = (count, LINE)
    wanted = lax.broadcasted_iota(jnp.int32, shape, 0) + offset
    total = jnp.zeros(shape, FLOAT)
    for line in range(lines.shape[0]):
        here = jnp.where(lines_at(line, shape) == wanted, lines[line : line + 1, :], 0.0)
        total = total + here
    return jnp.sum(total, axis=1, keepdims=True)


def pieces_of(grad_refs):
    ada, query_out, key_value, cross_pair, text_pair, mlp = grad_refs
    return [
        [(ada, 0, 6 * D)],
        [(query_out, 0, D), (key_value, 0, 2 * D)],
        [(query_out, D, D)],
        [(cross_pair, 0, D)],
        [(cross_pair, D, D)],
        [(text_pair, 0, D)],
        [(mlp.at[0], 0, HALF)],
        [(mlp.at[1], 0, HALF)],
    ]


def joined_pieces(refs):
    square, text_pair, mlp = refs
    parts, at = [], 0
    for place in range(5):
        parts.append((square, at, COL_SIZES[place]))
        at += COL_SIZES[place]
    return parts + [(text_pair, 0, D), (mlp, 0, HALF), (mlp, HALF, HALF)]


def statistics_kernel(place_ref, weight_ref, *refs):
    grad_refs, out_ref = refs[:6], refs[6]
    data_at, head_at = place_ref[0], place_ref[1]
    flat_at = data_at * 2 + head_at
    out_ref[STAT_LINES - 2 : STAT_LINES - 1, :] = weight_ref[...]
    out_ref[STAT_LINES - 1 : STAT_LINES, :] = jnp.zeros((1, LINE), FLOAT)
    for place, parts in enumerate(pieces_of(grad_refs)):
        across, down = 0.0, []
        for ref, first, columns in parts:
            rows = ref.shape[0]
            wide = jnp.zeros((rows, LINE), FLOAT)
            for line in range(columns // LINE):
                piece = ref[:, first + line * LINE : first + (line + 1) * LINE]
                square = piece * piece
                wide = wide + square
                down.append(jnp.sum(square, axis=0, keepdims=True))
            across = across + jnp.sum(wide, axis=1, keepdims=True)
        offset = (flat_at if place < 5 else data_at) * rows
        row_start, col_start = ROW_STARTS[place], COL_STARTS[place]
        if place == 7:
            row_start, col_start = col_start, row_start
        row_lines = (COL_SIZES if place == 7 else ROW_SIZES)[place] // LINE
        for line, entry in enumerate(down_lines(across, offset, row_lines)):
            out_ref[row_start + line : row_start + line + 1, :] = entry
        groups = {5: 2}.get(place, 1)
        size = len(down) // groups
        for line, entry in enumerate(down):
            if place < 5:
                out_ref[col_start + line : col_start + line + 1, :] = entry
            else:
                for half in range(2):
                    at = col_start + (line // size * 2 + half) * size + line % size
                    out_ref[at : at + 1, :] = jnp.where(head_at == half, entry, 0.0)


def lane_of(lines, lane):
    shape = (1, LINE)
    here = lax.broadcasted_iota(jnp.int32, shape, 1) == lane
    return jnp.sum(jnp.where(here, lines, 0.0), axis=1, keepdims=True)


def update_kernel(place_ref, sums_ref, row_ref, col_ref, *refs):
    grad_refs, outs = refs[:6], refs[6:]
    row_out, col_out, norm_out, total_out = outs[:4]
    clipped_refs, update_refs = outs[4:12], joined_pieces(outs[12:15])
    data_at, head_at = place_ref[0], place_ref[1]
    flat_at = data_at * 2 + head_at
    row_sums = sums_ref[0:ROW_LINES, :]
    square_total = jnp.sum(jnp.sum(row_sums, axis=0, keepdims=True), axis=1, keepdims=True)
    norm = jnp.sqrt(square_total)
    factor = 1.0 / jnp.maximum(1.0, norm / CLIP_NORM)
    norm_out[...] = jnp.broadcast_to(norm, (1, LINE))
    square_factor = factor * factor
    lane = lax.broadcasted_iota(jnp.int32, (1, LINE), 1)
    totals = jnp.zeros((1, LINE), FLOAT)
    for place, parts in enumerate(pieces_of(grad_refs)):
        rows_len, cols_len = ROW_SIZES[place], COL_SIZES[place]
        row_from, row_to = ROW_STARTS[place], ROW_STARTS[place] + rows_len // LINE
        col_from, col_to = COL_STARTS[place], COL_STARTS[place] + cols_len // LINE
        new_row = DECAY_RATE * row_ref[row_from:row_to, :] + (1.0 - DECAY_RATE) * (
            square_factor * sums_ref[row_from:row_to, :] / float(cols_len) + EPS_FACTOR
        )
        col_from, col_to = col_from - ROW_LINES, col_to - ROW_LINES
        new_col = DECAY_RATE * col_ref[col_from:col_to, :] + (1.0 - DECAY_RATE) * (
            square_factor
            * sums_ref[ROW_LINES + col_from : ROW_LINES + col_to, :]
            / float(rows_len)
            + EPS_FACTOR
        )
        row_out[row_from:row_to, :] = new_row
        col_out[col_from:col_to, :] = new_col
        row_mean = (
            jnp.sum(jnp.sum(new_row, axis=0, keepdims=True), axis=1, keepdims=True) / rows_len
        )
        rows = parts[0][0].shape[0]
        offset = (flat_at if place < 5 else data_at) * rows
        if place == 7:
            down = lax.rsqrt(from_lines(new_col, offset, rows))
            across = jnp.where(head_at == 0, new_row[:12], new_row[12:])
            across = lax.rsqrt(across / row_mean)
        else:
            down = lax.rsqrt(from_lines(new_row, offset, rows) / row_mean)
            if place == 5:
                keys = jnp.where(head_at == 0, new_col[0:3], new_col[3:6])
                values = jnp.where(head_at == 0, new_col[6:9], new_col[9:12])
                across = lax.rsqrt(jnp.concatenate([keys, values], axis=0))
            elif place == 6:
                across = lax.rsqrt(jnp.where(head_at == 0, new_col[:12], new_col[12:]))
            else:
                across = lax.rsqrt(new_col)
        square = jnp.zeros((rows, LINE), FLOAT)
        line_at = 0
        for ref, first, columns in parts:
            for line in range(columns // LINE):
                piece = ref[:, first + line * LINE : first + (line + 1) * LINE] * factor
                update = piece * (down * across[line_at : line_at + 1, :])
                clipped_refs[place][:, line_at * LINE : (line_at + 1) * LINE] = piece
                update_ref, update_at, _ = update_refs[place]
                update_at += line_at * LINE
                update_ref[:, update_at : update_at + LINE] = update
                square = square + update * update
                line_at += 1
        total = jnp.sum(jnp.sum(square, axis=0, keepdims=True), axis=1, keepdims=True)
        totals = jnp.where(lane == place, total, totals)
    total_out[...] = totals


def apply_kernel(total_ref, weight_ref, *refs):
    master_refs, update_refs = joined_pieces(refs[:3]), joined_pieces(refs[3:6])
    for place in range(8):
        entries = float(ROW_SIZES[place] * COL_SIZES[place])
        total = lane_of(total_ref[...], place)
        weight = lane_of(weight_ref[...], place)
        limit = jnp.maximum(1.0, jnp.sqrt(total / entries) / CLIP_UPDATE)
        rate = RELATIVE_RATE * jnp.maximum(SCALE_FLOOR, jnp.sqrt(weight / entries))
        scale = rate / limit
        ref, at, columns = master_refs[place]
        update = update_refs[place][0][:, at : at + columns]
        refs[6 + place][...] = ref[:, at : at + columns] - scale * update


def weight_kernel(*refs):
    lane = lax.broadcasted_iota(jnp.int32, (1, LINE), 1)
    totals = jnp.zeros((1, LINE), FLOAT)
    for place in range(8):
        ref, at, columns = joined_pieces(refs[:3])[place]
        matrix = ref[:, at : at + columns]
        total = jnp.sum(jnp.sum(matrix * matrix, axis=0, keepdims=True), axis=1, keepdims=True)
        totals = jnp.where(lane == place, total, totals)
    refs[3][...] = totals


def whole_call(kernel, shapes, *operands, places=0):
    memory = [pl.BlockSpec(memory_space=pltpu.SMEM)] * places
    memory += [pl.BlockSpec(memory_space=pltpu.VMEM)] * (len(operands) - places)
    return pl.pallas_call(
        kernel,
        in_specs=memory,
        out_specs=[pl.BlockSpec(memory_space=pltpu.VMEM)] * len(shapes),
        out_shape=[jax.ShapeDtypeStruct(shape, FLOAT) for shape in shapes],
        compiler_params=room(48),
        cost_estimate=LIGHT,
    )(*operands)


GELU_WIDTH = 0.7978845608028654
GELU_CUBE = 0.044715


def gelu_parts(values):
    square = values * values
    bend = jnp.tanh(values * (GELU_WIDTH + GELU_WIDTH * GELU_CUBE * square))
    half = 0.5 + 0.5 * bend
    slope = GELU_WIDTH + 3.0 * GELU_WIDTH * GELU_CUBE * square
    return values * half, half + (0.5 * values) * (1.0 - bend * bend) * slope


ROWS = 512
SHIFT_SELF, SCALE_SELF, GATE_SELF, SHIFT_MLP, SCALE_MLP, GATE_MLP = range(6)


def block_of(modulation_ref, place):
    return modulation_ref[:, place * D : (place + 1) * D]


def over_rows(frames, body, start=None):
    def step(place, carry):
        return body(pl.ds(pl.multiple_of(place * ROWS, ROWS), ROWS), carry)

    return lax.fori_loop(0, frames // ROWS, step, start)


def normed(values):
    centered = values - jnp.mean(values, axis=-1, keepdims=True)
    rate = lax.rsqrt(jnp.mean(centered * centered, axis=-1, keepdims=True) + EPS_NORM)
    return centered * rate, rate


def normed_back(grad, norm, rate):
    inner = jnp.mean(grad * norm, axis=-1, keepdims=True)
    return rate * (grad - jnp.mean(grad, axis=-1, keepdims=True) - norm * inner)


def down(values):
    return jnp.sum(values, axis=0, keepdims=True)


def no_sums(count):
    return (jnp.zeros((1, D), FLOAT),) * count


def first_kernel(
    in_ref, modulation_ref, query_weight_ref, pair_weight_ref, self_input_ref, query_ref, pair_ref
):
    shift = block_of(modulation_ref, SHIFT_SELF)
    scale = 1.0 + block_of(modulation_ref, SCALE_SELF)

    def some(rows, carry):
        norm, _ = normed(in_ref[rows, :].astype(FLOAT))
        self_input_ref[rows, :] = (norm * scale + shift).astype(BFLOAT)
        return carry

    over_rows(in_ref.shape[0], some)
    pair_ref[...] = nn(self_input_ref[...], pair_weight_ref[...]).astype(BFLOAT)
    query_ref[...] = nn(self_input_ref[...], query_weight_ref[...]).astype(BFLOAT)


def between_kernel(
    attn_ref,
    project_ref,
    in_ref,
    modulation_ref,
    query_weight_ref,
    branch_ref,
    after_ref,
    cross_input_ref,
    query_ref,
):
    branch_ref[...] = nn(attn_ref[...], project_ref[...])
    gate = block_of(modulation_ref, GATE_SELF)

    def some(rows, carry):
        after = in_ref[rows, :].astype(FLOAT) + gate * branch_ref[rows, :]
        after_ref[rows, :] = after
        norm, _ = normed(after)
        cross_input_ref[rows, :] = norm.astype(BFLOAT)
        return carry

    over_rows(in_ref.shape[0], some)
    query_ref[...] = nn(cross_input_ref[...], query_weight_ref[...]).astype(BFLOAT)


def mlp_kernel(
    attn_ref,
    project_ref,
    after_ref,
    modulation_ref,
    out_grad_ref,
    fc1_ref,
    fc2_ref,
    out_ref,
    res_grad_ref,
    cross_out_grad_ref,
    attn_grad_ref,
    sums_ref,
    part_ref,
    input_ref,
    grad_ref,
    input_t,
    grad_t,
    joined_ref,
    branch_ref,
    in_grad_ref,
):
    step = pl.program_id(0) * pl.num_programs(1) + pl.program_id(1)
    last = pl.num_programs(0) * pl.num_programs(1) - 1
    frames = attn_ref.shape[0]
    gate = block_of(modulation_ref, GATE_MLP)
    scale = 1.0 + block_of(modulation_ref, SCALE_MLP)

    @pl.when(step == 0)
    def _():
        shift = block_of(modulation_ref, SHIFT_MLP)
        joined_ref[...] = after_ref[...] + nn(attn_ref[...], project_ref[...])

        def some(rows, carry):
            norm, _ = normed(joined_ref[rows, :])
            input_ref[rows, :] = (norm * scale + shift).astype(BFLOAT)
            grad_ref[rows, :] = (gate * out_grad_ref[rows, :].astype(FLOAT)).astype(BFLOAT)
            return carry

        over_rows(frames, some)
        input_t[...] = input_ref[...].T
        grad_t[...] = grad_ref[...].T

    fc1, fc2 = fc1_ref[0], fc2_ref[0]
    act, slope = gelu_parts(nn(input_ref[...], fc1))
    act = act.astype(BFLOAT)
    pre_grad = (nn(grad_ref[...], fc2) * slope).astype(BFLOAT)
    branch, in_grad = nt(act, fc2), nt(pre_grad, fc1)

    @pl.when(step == 0)
    def _():
        branch_ref[...] = branch
        in_grad_ref[...] = in_grad

    @pl.when(step > 0)
    def _():
        branch_ref[...] += branch
        in_grad_ref[...] += in_grad

    far, size = part_ref.shape[2], part_ref.shape[4]
    for kind, product in enumerate((nn(input_t[...], pre_grad), nn(grad_t[...], act))):
        product = product.astype(BFLOAT)
        for place in range(4 * far):
            part_ref[0, place % 4, place // 4, kind] = product[place * size : (place + 1) * size]

    @pl.when(step == last)
    def _():
        def some(rows, carry):
            gate_sum, shift_sum, scale_sum = carry
            joined, branch_here = joined_ref[rows, :], branch_ref[rows, :]
            out_grad, in_grad_here = out_grad_ref[rows, :].astype(FLOAT), in_grad_ref[rows, :]
            out_ref[rows, :] = (joined + gate * branch_here).astype(BFLOAT)
            norm, rate = normed(joined)
            res_grad = out_grad + normed_back(in_grad_here * scale, norm, rate)
            res_grad_ref[rows, :] = res_grad
            cross_out_grad_ref[rows, :] = res_grad.astype(BFLOAT)
            return (
                gate_sum + down(out_grad * branch_here),
                shift_sum + down(in_grad_here),
                scale_sum + down(in_grad_here * norm),
            )

        gate_sum, shift_sum, scale_sum = over_rows(frames, some, no_sums(3))
        sums_ref[:, :D] = shift_sum
        sums_ref[:, D : 2 * D] = scale_sum
        sums_ref[:, 2 * D :] = gate_sum
        attn_grad_ref[...] = nt(cross_out_grad_ref[...], project_ref[...]).astype(BFLOAT)


def between_back_kernel(
    query_grad_ref,
    query_weight_ref,
    after_ref,
    res_grad_ref,
    branch_ref,
    modulation_ref,
    project_ref,
    self_res_ref,
    out_grad_ref,
    attn_grad_ref,
    sums_ref,
    in_grad_ref,
):
    in_grad_ref[...] = nt(query_grad_ref[...], query_weight_ref[...])
    gate = block_of(modulation_ref, GATE_SELF)

    def some(rows, carry):
        norm, rate = normed(after_ref[rows, :])
        res_grad = res_grad_ref[rows, :] + normed_back(in_grad_ref[rows, :], norm, rate)
        self_res_ref[rows, :] = res_grad
        out_grad_ref[rows, :] = (gate * res_grad).astype(BFLOAT)
        return (carry[0] + down(res_grad * branch_ref[rows, :]),)

    (sums_ref[...],) = over_rows(after_ref.shape[0], some, no_sums(1))
    attn_grad_ref[...] = nt(out_grad_ref[...], project_ref[...]).astype(BFLOAT)


def first_back_kernel(
    query_grad_ref,
    pair_grad_ref,
    query_weight_ref,
    pair_weight_ref,
    in_ref,
    modulation_ref,
    self_res_ref,
    out_ref,
    sums_ref,
    in_grad_ref,
):
    in_grad_ref[...] = nt(query_grad_ref[...], query_weight_ref[...]) + nt(
        pair_grad_ref[...], pair_weight_ref[...]
    )
    scale = 1.0 + block_of(modulation_ref, SCALE_SELF)

    def some(rows, carry):
        norm, rate = normed(in_ref[rows, :].astype(FLOAT))
        grad = in_grad_ref[rows, :]
        res_grad = self_res_ref[rows, :] + normed_back(grad * scale, norm, rate)
        out_ref[rows, :] = res_grad.astype(BFLOAT)
        return carry[0] + down(grad), carry[1] + down(grad * norm)

    shift_sum, scale_sum = over_rows(in_ref.shape[0], some, no_sums(2))
    sums_ref[:, :D] = shift_sum
    sums_ref[:, D:] = scale_sum


def left_half(weights):
    return weights, pl.BlockSpec((D, D), lambda step: (0, 0))


def right_half(weights):
    return weights, pl.BlockSpec((D, D), lambda step: (0, 1))


def frame_call(kernel, results, *operands, scratch=()):
    specs, arrays = [], []
    for operand in operands:
        if isinstance(operand, tuple):
            arrays.append(operand[0])
            specs.append(operand[1])
        else:
            arrays.append(operand)
            specs.append(whole_block(operand.shape))
    return pl.pallas_call(
        kernel,
        grid=(1,),
        in_specs=specs,
        out_specs=[whole_block(shape) for shape, _ in results],
        out_shape=[jax.ShapeDtypeStruct(shape, kind) for shape, kind in results],
        scratch_shapes=[pltpu.VMEM(shape, kind) for shape, kind in scratch],
        compiler_params=room(48),
        cost_estimate=LIGHT,
    )(*arrays)


MLP_TILE = 768


def mlp_both(cross_attn, project, after_self, modulation, out_grad, weights):
    frames = cross_attn.shape[0]
    far = lax.axis_size("far")
    rows = D // (4 * far)
    tiles = HALF // MLP_TILE
    once = dict(pipeline_mode=pl.Buffered(1))
    whole = pl.BlockSpec((frames, D), lambda half, tile: (0, 0), **once)
    square = (frames, D)
    return pl.pallas_call(
        mlp_kernel,
        grid=(2, tiles),
        in_specs=[
            whole,
            pl.BlockSpec((D, D), lambda half, tile: (0, 1), **once),
            whole,
            pl.BlockSpec((1, 6 * D), lambda half, tile: (0, 0)),
            whole,
            pl.BlockSpec((1, D, MLP_TILE), lambda half, tile: (half, 0, tile)),
            pl.BlockSpec((1, D, MLP_TILE), lambda half, tile: (half, 0, tile + tiles)),
        ],
        out_specs=[whole] * 4
        + [
            pl.BlockSpec((1, 3 * D), lambda half, tile: (0, 0)),
            pl.BlockSpec(
                (1, 4, far, 2, rows, MLP_TILE), lambda half, tile: (half, 0, 0, 0, 0, tile)
            ),
        ],
        out_shape=[
            jax.ShapeDtypeStruct(square, BFLOAT),
            jax.ShapeDtypeStruct(square, FLOAT),
            jax.ShapeDtypeStruct(square, BFLOAT),
            jax.ShapeDtypeStruct(square, BFLOAT),
            jax.ShapeDtypeStruct((1, 3 * D), FLOAT),
            jax.ShapeDtypeStruct((2, 4, far, 2, rows, HALF), BFLOAT),
        ],
        scratch_shapes=[
            pltpu.VMEM(square, BFLOAT),
            pltpu.VMEM(square, BFLOAT),
            pltpu.VMEM((D, frames), BFLOAT),
            pltpu.VMEM((D, frames), BFLOAT),
            pltpu.VMEM(square, FLOAT),
            pltpu.VMEM(square, FLOAT),
            pltpu.VMEM(square, FLOAT),
        ],
        compiler_params=room(48),
        cost_estimate=LIGHT,
    )(cross_attn, project, after_self, modulation, out_grad, weights, weights)


def per_device(
    block_in,
    text,
    timesteps,
    frame_mask,
    text_mask,
    cotangent,
    w_ada,
    w_qkv,
    w_out,
    w_cq,
    w_cout,
    w_ckv,
    w_fc1,
    w_fc2,
    row_state,
    col_state,
):
    clips = lax.axis_size(DP)
    devices = clips * 2
    data_at = lax.axis_index(DP)
    head_at = lax.axis_index("head")
    flat_at = data_at * 2 + head_at
    frames = block_in.shape[1]
    rows = w_qkv.shape[0]

    far = far_links()
    x_first = [far[0], row_link(), core_link()]
    y_first = [row_link(), far[0], core_link()]
    first = [
        gather_chain(
            with_bits(
                jnp.concatenate([w_qkv[:, :D], w_out, w_qkv[:, D:]], axis=1).astype(BFLOAT), "last"
            ),
            "last",
            far[:0:-1],
        )
    ]
    second = [
        gather_chain(
            with_bits(jnp.concatenate([w_cq, w_cout], axis=1).astype(BFLOAT), "last"),
            "last",
            far[:0:-1] + x_first,
        ),
        gather_chain(
            with_bits(w_ckv.astype(BFLOAT).reshape(w_ckv.shape[0], D), "columns"),
            "columns",
            far[:0:-1] + y_first,
        ),
    ]
    mlp_shard = jnp.concatenate([w_fc1.astype(BFLOAT), w_fc2.T.astype(BFLOAT)], axis=1)
    inputs = swap_place(block_in[0])
    joint_mask = jnp.concatenate([frame_mask[0], text_mask[0]])

    def add_step(link):
        return lambda state: state + cross(state, link)

    def project(steps):
        condition = embed_part(steps, flat_at * rows, rows)
        product = jnp.dot(condition, w_ada.astype(BFLOAT), preferred_element_type=FLOAT)
        return condition, product.reshape(clips // 2, 2, 6 * D)

    def keep_step(link):
        def step(state):
            condition, product = state
            bit = bit_of(link)
            dim = 1 if link == row_link() else dp_bits() - link[1].bit_length()
            kept = lax.dynamic_slice_in_dim(product, bit, 1, axis=dim)
            sent = lax.dynamic_slice_in_dim(product, 1 - bit, 1, axis=dim)
            product = kept + cross(sent, link)
            if link == row_link():
                product = product.reshape((2,) * (dp_bits() - 1) + (6 * D,))
            return condition, product

        return step

    def last_step(state):
        condition, product = state
        return condition, (product + cross(product, core_link())).reshape(1, 6 * D)

    steps = lax.dynamic_update_slice(jnp.zeros((clips,), jnp.int32), timesteps, (data_at,))
    timing = Chain(
        steps,
        [add_step(link) for link in [core_link()] + far_links()[1:] + far_links()[:1]]
        + [lambda steps: keep_step(row_link())(project(steps))]
        + [keep_step(link) for link in far_links()[1:] + far_links()[:1]]
        + [last_step],
    )
    far_count = len(far) - 1
    slots = far_count + 3
    for slot in range(slots):
        if slot < far_count:
            timing.advance(1 + (slot == 0) + (slot == far_count - 1))
        else:
            timing.advance((1, far_count, 2)[slot - far_count])
        if slot == far_count:
            joint = first[0].state
            first = [
                gather_chain(joint[..., : 2 * D], "last", x_first),
                gather_chain(joint[..., 2 * D :], "last", y_first),
            ]
        for chain in first:
            chain.advance()
        if slot >= 2:
            for chain in second:
                chain.advance()
        if slot == far_count - 1:
            inputs, mlp_shard, joint_mask, text = tie(
                [timing] + first + second, inputs, mlp_shard, joint_mask, text
            )
            mlp_all = lax.all_gather(mlp_shard, HEAD + DP, axis=0, tiled=True)
            masks = from_clip_core(joint_mask)
            clip_text = from_clip_core(text[0])
        elif slot < slots - 1:
            tie([timing] + first + (second if slot == far_count else []))
        else:
            wide = tie([timing] + first, w_ada, w_qkv, w_out, w_cq, w_cout, w_fc1, w_fc2)
            masters = [
                jnp.concatenate(wide[:5], axis=1),
                w_ckv.reshape(w_ckv.shape[0], D),
                jnp.concatenate([wide[5], wide[6].T], axis=1),
            ]
            (weight_squares,) = whole_call(weight_kernel, [(1, LINE)], *masters)
    condition, modulation = timing.finish()
    query_out, w_key_value = [chain.finish().reshape(D, 2 * D) for chain in first]
    square = (frames, D)
    core_at = data_at % 2
    own_allowed = lax.dynamic_slice_in_dim(masks, core_at * frames, frames)
    other_allowed = lax.dynamic_slice_in_dim(masks, (1 - core_at) * frames, frames)
    own_bias, other_bias = bias_of(own_allowed), bias_of(other_allowed)
    text_bias = bias_of(masks[2 * frames :])

    self_input, query, key_value = frame_call(
        first_kernel,
        [(square, BFLOAT), (square, BFLOAT), ((frames, 2 * D), BFLOAT)],
        inputs,
        modulation,
        left_half(query_out),
        w_key_value,
    )
    other_key_value = cross(key_value, core_link())
    query, other_key_value = tie(second, query, other_key_value)
    for chain in second:
        chain.advance()

    self_keys = [(key_value, own_bias), (other_key_value, other_bias)]
    self_attn, self_logs = attend(query, self_keys, plain_places)
    self_attn, cotangent = tie(second, self_attn, cotangent)
    swapped_cotangent = swap_only(cotangent[0])
    cross_pair, w_text = [chain.finish() for chain in second]
    cross_pair, w_text = cross_pair.reshape(D, 2 * D), w_text.reshape(DT, 2 * D)
    self_branch, after_self, cross_input, cross_query = frame_call(
        between_kernel,
        [(square, FLOAT), (square, FLOAT), (square, BFLOAT), (square, BFLOAT)],
        self_attn,
        right_half(query_out),
        inputs,
        modulation,
        left_half(cross_pair),
    )

    text_pair = nn(clip_text, w_text).astype(BFLOAT)
    text_keys = [(text_pair, text_bias)]
    cross_attn, cross_logs = attend(cross_query, text_keys, half_places)

    cross_attn, own, cotangent = tie([], cross_attn, on_own_chip(), cotangent)
    out_grad = jnp.where(own, cotangent[0], swapped_cotangent)
    block_out, cross_res_grad, cross_out_grad, cross_attn_grad, mlp_sums, mlp_part = mlp_both(
        cross_attn,
        cross_pair,
        after_self,
        modulation,
        out_grad,
        mlp_all.reshape(2, D, 2 * HALF),
    )
    mlp_part = lax.psum_scatter(
        mlp_part.reshape((8,) + mlp_part.shape[2:]),
        HEAD + ("near", "core"),
        scatter_dimension=0,
        tiled=False,
    )

    cross_query_grad, text_pair_grad = attend_back(
        cross_query, cross_attn, cross_attn_grad, cross_logs, text_keys, half_places
    )
    self_res_grad, self_out_grad, self_attn_grad, gate_self_grad = frame_call(
        between_back_kernel,
        [(square, FLOAT), (square, BFLOAT), (square, BFLOAT), ((1, D), FLOAT)],
        cross_query_grad,
        left_half(cross_pair),
        after_self,
        cross_res_grad,
        self_branch,
        modulation,
        right_half(query_out),
        scratch=[(square, FLOAT)],
    )

    query_grad, own_pair_grad, other_pair_grad = attend_back(
        query, self_attn, self_attn_grad, self_logs, self_keys, plain_places
    )
    pair_grad = (
        own_pair_grad.astype(FLOAT) + cross(other_pair_grad, core_link()).astype(FLOAT)
    ).astype(BFLOAT)
    last_chains = [
        scatter_chain(
            outer((self_input, query_grad), (self_attn, self_out_grad)), "last", False
        ),
        scatter_chain(outer((self_input, pair_grad)), "last", True),
    ]
    cross_query_grad, text_pair_grad = tie(last_chains, cross_query_grad, text_pair_grad)
    for chain in last_chains:
        chain.advance()
    cross_chains = [
        scatter_chain(
            outer((cross_input, cross_query_grad), (cross_attn, cross_out_grad)), "last", False
        ),
        scatter_chain(outer((clip_text, text_pair_grad)), "columns", True),
    ]
    query_grad, pair_grad = tie(cross_chains + last_chains, query_grad, pair_grad)
    for chain in last_chains + cross_chains:
        chain.advance()
    input_grad, self_sums = frame_call(
        first_back_kernel,
        [(square, BFLOAT), ((1, 2 * D), FLOAT)],
        query_grad,
        pair_grad,
        left_half(query_out),
        w_key_value,
        inputs,
        modulation,
        self_res_grad,
        scratch=[(square, FLOAT)],
    )
    modulation_grad = jnp.concatenate([self_sums, gate_self_grad, mlp_sums], axis=-1)

    def join_step(link):
        def step(state):
            other = cross(state, link)
            upper = bit_of(link) == 1
            dim = dp_bits() - 1 if link[0] == HEAD else dp_bits() - link[1].bit_length()
            low, high = jnp.where(upper, other, state), jnp.where(upper, state, other)
            return jnp.concatenate([low, high], axis=dim)

        return step

    far = far_links()
    shape = (1,) * dp_bits() + (6 * D,)
    joining = Chain(
        modulation_grad,
        [lambda state: (state + cross(state, core_link())).reshape(shape)]
        + [join_step(link) for link in far[:0:-1] + [far[0], row_link()]],
    )

    chains = last_chains + cross_chains
    joining.advance()
    block_out, input_grad, mlp_part = tie([joining] + chains, block_out, input_grad, mlp_part)
    mlp_raw = lax.psum_scatter(mlp_part, "far", scatter_dimension=0, tiled=False).astype(FLOAT)
    for chain in chains:
        chain.advance()
    joining.advance(len(far) - 1)
    block_out, input_grad = tie([joining] + chains, block_out, input_grad)
    for chain in chains:
        chain.advance()
    joining.advance(2)
    block_out, input_grad, mlp_raw = tie([joining] + chains, block_out, input_grad, mlp_raw)
    for chain in chains:
        chain.advance()
    block_out, input_grad = tie(chains, block_out, input_grad)
    other_out, other_grad = swap_only(block_out), swap_only(input_grad)
    for chain in cross_chains:
        chain.advance()
    tie(cross_chains)
    modulation_grad = joining.finish()
    ada_raw = jnp.einsum(
        "cr,cx->rx",
        condition.astype(FLOAT),
        modulation_grad.reshape(clips, 6 * D),
        precision=PRECISE,
    )

    cross_raw, ckv_raw = [chain.finish() for chain in cross_chains]
    query_out_raw, pair_raw = [chain.finish() for chain in last_chains]

    place = jnp.stack([data_at, head_at]).astype(jnp.int32)
    raw_grads = [ada_raw, query_out_raw, pair_raw, cross_raw, ckv_raw, mlp_raw]
    (statistics,) = whole_call(
        statistics_kernel, [(STAT_LINES, LINE)], place, weight_squares, *raw_grads, places=1
    )
    sums = sum_all(statistics)
    shapes = [(rows, columns) for columns in COL_SIZES[:5]]
    shapes += [masters[1].shape] + [(rows * 2, HALF)] * 2
    line = (1, LINE)
    row_new, col_new, norm, update_squares, *rest = whole_call(
        update_kernel,
        [(ROW_LINES, LINE), (COL_LINES, LINE), line, line]
        + shapes
        + [master.shape for master in masters],
        place,
        sums,
        row_state.reshape(ROW_LINES, LINE),
        col_state.reshape(COL_LINES, LINE),
        *raw_grads,
        places=1,
    )
    clipped, updates = list(rest[:8]), rest[8:]
    clipped[5] = clipped[5].reshape(w_ckv.shape)
    clipped[7] = clipped[7].T
    late, _ = tie([], on_own_chip(), update_squares)
    block_out = jnp.where(late, block_out, other_out)
    input_grad = jnp.where(late, input_grad, other_grad)
    update_squares, block_out, input_grad, *clipped = tie(
        [], sum_all(update_squares), block_out, input_grad, *clipped
    )
    updated = list(
        whole_call(
            apply_kernel,
            shapes,
            update_squares,
            sums[STAT_LINES - 2 : STAT_LINES - 1],
            *masters,
            *updates,
        )
    )
    updated[5] = updated[5].reshape(w_ckv.shape)
    updated[7] = updated[7].T
    return (
        block_out[None],
        input_grad[None],
        norm[0, 0],
        row_new.reshape(-1),
        col_new.reshape(-1),
        *clipped,
        *updated,
    )


def solution(mesh):
    devices = mesh.devices
    refined = jax.sharding.Mesh(devices.reshape(devices.shape[0] // 4, 2, 2, 2), ALL)
    return jax.shard_map(
        per_device,
        mesh=refined,
        in_specs=(
            P(DP, "head", None),
            P(DP, None, None),
            P(DP),
            P(DP, None),
            P(DP, None),
            P(DP, "head", None),
            P(ALL, None),
            P(ALL, None),
            P(ALL, None),
            P(ALL, None),
            P(ALL, None),
            P(DP, None, "head"),
            P(DP, "head"),
            P("head", DP),
            P(),
            P(),
        ),
        out_specs=(
            P(DP, "head", None),
            P(DP, "head", None),
            P(),
            P(),
            P(),
            P(ALL, None),
            P(ALL, None),
            P(ALL, None),
            P(ALL, None),
            P(ALL, None),
            P(DP, None, "head"),
            P(DP, "head"),
            P("head", DP),
            P(ALL, None),
            P(ALL, None),
            P(ALL, None),
            P(ALL, None),
            P(ALL, None),
            P(DP, None, "head"),
            P(DP, "head"),
            P("head", DP),
        ),
        check_vma=False,
    )
```

```python
import functools

import jax
import jax.numpy as jnp
from jax import lax
from jax.experimental import pallas as pl
from jax.experimental.pallas import tpu as pltpu
from jax.sharding import PartitionSpec as P

D = 768
FF = 3072
DT = 1024
HD = 64
HALF = FF // 2

PRECISE = lax.Precision.HIGHEST
FLOAT = jnp.float32
BFLOAT = jnp.bfloat16
EPS_NORM = 1e-06
EPS_FACTOR = 1e-30
CLIP_NORM = 1.0
CLIP_UPDATE = 0.25
DECAY_RATE = 0.5
RELATIVE_RATE = 4.0
SCALE_FLOOR = 0.001
SCORE_SCALE = 0.125
MASKED_SCORE = -1e30
DP = ("far", "near", "core")
ALL = DP + ("head",)
HEAD = ("head",)
PAIR = 2 * HD
PAIRS = D // PAIR


def embed_part(steps, first, count):
    halfway = D // 2
    place = first + jnp.arange(count)
    freqs = jnp.exp(-jnp.log(10000.0) * (place % halfway).astype(FLOAT) / halfway)
    angles = steps.astype(FLOAT)[:, None] * freqs
    waves = jnp.where(place < halfway, jnp.cos(angles), jnp.sin(angles))
    return jax.nn.silu(waves).astype(BFLOAT)


def core_link():
    return (DP, 1)


def row_link():
    return (HEAD, 1)


def far_links():
    masks, mask = [], 2
    while mask < lax.axis_size(DP):
        masks.append(mask)
        mask = mask * 2
    return [(DP, mask) for mask in masks]


def dp_bits():
    return lax.axis_size(DP).bit_length() - 1


def bit_of(link):
    return (lax.axis_index(link[0]) // link[1]) % 2


def cross(values, link):
    pairs = [(place, place ^ link[1]) for place in range(lax.axis_size(link[0]))]
    return lax.ppermute(values, link[0], pairs)


def dim_of(link, head):
    if link[0] == HEAD:
        return {"first": 0, "last": dp_bits(), "columns": dp_bits() + 1}[head]
    return (1 if head == "first" else 0) + dp_bits() - link[1].bit_length()


def leading(head):
    return dp_bits() + (0 if head == "columns" else 1)


def grow(block, link, head):
    other = cross(block, link)
    upper = bit_of(link) == 1
    low = jnp.where(upper, other, block)
    high = jnp.where(upper, block, other)
    return jnp.concatenate([low, high], axis=dim_of(link, head))


def shrink(block, link, head, kind=BFLOAT):
    dim, bit = dim_of(link, head), bit_of(link)
    half = block.shape[dim] // 2
    kept = lax.dynamic_slice_in_dim(block, bit * half, half, axis=dim)
    sent = lax.dynamic_slice_in_dim(block, (1 - bit) * half, half, axis=dim)
    return (kept.astype(FLOAT) + cross(sent.astype(BFLOAT), link).astype(FLOAT)).astype(kind)


class Chain:
    def __init__(self, state, steps):
        self.state, self.steps = state, list(steps)

    def advance(self, count=1):
        for _ in range(min(count, len(self.steps))):
            self.state = self.steps.pop(0)(self.state)
        return self

    def finish(self):
        return self.advance(len(self.steps)).state


def tie(chains, *values):
    states, values = lax.optimization_barrier(([chain.state for chain in chains], values))
    for chain, state in zip(chains, states):
        chain.state = state
    return values


def gather_chain(block, head, links):
    return Chain(block, [lambda state, link=link: grow(state, link, head) for link in links])


def with_bits(shard, head):
    return shard.reshape((1,) * leading(head) + shard.shape)


def scatter_chain(matrix, head, row_early):
    bits = leading(head)
    rows, columns = matrix.shape[-2:]
    split = dp_bits() if head == "first" else bits
    block = matrix.reshape((2,) * bits + (rows // 2**split, columns))
    far = far_links()
    plane = [far[0], row_link()] if row_early else [row_link(), far[0]]
    order = [core_link()] + plane + far[1:]
    kinds = [BFLOAT] * (len(order) - 1) + [FLOAT]
    steps = [
        lambda state, link=link, kind=kind: shrink(state, link, head, kind)
        for link, kind in zip(order, kinds)
    ]
    return Chain(block, steps + [lambda state: state.reshape(state.shape[bits:])])


def sum_all(values):
    for link in [core_link()] + far_links() + [row_link()]:
        values = values + cross(values, link)
    return values


def on_own_chip():
    return bit_of(core_link()) == bit_of(row_link())


def swap_only(values):
    pairs = []
    for place in range(lax.axis_size(DP)):
        for head in range(2):
            if place & 1 != head:
                pairs.append((place * 2 + head, ((place & ~1) | head) * 2 + (place & 1)))
    return lax.ppermute(values, ALL, pairs)


def swap_place(values):
    return jnp.where(on_own_chip(), values, swap_only(values))


def from_clip_core(values):
    pairs = []
    for place in range(0, lax.axis_size(DP), 2):
        for head in range(2):
            pairs.append(((place + head) * 2 + head, (place + 1 - head) * 2 + head))
    return jnp.where(on_own_chip(), values, lax.ppermute(values, ALL, pairs))


def nt(left, right):
    return lax.dot_general(left, right, (((1,), (1,)), ((), ())), preferred_element_type=FLOAT)


def nn(left, right):
    return lax.dot_general(left, right, (((1,), (0,)), ((), ())), preferred_element_type=FLOAT)


def lanes_of(length):
    return lax.broadcasted_iota(jnp.int32, (length, PAIR), 1)


def with_spare(pair, head, spare):
    lane = lanes_of(pair.shape[0])
    rest = jnp.where(lane == HD * (1 - head), spare, jnp.zeros_like(pair))
    return jnp.where(lane // HD == head, pair, rest)


def attend_kernel(blocks, *refs):
    query_ref, out_ref, log_ref = refs[0], refs[1 + 3 * blocks], refs[2 + 3 * blocks]
    ins = refs[1 : 1 + 3 * blocks]
    one = jnp.ones((1, 1), BFLOAT)
    for place in range(log_ref.shape[0]):
        columns = pl.ds(place * PAIR, PAIR)
        queries = query_ref[:, columns] * jnp.asarray(SCORE_SCALE, BFLOAT)
        values_t = [ref[:, columns].T for ref in ins[1::3]]
        results, logs = [], []
        for head in range(2):
            query = with_spare(queries, head, one)
            scores = [
                nt(with_spare(key_ref[:, columns], head, bias_ref[...]), query)
                for key_ref, bias_ref in zip(ins[0::3], ins[2::3])
            ]
            peak = functools.reduce(
                jnp.maximum, [jnp.max(score, axis=0, keepdims=True) for score in scores]
            )
            total = None
            for score, value_t in zip(scores, values_t):
                probs = jnp.exp(score - peak).astype(BFLOAT)
                row = lax.broadcasted_iota(jnp.int32, value_t.shape, 0)
                term = nn(jnp.where(row // HD == head, value_t, one), probs)
                total = term if total is None else total + term
            weight = total[HD * (1 - head) : HD * (1 - head) + 1, :]
            results.append(total[HD * head : HD * (head + 1), :] / weight)
            logs.append(peak + jnp.log(weight))
        out_ref[:, columns] = jnp.concatenate(results, axis=0).T.astype(BFLOAT)
        log_ref[place] = jnp.concatenate(logs, axis=0)


def back_kernel(blocks, places, *refs):
    query_ref, out_ref, grad_ref, log_ref = refs[:4]
    ins = refs[4 : 4 + 3 * blocks]
    query_grad_ref, pair_grad_refs = refs[4 + 3 * blocks], refs[5 + 3 * blocks :]
    zero = jnp.zeros((1, 1), BFLOAT)
    one = jnp.ones((1, 1), BFLOAT)
    chooser = (
        lax.broadcasted_iota(jnp.int32, (8, PAIR), 1) // HD
        == lax.broadcasted_iota(jnp.int32, (8, PAIR), 0)
    ).astype(FLOAT)
    count = log_ref.shape[0]
    for place in range(count):
        columns = pl.ds(place * PAIR, PAIR)
        queries = query_ref[:, columns] * jnp.asarray(SCORE_SCALE, BFLOAT)
        out_grad = grad_ref[:, columns]
        product = out_ref[:, columns].astype(FLOAT) * out_grad.astype(FLOAT)
        inner = lax.dot_general(
            chooser,
            product,
            (((1,), (1,)), ((), ())),
            precision=PRECISE,
            preferred_element_type=FLOAT,
        )
        query_parts = [None, None]
        for block in range(blocks):
            keys, values = ins[3 * block][:, columns], ins[3 * block + 1][:, columns]
            bias, keys_t = ins[3 * block + 2][...], keys.T
            key_grad, value_grad = None, None
            for head in range(2):
                grad_here = with_spare(out_grad, head, zero)
                score = nt(with_spare(keys, head, bias), with_spare(queries, head, one))
                probs = jnp.exp(score - log_ref[place, head : head + 1, :])
                prob_grad = nt(values, grad_here)
                score_grad = (probs * (prob_grad - inner[head : head + 1, :])).astype(BFLOAT)
                value_term = nn(probs.astype(BFLOAT), grad_here)
                key_term = nn(score_grad, with_spare(queries, head, zero))
                query_term = nn(keys_t[HD * head : HD * (head + 1), :], score_grad)
                value_grad = value_term if value_grad is None else value_grad + value_term
                key_grad = key_term if key_grad is None else key_grad + key_term
                query_parts[head] = (
                    query_term if query_parts[head] is None else query_parts[head] + query_term
                )
            key_at, value_at = places(pl.program_id(0) * count + place)
            key_at = pl.multiple_of(key_at * PAIR, PAIR)
            value_at = pl.multiple_of(value_at * PAIR, PAIR)
            pair_grad_refs[block][:, pl.ds(key_at, PAIR)] = key_grad.astype(BFLOAT)
            pair_grad_refs[block][:, pl.ds(value_at, PAIR)] = value_grad.astype(BFLOAT)
        joined = jnp.concatenate(query_parts, axis=0) * SCORE_SCALE
        query_grad_ref[:, columns] = joined.T.astype(BFLOAT)


def column_block(length, count):
    return pl.BlockSpec((length, PAIR * count), lambda step: (0, step))


def plain_places(pair):
    return pair, pair + PAIRS


def half_places(pair):
    half, part = pair // (PAIRS // 2), pair % (PAIRS // 2)
    return half * PAIRS + part, half * PAIRS + PAIRS // 2 + part


def whole_block(shape):
    return pl.BlockSpec(shape, lambda pair: (0,) * len(shape))


def log_block(frames, count):
    return pl.BlockSpec((count, 2, frames), lambda step: (step, 0, 0))


def key_specs(key_values, places, count):
    specs, operands = [], []
    for joint, bias in key_values:
        length = joint.shape[0]
        specs += [
            pl.BlockSpec(
                (length, PAIR * count), lambda step: (0, places(step * count)[0] // count)
            ),
            pl.BlockSpec(
                (length, PAIR * count), lambda step: (0, places(step * count)[1] // count)
            ),
            whole_block((length, PAIR)),
        ]
        operands += [joint, joint, bias]
    return specs, operands


def room(mebibytes):
    return pltpu.CompilerParams(vmem_limit_bytes=mebibytes * 1024 * 1024)


LIGHT = pl.CostEstimate(flops=1000, bytes_accessed=1000, transcendentals=0)


def attend(queries, key_values, places, count=1):
    frames, blocks = queries.shape[0], len(key_values)
    specs, operands = key_specs(key_values, places, count)
    return pl.pallas_call(
        functools.partial(attend_kernel, blocks),
        grid=(PAIRS // count,),
        in_specs=[column_block(frames, count)] + specs,
        out_specs=[column_block(frames, count), log_block(frames, count)],
        out_shape=[
            jax.ShapeDtypeStruct((frames, D), BFLOAT),
            jax.ShapeDtypeStruct((PAIRS, 2, frames), FLOAT),
        ],
        compiler_params=room(48),
        cost_estimate=LIGHT,
    )(queries, *operands)


def attend_back(queries, out, out_grad, logs, key_values, places, count=1):
    frames, blocks = queries.shape[0], len(key_values)
    specs, operands = key_specs(key_values, places, count)
    return pl.pallas_call(
        functools.partial(back_kernel, blocks, places),
        grid=(PAIRS // count,),
        in_specs=[column_block(frames, count)] * 3 + [log_block(frames, count)] + specs,
        out_specs=[column_block(frames, count)] + [whole_block(joint.shape) for joint, _ in key_values],
        out_shape=[jax.ShapeDtypeStruct((frames, D), BFLOAT)]
        + [jax.ShapeDtypeStruct(joint.shape, BFLOAT) for joint, _ in key_values],
        compiler_params=room(48),
        cost_estimate=LIGHT,
    )(queries, out, out_grad, logs, *operands)


def outer_kernel(*refs):
    out_ref, count = refs[-1], len(refs) // 2
    at = 0
    for place in range(count):
        left, right = refs[2 * place], refs[2 * place + 1]
        width = right.shape[1]
        product = lax.dot_general(
            left[...], right[...], (((0,), (0,)), ((), ())), preferred_element_type=FLOAT
        )
        out_ref[:, at : at + width] = product.astype(BFLOAT)
        at += width


def outer(*pairs):
    operands = [matrix for pair in pairs for matrix in pair]
    shape = (pairs[0][0].shape[1], sum(right.shape[1] for _, right in pairs))
    return pl.pallas_call(
        outer_kernel,
        out_shape=jax.ShapeDtypeStruct(shape, BFLOAT),
        compiler_params=room(48),
        cost_estimate=LIGHT,
    )(*operands)


def bias_of(allowed):
    column = jnp.where(allowed > 0, 0.0, MASKED_SCORE).astype(BFLOAT)
    return jnp.broadcast_to(column[:, None], (allowed.shape[0], PAIR))


LINE = 128
ROW_SIZES = [D, D, D, D, D, DT, D, FF]
COL_SIZES = [6 * D, 3 * D, D, D, D, 2 * D, FF, D]
ROW_LINES = sum(ROW_SIZES) // LINE
COL_LINES = sum(COL_SIZES) // LINE
STAT_LINES = ROW_LINES + COL_LINES + 2


def starts_of(sizes, first):
    starts = []
    for size in sizes:
        starts.append(first)
        first += size // LINE
    return starts


ROW_STARTS = starts_of(ROW_SIZES, 0)
COL_STARTS = starts_of(COL_SIZES, ROW_LINES)


def lines_at(line, shape):
    return lax.broadcasted_iota(jnp.int32, shape, 1) + line * LINE


def down_lines(column, offset, lines):
    shape = (column.shape[0], LINE)
    wanted = lax.broadcasted_iota(jnp.int32, shape, 0) + offset
    return [
        jnp.sum(jnp.where(lines_at(line, shape) == wanted, column, 0.0), axis=0, keepdims=True)
        for line in range(lines)
    ]


def from_lines(lines, offset, count):
    shape = (count, LINE)
    wanted = lax.broadcasted_iota(jnp.int32, shape, 0) + offset
    total = jnp.zeros(shape, FLOAT)
    for line in range(lines.shape[0]):
        here = jnp.where(lines_at(line, shape) == wanted, lines[line : line + 1, :], 0.0)
        total = total + here
    return jnp.sum(total, axis=1, keepdims=True)


def pieces_of(grad_refs):
    ada, query_out, key_value, cross_pair, text_pair, mlp = grad_refs
    return [
        [(ada, 0, 6 * D)],
        [(query_out, 0, D), (key_value, 0, 2 * D)],
        [(query_out, D, D)],
        [(cross_pair, 0, D)],
        [(cross_pair, D, D)],
        [(text_pair, 0, D)],
        [(mlp.at[0], 0, HALF)],
        [(mlp.at[1], 0, HALF)],
    ]


def joined_pieces(refs):
    square, text_pair, mlp = refs
    parts, at = [], 0
    for place in range(5):
        parts.append((square, at, COL_SIZES[place]))
        at += COL_SIZES[place]
    return parts + [(text_pair, 0, D), (mlp, 0, HALF), (mlp, HALF, HALF)]


def statistics_kernel(place_ref, weight_ref, *refs):
    grad_refs, out_ref = refs[:6], refs[6]
    data_at, head_at = place_ref[0], place_ref[1]
    flat_at = data_at * 2 + head_at
    out_ref[STAT_LINES - 2 : STAT_LINES - 1, :] = weight_ref[...]
    out_ref[STAT_LINES - 1 : STAT_LINES, :] = jnp.zeros((1, LINE), FLOAT)
    for place, parts in enumerate(pieces_of(grad_refs)):
        across, down = 0.0, []
        for ref, first, columns in parts:
            rows = ref.shape[0]
            wide = jnp.zeros((rows, LINE), FLOAT)
            for line in range(columns // LINE):
                piece = ref[:, first + line * LINE : first + (line + 1) * LINE]
                square = piece * piece
                wide = wide + square
                down.append(jnp.sum(square, axis=0, keepdims=True))
            across = across + jnp.sum(wide, axis=1, keepdims=True)
        offset = (flat_at if place < 5 else data_at) * rows
        row_start, col_start = ROW_STARTS[place], COL_STARTS[place]
        if place == 7:
            row_start, col_start = col_start, row_start
        row_lines = (COL_SIZES if place == 7 else ROW_SIZES)[place] // LINE
        for line, entry in enumerate(down_lines(across, offset, row_lines)):
            out_ref[row_start + line : row_start + line + 1, :] = entry
        groups = {5: 2}.get(place, 1)
        size = len(down) // groups
        for line, entry in enumerate(down):
            if place < 5:
                out_ref[col_start + line : col_start + line + 1, :] = entry
            else:
                for half in range(2):
                    at = col_start + (line // size * 2 + half) * size + line % size
                    out_ref[at : at + 1, :] = jnp.where(head_at == half, entry, 0.0)


def lane_of(lines, lane):
    shape = (1, LINE)
    here = lax.broadcasted_iota(jnp.int32, shape, 1) == lane
    return jnp.sum(jnp.where(here, lines, 0.0), axis=1, keepdims=True)


def update_kernel(place_ref, sums_ref, row_ref, col_ref, *refs):
    grad_refs, outs = refs[:6], refs[6:]
    row_out, col_out, norm_out, total_out = outs[:4]
    clipped_refs, update_refs = outs[4:12], joined_pieces(outs[12:15])
    data_at, head_at = place_ref[0], place_ref[1]
    flat_at = data_at * 2 + head_at
    row_sums = sums_ref[0:ROW_LINES, :]
    square_total = jnp.sum(jnp.sum(row_sums, axis=0, keepdims=True), axis=1, keepdims=True)
    norm = jnp.sqrt(square_total)
    factor = 1.0 / jnp.maximum(1.0, norm / CLIP_NORM)
    norm_out[...] = jnp.broadcast_to(norm, (1, LINE))
    square_factor = factor * factor
    lane = lax.broadcasted_iota(jnp.int32, (1, LINE), 1)
    totals = jnp.zeros((1, LINE), FLOAT)
    for place, parts in enumerate(pieces_of(grad_refs)):
        rows_len, cols_len = ROW_SIZES[place], COL_SIZES[place]
        row_from, row_to = ROW_STARTS[place], ROW_STARTS[place] + rows_len // LINE
        col_from, col_to = COL_STARTS[place], COL_STARTS[place] + cols_len // LINE
        new_row = DECAY_RATE * row_ref[row_from:row_to, :] + (1.0 - DECAY_RATE) * (
            square_factor * sums_ref[row_from:row_to, :] / float(cols_len) + EPS_FACTOR
        )
        col_from, col_to = col_from - ROW_LINES, col_to - ROW_LINES
        new_col = DECAY_RATE * col_ref[col_from:col_to, :] + (1.0 - DECAY_RATE) * (
            square_factor
            * sums_ref[ROW_LINES + col_from : ROW_LINES + col_to, :]
            / float(rows_len)
            + EPS_FACTOR
        )
        row_out[row_from:row_to, :] = new_row
        col_out[col_from:col_to, :] = new_col
        row_mean = (
            jnp.sum(jnp.sum(new_row, axis=0, keepdims=True), axis=1, keepdims=True) / rows_len
        )
        rows = parts[0][0].shape[0]
        offset = (flat_at if place < 5 else data_at) * rows
        if place == 7:
            down = lax.rsqrt(from_lines(new_col, offset, rows))
            across = jnp.where(head_at == 0, new_row[:12], new_row[12:])
            across = lax.rsqrt(across / row_mean)
        else:
            down = lax.rsqrt(from_lines(new_row, offset, rows) / row_mean)
            if place == 5:
                keys = jnp.where(head_at == 0, new_col[0:3], new_col[3:6])
                values = jnp.where(head_at == 0, new_col[6:9], new_col[9:12])
                across = lax.rsqrt(jnp.concatenate([keys, values], axis=0))
            elif place == 6:
                across = lax.rsqrt(jnp.where(head_at == 0, new_col[:12], new_col[12:]))
            else:
                across = lax.rsqrt(new_col)
        square = jnp.zeros((rows, LINE), FLOAT)
        line_at = 0
        for ref, first, columns in parts:
            for line in range(columns // LINE):
                piece = ref[:, first + line * LINE : first + (line + 1) * LINE] * factor
                update = piece * (down * across[line_at : line_at + 1, :])
                clipped_refs[place][:, line_at * LINE : (line_at + 1) * LINE] = piece
                update_ref, update_at, _ = update_refs[place]
                update_at += line_at * LINE
                update_ref[:, update_at : update_at + LINE] = update
                square = square + update * update
                line_at += 1
        total = jnp.sum(jnp.sum(square, axis=0, keepdims=True), axis=1, keepdims=True)
        totals = jnp.where(lane == place, total, totals)
    total_out[...] = totals


def apply_kernel(total_ref, weight_ref, *refs):
    master_refs, update_refs = joined_pieces(refs[:3]), joined_pieces(refs[3:6])
    for place in range(8):
        entries = float(ROW_SIZES[place] * COL_SIZES[place])
        total = lane_of(total_ref[...], place)
        weight = lane_of(weight_ref[...], place)
        limit = jnp.maximum(1.0, jnp.sqrt(total / entries) / CLIP_UPDATE)
        rate = RELATIVE_RATE * jnp.maximum(SCALE_FLOOR, jnp.sqrt(weight / entries))
        scale = rate / limit
        ref, at, columns = master_refs[place]
        update = update_refs[place][0][:, at : at + columns]
        refs[6 + place][...] = ref[:, at : at + columns] - scale * update


def weight_kernel(*refs):
    lane = lax.broadcasted_iota(jnp.int32, (1, LINE), 1)
    totals = jnp.zeros((1, LINE), FLOAT)
    for place in range(8):
        ref, at, columns = joined_pieces(refs[:3])[place]
        matrix = ref[:, at : at + columns]
        total = jnp.sum(jnp.sum(matrix * matrix, axis=0, keepdims=True), axis=1, keepdims=True)
        totals = jnp.where(lane == place, total, totals)
    refs[3][...] = totals


def whole_call(kernel, shapes, *operands, places=0):
    memory = [pl.BlockSpec(memory_space=pltpu.SMEM)] * places
    memory += [pl.BlockSpec(memory_space=pltpu.VMEM)] * (len(operands) - places)
    return pl.pallas_call(
        kernel,
        in_specs=memory,
        out_specs=[pl.BlockSpec(memory_space=pltpu.VMEM)] * len(shapes),
        out_shape=[jax.ShapeDtypeStruct(shape, FLOAT) for shape in shapes],
        compiler_params=room(48),
        cost_estimate=LIGHT,
    )(*operands)


GELU_WIDTH = 0.7978845608028654
GELU_CUBE = 0.044715


def gelu_parts(values):
    square = values * values
    bend = jnp.tanh(values * (GELU_WIDTH + GELU_WIDTH * GELU_CUBE * square))
    half = 0.5 + 0.5 * bend
    slope = GELU_WIDTH + 3.0 * GELU_WIDTH * GELU_CUBE * square
    return values * half, half + (0.5 * values) * (1.0 - bend * bend) * slope


ROWS = 512
SHIFT_SELF, SCALE_SELF, GATE_SELF, SHIFT_MLP, SCALE_MLP, GATE_MLP = range(6)


def block_of(modulation_ref, place):
    return modulation_ref[:, place * D : (place + 1) * D]


def over_rows(frames, body, start=None):
    def step(place, carry):
        return body(pl.ds(pl.multiple_of(place * ROWS, ROWS), ROWS), carry)

    return lax.fori_loop(0, frames // ROWS, step, start)


def normed(values):
    centered = values - jnp.mean(values, axis=-1, keepdims=True)
    rate = lax.rsqrt(jnp.mean(centered * centered, axis=-1, keepdims=True) + EPS_NORM)
    return centered * rate, rate


def normed_back(grad, norm, rate):
    inner = jnp.mean(grad * norm, axis=-1, keepdims=True)
    return rate * (grad - jnp.mean(grad, axis=-1, keepdims=True) - norm * inner)


def down(values):
    return jnp.sum(values, axis=0, keepdims=True)


def no_sums(count):
    return (jnp.zeros((1, D), FLOAT),) * count


def first_kernel(
    in_ref, modulation_ref, query_weight_ref, pair_weight_ref, self_input_ref, query_ref, pair_ref
):
    shift = block_of(modulation_ref, SHIFT_SELF)
    scale = 1.0 + block_of(modulation_ref, SCALE_SELF)

    def some(rows, carry):
        norm, _ = normed(in_ref[rows, :].astype(FLOAT))
        self_input_ref[rows, :] = (norm * scale + shift).astype(BFLOAT)
        return carry

    over_rows(in_ref.shape[0], some)
    pair_ref[...] = nn(self_input_ref[...], pair_weight_ref[...]).astype(BFLOAT)
    query_ref[...] = nn(self_input_ref[...], query_weight_ref[...]).astype(BFLOAT)


def between_kernel(
    attn_ref,
    project_ref,
    in_ref,
    modulation_ref,
    query_weight_ref,
    branch_ref,
    after_ref,
    cross_input_ref,
    query_ref,
):
    branch_ref[...] = nn(attn_ref[...], project_ref[...])
    gate = block_of(modulation_ref, GATE_SELF)

    def some(rows, carry):
        after = in_ref[rows, :].astype(FLOAT) + gate * branch_ref[rows, :]
        after_ref[rows, :] = after
        norm, _ = normed(after)
        cross_input_ref[rows, :] = norm.astype(BFLOAT)
        return carry

    over_rows(in_ref.shape[0], some)
    query_ref[...] = nn(cross_input_ref[...], query_weight_ref[...]).astype(BFLOAT)


def mlp_kernel(
    attn_ref,
    project_ref,
    after_ref,
    modulation_ref,
    out_grad_ref,
    fc1_ref,
    fc2_ref,
    out_ref,
    res_grad_ref,
    cross_out_grad_ref,
    attn_grad_ref,
    sums_ref,
    part_ref,
    input_ref,
    grad_ref,
    input_t,
    grad_t,
    joined_ref,
    branch_ref,
    in_grad_ref,
):
    step = pl.program_id(0) * pl.num_programs(1) + pl.program_id(1)
    last = pl.num_programs(0) * pl.num_programs(1) - 1
    frames = attn_ref.shape[0]
    gate = block_of(modulation_ref, GATE_MLP)
    scale = 1.0 + block_of(modulation_ref, SCALE_MLP)

    @pl.when(step == 0)
    def _():
        shift = block_of(modulation_ref, SHIFT_MLP)
        joined_ref[...] = after_ref[...] + nn(attn_ref[...], project_ref[...])

        def some(rows, carry):
            norm, _ = normed(joined_ref[rows, :])
            input_ref[rows, :] = (norm * scale + shift).astype(BFLOAT)
            grad_ref[rows, :] = (gate * out_grad_ref[rows, :].astype(FLOAT)).astype(BFLOAT)
            return carry

        over_rows(frames, some)
        input_t[...] = input_ref[...].T
        grad_t[...] = grad_ref[...].T

    fc1, fc2 = fc1_ref[0], fc2_ref[0]
    act, slope = gelu_parts(nn(input_ref[...], fc1))
    act = act.astype(BFLOAT)
    pre_grad = (nn(grad_ref[...], fc2) * slope).astype(BFLOAT)
    branch, in_grad = nt(act, fc2), nt(pre_grad, fc1)

    @pl.when(step == 0)
    def _():
        branch_ref[...] = branch
        in_grad_ref[...] = in_grad

    @pl.when(step > 0)
    def _():
        branch_ref[...] += branch
        in_grad_ref[...] += in_grad

    far, size = part_ref.shape[2], part_ref.shape[4]
    for kind, product in enumerate((nn(input_t[...], pre_grad), nn(grad_t[...], act))):
        product = product.astype(BFLOAT)
        for place in range(4 * far):
            part_ref[0, place % 4, place // 4, kind] = product[place * size : (place + 1) * size]

    @pl.when(step == last)
    def _():
        def some(rows, carry):
            gate_sum, shift_sum, scale_sum = carry
            joined, branch_here = joined_ref[rows, :], branch_ref[rows, :]
            out_grad, in_grad_here = out_grad_ref[rows, :].astype(FLOAT), in_grad_ref[rows, :]
            out_ref[rows, :] = (joined + gate * branch_here).astype(BFLOAT)
            norm, rate = normed(joined)
            res_grad = out_grad + normed_back(in_grad_here * scale, norm, rate)
            res_grad_ref[rows, :] = res_grad
            cross_out_grad_ref[rows, :] = res_grad.astype(BFLOAT)
            return (
                gate_sum + down(out_grad * branch_here),
                shift_sum + down(in_grad_here),
                scale_sum + down(in_grad_here * norm),
            )

        gate_sum, shift_sum, scale_sum = over_rows(frames, some, no_sums(3))
        sums_ref[:, :D] = shift_sum
        sums_ref[:, D : 2 * D] = scale_sum
        sums_ref[:, 2 * D :] = gate_sum
        attn_grad_ref[...] = nt(cross_out_grad_ref[...], project_ref[...]).astype(BFLOAT)


def between_back_kernel(
    query_grad_ref,
    query_weight_ref,
    after_ref,
    res_grad_ref,
    branch_ref,
    modulation_ref,
    project_ref,
    self_res_ref,
    out_grad_ref,
    attn_grad_ref,
    sums_ref,
    in_grad_ref,
):
    in_grad_ref[...] = nt(query_grad_ref[...], query_weight_ref[...])
    gate = block_of(modulation_ref, GATE_SELF)

    def some(rows, carry):
        norm, rate = normed(after_ref[rows, :])
        res_grad = res_grad_ref[rows, :] + normed_back(in_grad_ref[rows, :], norm, rate)
        self_res_ref[rows, :] = res_grad
        out_grad_ref[rows, :] = (gate * res_grad).astype(BFLOAT)
        return (carry[0] + down(res_grad * branch_ref[rows, :]),)

    (sums_ref[...],) = over_rows(after_ref.shape[0], some, no_sums(1))
    attn_grad_ref[...] = nt(out_grad_ref[...], project_ref[...]).astype(BFLOAT)


def first_back_kernel(
    query_grad_ref,
    pair_grad_ref,
    query_weight_ref,
    pair_weight_ref,
    in_ref,
    modulation_ref,
    self_res_ref,
    out_ref,
    sums_ref,
    in_grad_ref,
):
    in_grad_ref[...] = nt(query_grad_ref[...], query_weight_ref[...]) + nt(
        pair_grad_ref[...], pair_weight_ref[...]
    )
    scale = 1.0 + block_of(modulation_ref, SCALE_SELF)

    def some(rows, carry):
        norm, rate = normed(in_ref[rows, :].astype(FLOAT))
        grad = in_grad_ref[rows, :]
        res_grad = self_res_ref[rows, :] + normed_back(grad * scale, norm, rate)
        out_ref[rows, :] = res_grad.astype(BFLOAT)
        return carry[0] + down(grad), carry[1] + down(grad * norm)

    shift_sum, scale_sum = over_rows(in_ref.shape[0], some, no_sums(2))
    sums_ref[:, :D] = shift_sum
    sums_ref[:, D:] = scale_sum


def left_half(weights):
    return weights, pl.BlockSpec((D, D), lambda step: (0, 0))


def right_half(weights):
    return weights, pl.BlockSpec((D, D), lambda step: (0, 1))


def frame_call(kernel, results, *operands, scratch=()):
    specs, arrays = [], []
    for operand in operands:
        if isinstance(operand, tuple):
            arrays.append(operand[0])
            specs.append(operand[1])
        else:
            arrays.append(operand)
            specs.append(whole_block(operand.shape))
    return pl.pallas_call(
        kernel,
        grid=(1,),
        in_specs=specs,
        out_specs=[whole_block(shape) for shape, _ in results],
        out_shape=[jax.ShapeDtypeStruct(shape, kind) for shape, kind in results],
        scratch_shapes=[pltpu.VMEM(shape, kind) for shape, kind in scratch],
        compiler_params=room(48),
        cost_estimate=LIGHT,
    )(*arrays)


MLP_TILE = 768


def mlp_both(cross_attn, project, after_self, modulation, out_grad, weights):
    frames = cross_attn.shape[0]
    far = lax.axis_size("far")
    rows = D // (4 * far)
    tiles = HALF // MLP_TILE
    once = dict(pipeline_mode=pl.Buffered(1))
    whole = pl.BlockSpec((frames, D), lambda half, tile: (0, 0), **once)
    square = (frames, D)
    return pl.pallas_call(
        mlp_kernel,
        grid=(2, tiles),
        in_specs=[
            whole,
            pl.BlockSpec((D, D), lambda half, tile: (0, 1), **once),
            whole,
            pl.BlockSpec((1, 6 * D), lambda half, tile: (0, 0)),
            whole,
            pl.BlockSpec((1, D, MLP_TILE), lambda half, tile: (half, 0, tile)),
            pl.BlockSpec((1, D, MLP_TILE), lambda half, tile: (half, 0, tile + tiles)),
        ],
        out_specs=[whole] * 4
        + [
            pl.BlockSpec((1, 3 * D), lambda half, tile: (0, 0)),
            pl.BlockSpec(
                (1, 4, far, 2, rows, MLP_TILE), lambda half, tile: (half, 0, 0, 0, 0, tile)
            ),
        ],
        out_shape=[
            jax.ShapeDtypeStruct(square, BFLOAT),
            jax.ShapeDtypeStruct(square, FLOAT),
            jax.ShapeDtypeStruct(square, BFLOAT),
            jax.ShapeDtypeStruct(square, BFLOAT),
            jax.ShapeDtypeStruct((1, 3 * D), FLOAT),
            jax.ShapeDtypeStruct((2, 4, far, 2, rows, HALF), BFLOAT),
        ],
        scratch_shapes=[
            pltpu.VMEM(square, BFLOAT),
            pltpu.VMEM(square, BFLOAT),
            pltpu.VMEM((D, frames), BFLOAT),
            pltpu.VMEM((D, frames), BFLOAT),
            pltpu.VMEM(square, FLOAT),
            pltpu.VMEM(square, FLOAT),
            pltpu.VMEM(square, FLOAT),
        ],
        compiler_params=room(48),
        cost_estimate=LIGHT,
    )(cross_attn, project, after_self, modulation, out_grad, weights, weights)


def per_device(
    block_in,
    text,
    timesteps,
    frame_mask,
    text_mask,
    cotangent,
    w_ada,
    w_qkv,
    w_out,
    w_cq,
    w_cout,
    w_ckv,
    w_fc1,
    w_fc2,
    row_state,
    col_state,
):
    clips = lax.axis_size(DP)
    devices = clips * 2
    data_at = lax.axis_index(DP)
    head_at = lax.axis_index("head")
    flat_at = data_at * 2 + head_at
    frames = block_in.shape[1]
    rows = w_qkv.shape[0]

    far = far_links()
    x_first = [far[0], row_link(), core_link()]
    y_first = [row_link(), far[0], core_link()]
    first = [
        gather_chain(
            with_bits(
                jnp.concatenate([w_qkv[:, :D], w_out, w_qkv[:, D:]], axis=1).astype(BFLOAT), "last"
            ),
            "last",
            far[:0:-1],
        )
    ]
    second = [
        gather_chain(
            with_bits(jnp.concatenate([w_cq, w_cout], axis=1).astype(BFLOAT), "last"),
            "last",
            far[:0:-1] + x_first,
        ),
        gather_chain(
            with_bits(w_ckv.astype(BFLOAT).reshape(w_ckv.shape[0], D), "columns"),
            "columns",
            far[:0:-1] + y_first,
        ),
    ]
    mlp_shard = jnp.concatenate([w_fc1.astype(BFLOAT), w_fc2.T.astype(BFLOAT)], axis=1)
    inputs = swap_place(block_in[0])
    joint_mask = jnp.concatenate([frame_mask[0], text_mask[0]])

    def add_step(link):
        return lambda state: state + cross(state, link)

    def project(steps):
        condition = embed_part(steps, flat_at * rows, rows)
        product = jnp.dot(condition, w_ada.astype(BFLOAT), preferred_element_type=FLOAT)
        return condition, product.reshape(clips // 2, 2, 6 * D)

    def keep_step(link):
        def step(state):
            condition, product = state
            bit = bit_of(link)
            dim = 1 if link == row_link() else dp_bits() - link[1].bit_length()
            kept = lax.dynamic_slice_in_dim(product, bit, 1, axis=dim)
            sent = lax.dynamic_slice_in_dim(product, 1 - bit, 1, axis=dim)
            product = kept + cross(sent, link)
            if link == row_link():
                product = product.reshape((2,) * (dp_bits() - 1) + (6 * D,))
            return condition, product

        return step

    def last_step(state):
        condition, product = state
        return condition, (product + cross(product, core_link())).reshape(1, 6 * D)

    steps = lax.dynamic_update_slice(jnp.zeros((clips,), jnp.int32), timesteps, (data_at,))
    timing = Chain(
        steps,
        [add_step(link) for link in [core_link()] + far_links()[1:] + far_links()[:1]]
        + [lambda steps: keep_step(row_link())(project(steps))]
        + [keep_step(link) for link in far_links()[1:] + far_links()[:1]]
        + [last_step],
    )
    far_count = len(far) - 1
    slots = far_count + 3
    for slot in range(slots):
        if slot < far_count:
            timing.advance(1 + (slot == 0) + (slot == far_count - 1))
        else:
            timing.advance((1, far_count, 2)[slot - far_count])
        if slot == far_count:
            joint = first[0].state
            first = [
                gather_chain(joint[..., : 2 * D], "last", x_first),
                gather_chain(joint[..., 2 * D :], "last", y_first),
            ]
        for chain in first:
            chain.advance()
        if slot >= 2:
            for chain in second:
                chain.advance()
        if slot == far_count - 1:
            inputs, mlp_shard, joint_mask, text = tie(
                [timing] + first + second, inputs, mlp_shard, joint_mask, text
            )
            mlp_all = lax.all_gather(mlp_shard, HEAD + DP, axis=0, tiled=True)
            masks = from_clip_core(joint_mask)
            clip_text = from_clip_core(text[0])
        elif slot < slots - 1:
            tie([timing] + first + (second if slot == far_count else []))
        else:
            wide = tie([timing] + first, w_ada, w_qkv, w_out, w_cq, w_cout, w_fc1, w_fc2)
            masters = [
                jnp.concatenate(wide[:5], axis=1),
                w_ckv.reshape(w_ckv.shape[0], D),
                jnp.concatenate([wide[5], wide[6].T], axis=1),
            ]
            (weight_squares,) = whole_call(weight_kernel, [(1, LINE)], *masters)
    condition, modulation = timing.finish()
    query_out, w_key_value = [chain.finish().reshape(D, 2 * D) for chain in first]
    square = (frames, D)
    core_at = data_at % 2
    own_allowed = lax.dynamic_slice_in_dim(masks, core_at * frames, frames)
    other_allowed = lax.dynamic_slice_in_dim(masks, (1 - core_at) * frames, frames)
    own_bias, other_bias = bias_of(own_allowed), bias_of(other_allowed)
    text_bias = bias_of(masks[2 * frames :])

    self_input, query, key_value = frame_call(
        first_kernel,
        [(square, BFLOAT), (square, BFLOAT), ((frames, 2 * D), BFLOAT)],
        inputs,
        modulation,
        left_half(query_out),
        w_key_value,
    )
    other_key_value = cross(key_value, core_link())
    query, other_key_value = tie(second, query, other_key_value)
    for chain in second:
        chain.advance()

    self_keys = [(key_value, own_bias), (other_key_value, other_bias)]
    self_attn, self_logs = attend(query, self_keys, plain_places, 2)
    self_attn, cotangent = tie(second, self_attn, cotangent)
    swapped_cotangent = swap_only(cotangent[0])
    cross_pair, w_text = [chain.finish() for chain in second]
    cross_pair, w_text = cross_pair.reshape(D, 2 * D), w_text.reshape(DT, 2 * D)
    self_branch, after_self, cross_input, cross_query = frame_call(
        between_kernel,
        [(square, FLOAT), (square, FLOAT), (square, BFLOAT), (square, BFLOAT)],
        self_attn,
        right_half(query_out),
        inputs,
        modulation,
        left_half(cross_pair),
    )

    text_pair = nn(clip_text, w_text).astype(BFLOAT)
    text_keys = [(text_pair, text_bias)]
    cross_attn, cross_logs = attend(cross_query, text_keys, half_places, PAIRS // 2)

    cross_attn, own, cotangent = tie([], cross_attn, on_own_chip(), cotangent)
    out_grad = jnp.where(own, cotangent[0], swapped_cotangent)
    block_out, cross_res_grad, cross_out_grad, cross_attn_grad, mlp_sums, mlp_part = mlp_both(
        cross_attn,
        cross_pair,
        after_self,
        modulation,
        out_grad,
        mlp_all.reshape(2, D, 2 * HALF),
    )
    mlp_part = lax.psum_scatter(
        mlp_part.reshape((8,) + mlp_part.shape[2:]),
        HEAD + ("near", "core"),
        scatter_dimension=0,
        tiled=False,
    )

    cross_query_grad, text_pair_grad = attend_back(
        cross_query, cross_attn, cross_attn_grad, cross_logs, text_keys, half_places, PAIRS // 2
    )
    self_res_grad, self_out_grad, self_attn_grad, gate_self_grad = frame_call(
        between_back_kernel,
        [(square, FLOAT), (square, BFLOAT), (square, BFLOAT), ((1, D), FLOAT)],
        cross_query_grad,
        left_half(cross_pair),
        after_self,
        cross_res_grad,
        self_branch,
        modulation,
        right_half(query_out),
        scratch=[(square, FLOAT)],
    )

    query_grad, own_pair_grad, other_pair_grad = attend_back(
        query, self_attn, self_attn_grad, self_logs, self_keys, plain_places, 2
    )
    pair_grad = (
        own_pair_grad.astype(FLOAT) + cross(other_pair_grad, core_link()).astype(FLOAT)
    ).astype(BFLOAT)
    last_chains = [
        scatter_chain(
            outer((self_input, query_grad), (self_attn, self_out_grad)), "last", False
        ),
        scatter_chain(outer((self_input, pair_grad)), "last", True),
    ]
    cross_query_grad, text_pair_grad = tie(last_chains, cross_query_grad, text_pair_grad)
    for chain in last_chains:
        chain.advance()
    cross_chains = [
        scatter_chain(
            outer((cross_input, cross_query_grad), (cross_attn, cross_out_grad)), "last", False
        ),
        scatter_chain(outer((clip_text, text_pair_grad)), "columns", True),
    ]
    query_grad, pair_grad = tie(cross_chains + last_chains, query_grad, pair_grad)
    for chain in last_chains + cross_chains:
        chain.advance()
    input_grad, self_sums = frame_call(
        first_back_kernel,
        [(square, BFLOAT), ((1, 2 * D), FLOAT)],
        query_grad,
        pair_grad,
        left_half(query_out),
        w_key_value,
        inputs,
        modulation,
        self_res_grad,
        scratch=[(square, FLOAT)],
    )
    modulation_grad = jnp.concatenate([self_sums, gate_self_grad, mlp_sums], axis=-1)

    def join_step(link):
        def step(state):
            other = cross(state, link)
            upper = bit_of(link) == 1
            dim = dp_bits() - 1 if link[0] == HEAD else dp_bits() - link[1].bit_length()
            low, high = jnp.where(upper, other, state), jnp.where(upper, state, other)
            return jnp.concatenate([low, high], axis=dim)

        return step

    far = far_links()
    shape = (1,) * dp_bits() + (6 * D,)
    joining = Chain(
        modulation_grad,
        [lambda state: (state + cross(state, core_link())).reshape(shape)]
        + [join_step(link) for link in far[:0:-1] + [far[0], row_link()]],
    )

    chains = last_chains + cross_chains
    joining.advance()
    block_out, input_grad, mlp_part = tie([joining] + chains, block_out, input_grad, mlp_part)
    mlp_raw = lax.psum_scatter(mlp_part, "far", scatter_dimension=0, tiled=False).astype(FLOAT)
    for chain in chains:
        chain.advance()
    joining.advance(len(far) - 1)
    block_out, input_grad = tie([joining] + chains, block_out, input_grad)
    for chain in chains:
        chain.advance()
    joining.advance(2)
    block_out, input_grad, mlp_raw = tie([joining] + chains, block_out, input_grad, mlp_raw)
    for chain in chains:
        chain.advance()
    block_out, input_grad = tie(chains, block_out, input_grad)
    other_out, other_grad = swap_only(block_out), swap_only(input_grad)
    for chain in cross_chains:
        chain.advance()
    tie(cross_chains)
    modulation_grad = joining.finish()
    ada_raw = jnp.einsum(
        "cr,cx->rx",
        condition.astype(FLOAT),
        modulation_grad.reshape(clips, 6 * D),
        precision=PRECISE,
    )

    cross_raw, ckv_raw = [chain.finish() for chain in cross_chains]
    query_out_raw, pair_raw = [chain.finish() for chain in last_chains]

    place = jnp.stack([data_at, head_at]).astype(jnp.int32)
    raw_grads = [ada_raw, query_out_raw, pair_raw, cross_raw, ckv_raw, mlp_raw]
    (statistics,) = whole_call(
        statistics_kernel, [(STAT_LINES, LINE)], place, weight_squares, *raw_grads, places=1
    )
    sums = sum_all(statistics)
    shapes = [(rows, columns) for columns in COL_SIZES[:5]]
    shapes += [masters[1].shape] + [(rows * 2, HALF)] * 2
    line = (1, LINE)
    row_new, col_new, norm, update_squares, *rest = whole_call(
        update_kernel,
        [(ROW_LINES, LINE), (COL_LINES, LINE), line, line]
        + shapes
        + [master.shape for master in masters],
        place,
        sums,
        row_state.reshape(ROW_LINES, LINE),
        col_state.reshape(COL_LINES, LINE),
        *raw_grads,
        places=1,
    )
    clipped, updates = list(rest[:8]), rest[8:]
    clipped[5] = clipped[5].reshape(w_ckv.shape)
    clipped[7] = clipped[7].T
    late, _ = tie([], on_own_chip(), update_squares)
    block_out = jnp.where(late, block_out, other_out)
    input_grad = jnp.where(late, input_grad, other_grad)
    update_squares, block_out, input_grad, *clipped = tie(
        [], sum_all(update_squares), block_out, input_grad, *clipped
    )
    updated = list(
        whole_call(
            apply_kernel,
            shapes,
            update_squares,
            sums[STAT_LINES - 2 : STAT_LINES - 1],
            *masters,
            *updates,
        )
    )
    updated[5] = updated[5].reshape(w_ckv.shape)
    updated[7] = updated[7].T
    return (
        block_out[None],
        input_grad[None],
        norm[0, 0],
        row_new.reshape(-1),
        col_new.reshape(-1),
        *clipped,
        *updated,
    )


def solution(mesh):
    devices = mesh.devices
    refined = jax.sharding.Mesh(devices.reshape(devices.shape[0] // 4, 2, 2, 2), ALL)
    return jax.shard_map(
        per_device,
        mesh=refined,
        in_specs=(
            P(DP, "head", None),
            P(DP, None, None),
            P(DP),
            P(DP, None),
            P(DP, None),
            P(DP, "head", None),
            P(ALL, None),
            P(ALL, None),
            P(ALL, None),
            P(ALL, None),
            P(ALL, None),
            P(DP, None, "head"),
            P(DP, "head"),
            P("head", DP),
            P(),
            P(),
        ),
        out_specs=(
            P(DP, "head", None),
            P(DP, "head", None),
            P(),
            P(),
            P(),
            P(ALL, None),
            P(ALL, None),
            P(ALL, None),
            P(ALL, None),
            P(ALL, None),
            P(DP, None, "head"),
            P(DP, "head"),
            P("head", DP),
            P(ALL, None),
            P(ALL, None),
            P(ALL, None),
            P(ALL, None),
            P(ALL, None),
            P(DP, None, "head"),
            P(DP, "head"),
            P("head", DP),
        ),
        check_vma=False,
    )
```

```python
import functools

import jax
import jax.numpy as jnp
from jax import lax
from jax.experimental import pallas as pl
from jax.experimental.pallas import tpu as pltpu
from jax.sharding import PartitionSpec as P

D = 768
FF = 3072
DT = 1024
HD = 64
HALF = FF // 2

PRECISE = lax.Precision.HIGHEST
FLOAT = jnp.float32
BFLOAT = jnp.bfloat16
EPS_NORM = 1e-06
EPS_FACTOR = 1e-30
CLIP_NORM = 1.0
CLIP_UPDATE = 0.25
DECAY_RATE = 0.5
RELATIVE_RATE = 4.0
SCALE_FLOOR = 0.001
SCORE_SCALE = 0.125
MASKED_SCORE = -1e30
DP = ("far", "near", "core")
ALL = DP + ("head",)
HEAD = ("head",)
PAIR = 2 * HD
PAIRS = D // PAIR


def embed_part(steps, first, count):
    halfway = D // 2
    place = first + jnp.arange(count)
    freqs = jnp.exp(-jnp.log(10000.0) * (place % halfway).astype(FLOAT) / halfway)
    angles = steps.astype(FLOAT)[:, None] * freqs
    waves = jnp.where(place < halfway, jnp.cos(angles), jnp.sin(angles))
    return jax.nn.silu(waves).astype(BFLOAT)


def core_link():
    return (DP, 1)


def row_link():
    return (HEAD, 1)


def far_links():
    masks, mask = [], 2
    while mask < lax.axis_size(DP):
        masks.append(mask)
        mask = mask * 2
    return [(DP, mask) for mask in masks]


def dp_bits():
    return lax.axis_size(DP).bit_length() - 1


def bit_of(link):
    return (lax.axis_index(link[0]) // link[1]) % 2


def cross(values, link):
    pairs = [(place, place ^ link[1]) for place in range(lax.axis_size(link[0]))]
    return lax.ppermute(values, link[0], pairs)


def dim_of(link, head):
    if link[0] == HEAD:
        return {"first": 0, "last": dp_bits(), "columns": dp_bits() + 1}[head]
    return (1 if head == "first" else 0) + dp_bits() - link[1].bit_length()


def leading(head):
    return dp_bits() + (0 if head == "columns" else 1)


def grow(block, link, head):
    other = cross(block, link)
    upper = bit_of(link) == 1
    low = jnp.where(upper, other, block)
    high = jnp.where(upper, block, other)
    return jnp.concatenate([low, high], axis=dim_of(link, head))


def shrink(block, link, head, kind=BFLOAT):
    dim, bit = dim_of(link, head), bit_of(link)
    half = block.shape[dim] // 2
    kept = lax.dynamic_slice_in_dim(block, bit * half, half, axis=dim)
    sent = lax.dynamic_slice_in_dim(block, (1 - bit) * half, half, axis=dim)
    return (kept.astype(FLOAT) + cross(sent.astype(BFLOAT), link).astype(FLOAT)).astype(kind)


class Chain:
    def __init__(self, state, steps):
        self.state, self.steps = state, list(steps)

    def advance(self, count=1):
        for _ in range(min(count, len(self.steps))):
            self.state = self.steps.pop(0)(self.state)
        return self

    def finish(self):
        return self.advance(len(self.steps)).state


def tie(chains, *values):
    states, values = lax.optimization_barrier(([chain.state for chain in chains], values))
    for chain, state in zip(chains, states):
        chain.state = state
    return values


def gather_chain(block, head, links):
    return Chain(block, [lambda state, link=link: grow(state, link, head) for link in links])


def with_bits(shard, head):
    return shard.reshape((1,) * leading(head) + shard.shape)


def scatter_chain(matrix, head, row_early):
    bits = leading(head)
    rows, columns = matrix.shape[-2:]
    split = dp_bits() if head == "first" else bits
    block = matrix.reshape((2,) * bits + (rows // 2**split, columns))
    far = far_links()
    plane = [far[0], row_link()] if row_early else [row_link(), far[0]]
    order = [core_link()] + plane + far[1:]
    kinds = [BFLOAT] * (len(order) - 1) + [FLOAT]
    steps = [
        lambda state, link=link, kind=kind: shrink(state, link, head, kind)
        for link, kind in zip(order, kinds)
    ]
    return Chain(block, steps + [lambda state: state.reshape(state.shape[bits:])])


def sum_all(values):
    for link in [core_link()] + far_links() + [row_link()]:
        values = values + cross(values, link)
    return values


def on_own_chip():
    return bit_of(core_link()) == bit_of(row_link())


def swap_only(values):
    pairs = []
    for place in range(lax.axis_size(DP)):
        for head in range(2):
            if place & 1 != head:
                pairs.append((place * 2 + head, ((place & ~1) | head) * 2 + (place & 1)))
    return lax.ppermute(values, ALL, pairs)


def swap_place(values):
    return jnp.where(on_own_chip(), values, swap_only(values))


def from_clip_core(values):
    pairs = []
    for place in range(0, lax.axis_size(DP), 2):
        for head in range(2):
            pairs.append(((place + head) * 2 + head, (place + 1 - head) * 2 + head))
    return jnp.where(on_own_chip(), values, lax.ppermute(values, ALL, pairs))


def nt(left, right):
    return lax.dot_general(left, right, (((1,), (1,)), ((), ())), preferred_element_type=FLOAT)


def nn(left, right):
    return lax.dot_general(left, right, (((1,), (0,)), ((), ())), preferred_element_type=FLOAT)


def lanes_of(length):
    return lax.broadcasted_iota(jnp.int32, (length, PAIR), 1)


def with_spare(pair, head, spare):
    lane = lanes_of(pair.shape[0])
    rest = jnp.where(lane == HD * (1 - head), spare, jnp.zeros_like(pair))
    return jnp.where(lane // HD == head, pair, rest)


def attend_kernel(blocks, *refs):
    query_ref, out_ref, log_ref = refs[0], refs[1 + 3 * blocks], refs[2 + 3 * blocks]
    ins = refs[1 : 1 + 3 * blocks]
    one = jnp.ones((1, 1), BFLOAT)
    for place in range(log_ref.shape[0]):
        columns = pl.ds(place * PAIR, PAIR)
        queries = query_ref[:, columns] * jnp.asarray(SCORE_SCALE, BFLOAT)
        values_t = [ref[:, columns].T for ref in ins[1::3]]
        results, logs = [], []
        for head in range(2):
            query = with_spare(queries, head, one)
            scores = [
                nt(with_spare(key_ref[:, columns], head, bias_ref[...]), query)
                for key_ref, bias_ref in zip(ins[0::3], ins[2::3])
            ]
            peak = functools.reduce(
                jnp.maximum, [jnp.max(score, axis=0, keepdims=True) for score in scores]
            )
            total = None
            for score, value_t in zip(scores, values_t):
                probs = jnp.exp(score - peak).astype(BFLOAT)
                row = lax.broadcasted_iota(jnp.int32, value_t.shape, 0)
                term = nn(jnp.where(row // HD == head, value_t, one), probs)
                total = term if total is None else total + term
            weight = total[HD * (1 - head) : HD * (1 - head) + 1, :]
            results.append(total[HD * head : HD * (head + 1), :] / weight)
            logs.append(peak + jnp.log(weight))
        out_ref[:, columns] = jnp.concatenate(results, axis=0).T.astype(BFLOAT)
        log_ref[place] = jnp.concatenate(logs, axis=0)


def back_kernel(blocks, places, *refs):
    query_ref, out_ref, grad_ref, log_ref = refs[:4]
    ins = refs[4 : 4 + 3 * blocks]
    query_grad_ref, pair_grad_refs = refs[4 + 3 * blocks], refs[5 + 3 * blocks :]
    zero = jnp.zeros((1, 1), BFLOAT)
    one = jnp.ones((1, 1), BFLOAT)
    chooser = (
        lax.broadcasted_iota(jnp.int32, (8, PAIR), 1) // HD
        == lax.broadcasted_iota(jnp.int32, (8, PAIR), 0)
    ).astype(FLOAT)
    count = log_ref.shape[0]
    for place in range(count):
        columns = pl.ds(place * PAIR, PAIR)
        queries = query_ref[:, columns] * jnp.asarray(SCORE_SCALE, BFLOAT)
        out_grad = grad_ref[:, columns]
        product = out_ref[:, columns].astype(FLOAT) * out_grad.astype(FLOAT)
        inner = lax.dot_general(
            chooser,
            product,
            (((1,), (1,)), ((), ())),
            precision=PRECISE,
            preferred_element_type=FLOAT,
        )
        query_parts = [None, None]
        for block in range(blocks):
            keys, values = ins[3 * block][:, columns], ins[3 * block + 1][:, columns]
            bias, keys_t = ins[3 * block + 2][...], keys.T
            key_grad, value_grad = None, None
            for head in range(2):
                grad_here = with_spare(out_grad, head, zero)
                score = nt(with_spare(keys, head, bias), with_spare(queries, head, one))
                probs = jnp.exp(score - log_ref[place, head : head + 1, :])
                prob_grad = nt(values, grad_here)
                score_grad = (probs * (prob_grad - inner[head : head + 1, :])).astype(BFLOAT)
                value_term = nn(probs.astype(BFLOAT), grad_here)
                key_term = nn(score_grad, with_spare(queries, head, zero))
                query_term = nn(keys_t[HD * head : HD * (head + 1), :], score_grad)
                value_grad = value_term if value_grad is None else value_grad + value_term
                key_grad = key_term if key_grad is None else key_grad + key_term
                query_parts[head] = (
                    query_term if query_parts[head] is None else query_parts[head] + query_term
                )
            key_at, value_at = places(pl.program_id(0) * count + place)
            key_at = pl.multiple_of(key_at * PAIR, PAIR)
            value_at = pl.multiple_of(value_at * PAIR, PAIR)
            pair_grad_refs[block][:, pl.ds(key_at, PAIR)] = key_grad.astype(BFLOAT)
            pair_grad_refs[block][:, pl.ds(value_at, PAIR)] = value_grad.astype(BFLOAT)
        joined = jnp.concatenate(query_parts, axis=0) * SCORE_SCALE
        query_grad_ref[:, columns] = joined.T.astype(BFLOAT)


def column_block(length, count):
    return pl.BlockSpec((length, PAIR * count), lambda step: (0, step))


def plain_places(pair):
    return pair, pair + PAIRS


def half_places(pair):
    half, part = pair // (PAIRS // 2), pair % (PAIRS // 2)
    return half * PAIRS + part, half * PAIRS + PAIRS // 2 + part


def whole_block(shape):
    return pl.BlockSpec(shape, lambda pair: (0,) * len(shape))


def log_block(frames, count):
    return pl.BlockSpec((count, 2, frames), lambda step: (step, 0, 0))


def key_specs(key_values, places, count):
    specs, operands = [], []
    for joint, bias in key_values:
        length = joint.shape[0]
        specs += [
            pl.BlockSpec(
                (length, PAIR * count), lambda step: (0, places(step * count)[0] // count)
            ),
            pl.BlockSpec(
                (length, PAIR * count), lambda step: (0, places(step * count)[1] // count)
            ),
            whole_block((length, PAIR)),
        ]
        operands += [joint, joint, bias]
    return specs, operands


def room(mebibytes):
    return pltpu.CompilerParams(vmem_limit_bytes=mebibytes * 1024 * 1024)


LIGHT = pl.CostEstimate(flops=1000, bytes_accessed=1000, transcendentals=0)


def attend(queries, key_values, places, count=1):
    frames, blocks = queries.shape[0], len(key_values)
    specs, operands = key_specs(key_values, places, count)
    return pl.pallas_call(
        functools.partial(attend_kernel, blocks),
        grid=(PAIRS // count,),
        in_specs=[column_block(frames, count)] + specs,
        out_specs=[column_block(frames, count), log_block(frames, count)],
        out_shape=[
            jax.ShapeDtypeStruct((frames, D), BFLOAT),
            jax.ShapeDtypeStruct((PAIRS, 2, frames), FLOAT),
        ],
        compiler_params=room(48),
        cost_estimate=LIGHT,
    )(queries, *operands)


def attend_back(queries, out, out_grad, logs, key_values, places, count=1):
    frames, blocks = queries.shape[0], len(key_values)
    specs, operands = key_specs(key_values, places, count)
    return pl.pallas_call(
        functools.partial(back_kernel, blocks, places),
        grid=(PAIRS // count,),
        in_specs=[column_block(frames, count)] * 3 + [log_block(frames, count)] + specs,
        out_specs=[column_block(frames, count)] + [whole_block(joint.shape) for joint, _ in key_values],
        out_shape=[jax.ShapeDtypeStruct((frames, D), BFLOAT)]
        + [jax.ShapeDtypeStruct(joint.shape, BFLOAT) for joint, _ in key_values],
        compiler_params=room(48),
        cost_estimate=LIGHT,
    )(queries, out, out_grad, logs, *operands)


def outer_kernel(*refs):
    out_ref, count = refs[-1], len(refs) // 2
    at = 0
    for place in range(count):
        left, right = refs[2 * place], refs[2 * place + 1]
        width = right.shape[1]
        product = lax.dot_general(
            left[...], right[...], (((0,), (0,)), ((), ())), preferred_element_type=FLOAT
        )
        out_ref[:, at : at + width] = product.astype(BFLOAT)
        at += width


def outer(*pairs):
    operands = [matrix for pair in pairs for matrix in pair]
    shape = (pairs[0][0].shape[1], sum(right.shape[1] for _, right in pairs))
    return pl.pallas_call(
        outer_kernel,
        out_shape=jax.ShapeDtypeStruct(shape, BFLOAT),
        compiler_params=room(48),
        cost_estimate=LIGHT,
    )(*operands)


def bias_of(allowed):
    column = jnp.where(allowed > 0, 0.0, MASKED_SCORE).astype(BFLOAT)
    return jnp.broadcast_to(column[:, None], (allowed.shape[0], PAIR))


LINE = 128
ROW_SIZES = [D, D, D, D, D, DT, D, FF]
COL_SIZES = [6 * D, 3 * D, D, D, D, 2 * D, FF, D]
ROW_LINES = sum(ROW_SIZES) // LINE
COL_LINES = sum(COL_SIZES) // LINE
STAT_LINES = ROW_LINES + COL_LINES + 2


def starts_of(sizes, first):
    starts = []
    for size in sizes:
        starts.append(first)
        first += size // LINE
    return starts


ROW_STARTS = starts_of(ROW_SIZES, 0)
COL_STARTS = starts_of(COL_SIZES, ROW_LINES)


def lines_at(line, shape):
    return lax.broadcasted_iota(jnp.int32, shape, 1) + line * LINE


def down_lines(column, offset, lines):
    shape = (column.shape[0], LINE)
    wanted = lax.broadcasted_iota(jnp.int32, shape, 0) + offset
    return [
        jnp.sum(jnp.where(lines_at(line, shape) == wanted, column, 0.0), axis=0, keepdims=True)
        for line in range(lines)
    ]


def from_lines(lines, offset, count):
    shape = (count, LINE)
    wanted = lax.broadcasted_iota(jnp.int32, shape, 0) + offset
    total = jnp.zeros(shape, FLOAT)
    for line in range(lines.shape[0]):
        here = jnp.where(lines_at(line, shape) == wanted, lines[line : line + 1, :], 0.0)
        total = total + here
    return jnp.sum(total, axis=1, keepdims=True)


def pieces_of(grad_refs):
    ada, query_out, key_value, cross_pair, text_pair, mlp = grad_refs
    return [
        [(ada, 0, 6 * D)],
        [(query_out, 0, D), (key_value, 0, 2 * D)],
        [(query_out, D, D)],
        [(cross_pair, 0, D)],
        [(cross_pair, D, D)],
        [(text_pair, 0, D)],
        [(mlp.at[0], 0, HALF)],
        [(mlp.at[1], 0, HALF)],
    ]


def joined_pieces(refs):
    square, text_pair, mlp = refs
    parts, at = [], 0
    for place in range(5):
        parts.append((square, at, COL_SIZES[place]))
        at += COL_SIZES[place]
    return parts + [(text_pair, 0, D), (mlp, 0, HALF), (mlp, HALF, HALF)]


def statistics_kernel(place_ref, weight_ref, *refs):
    grad_refs, out_ref = refs[:6], refs[6]
    data_at, head_at = place_ref[0], place_ref[1]
    flat_at = data_at * 2 + head_at
    out_ref[STAT_LINES - 2 : STAT_LINES - 1, :] = weight_ref[...]
    out_ref[STAT_LINES - 1 : STAT_LINES, :] = jnp.zeros((1, LINE), FLOAT)
    for place, parts in enumerate(pieces_of(grad_refs)):
        across, down = 0.0, []
        for ref, first, columns in parts:
            rows = ref.shape[0]
            wide = jnp.zeros((rows, LINE), FLOAT)
            for line in range(columns // LINE):
                piece = ref[:, first + line * LINE : first + (line + 1) * LINE]
                square = piece * piece
                wide = wide + square
                down.append(jnp.sum(square, axis=0, keepdims=True))
            across = across + jnp.sum(wide, axis=1, keepdims=True)
        offset = (flat_at if place < 5 else data_at) * rows
        row_start, col_start = ROW_STARTS[place], COL_STARTS[place]
        if place == 7:
            row_start, col_start = col_start, row_start
        row_lines = (COL_SIZES if place == 7 else ROW_SIZES)[place] // LINE
        for line, entry in enumerate(down_lines(across, offset, row_lines)):
            out_ref[row_start + line : row_start + line + 1, :] = entry
        groups = {5: 2}.get(place, 1)
        size = len(down) // groups
        for line, entry in enumerate(down):
            if place < 5:
                out_ref[col_start + line : col_start + line + 1, :] = entry
            else:
                for half in range(2):
                    at = col_start + (line // size * 2 + half) * size + line % size
                    out_ref[at : at + 1, :] = jnp.where(head_at == half, entry, 0.0)


def lane_of(lines, lane):
    shape = (1, LINE)
    here = lax.broadcasted_iota(jnp.int32, shape, 1) == lane
    return jnp.sum(jnp.where(here, lines, 0.0), axis=1, keepdims=True)


def update_kernel(place_ref, sums_ref, row_ref, col_ref, *refs):
    grad_refs, outs = refs[:6], refs[6:]
    row_out, col_out, norm_out, total_out = outs[:4]
    clipped_refs, update_refs = outs[4:12], joined_pieces(outs[12:15])
    data_at, head_at = place_ref[0], place_ref[1]
    flat_at = data_at * 2 + head_at
    row_sums = sums_ref[0:ROW_LINES, :]
    square_total = jnp.sum(jnp.sum(row_sums, axis=0, keepdims=True), axis=1, keepdims=True)
    norm = jnp.sqrt(square_total)
    factor = 1.0 / jnp.maximum(1.0, norm / CLIP_NORM)
    norm_out[...] = jnp.broadcast_to(norm, (1, LINE))
    square_factor = factor * factor
    lane = lax.broadcasted_iota(jnp.int32, (1, LINE), 1)
    totals = jnp.zeros((1, LINE), FLOAT)
    for place, parts in enumerate(pieces_of(grad_refs)):
        rows_len, cols_len = ROW_SIZES[place], COL_SIZES[place]
        row_from, row_to = ROW_STARTS[place], ROW_STARTS[place] + rows_len // LINE
        col_from, col_to = COL_STARTS[place], COL_STARTS[place] + cols_len // LINE
        new_row = DECAY_RATE * row_ref[row_from:row_to, :] + (1.0 - DECAY_RATE) * (
            square_factor * sums_ref[row_from:row_to, :] / float(cols_len) + EPS_FACTOR
        )
        col_from, col_to = col_from - ROW_LINES, col_to - ROW_LINES
        new_col = DECAY_RATE * col_ref[col_from:col_to, :] + (1.0 - DECAY_RATE) * (
            square_factor
            * sums_ref[ROW_LINES + col_from : ROW_LINES + col_to, :]
            / float(rows_len)
            + EPS_FACTOR
        )
        row_out[row_from:row_to, :] = new_row
        col_out[col_from:col_to, :] = new_col
        row_mean = (
            jnp.sum(jnp.sum(new_row, axis=0, keepdims=True), axis=1, keepdims=True) / rows_len
        )
        rows = parts[0][0].shape[0]
        offset = (flat_at if place < 5 else data_at) * rows
        if place == 7:
            down = lax.rsqrt(from_lines(new_col, offset, rows))
            across = jnp.where(head_at == 0, new_row[:12], new_row[12:])
            across = lax.rsqrt(across / row_mean)
        else:
            down = lax.rsqrt(from_lines(new_row, offset, rows) / row_mean)
            if place == 5:
                keys = jnp.where(head_at == 0, new_col[0:3], new_col[3:6])
                values = jnp.where(head_at == 0, new_col[6:9], new_col[9:12])
                across = lax.rsqrt(jnp.concatenate([keys, values], axis=0))
            elif place == 6:
                across = lax.rsqrt(jnp.where(head_at == 0, new_col[:12], new_col[12:]))
            else:
                across = lax.rsqrt(new_col)
        square = jnp.zeros((rows, LINE), FLOAT)
        line_at = 0
        for ref, first, columns in parts:
            for line in range(columns // LINE):
                piece = ref[:, first + line * LINE : first + (line + 1) * LINE] * factor
                update = piece * (down * across[line_at : line_at + 1, :])
                clipped_refs[place][:, line_at * LINE : (line_at + 1) * LINE] = piece
                update_ref, update_at, _ = update_refs[place]
                update_at += line_at * LINE
                update_ref[:, update_at : update_at + LINE] = update
                square = square + update * update
                line_at += 1
        total = jnp.sum(jnp.sum(square, axis=0, keepdims=True), axis=1, keepdims=True)
        totals = jnp.where(lane == place, total, totals)
    total_out[...] = totals


def apply_kernel(total_ref, weight_ref, *refs):
    master_refs, update_refs = joined_pieces(refs[:3]), joined_pieces(refs[3:6])
    for place in range(8):
        entries = float(ROW_SIZES[place] * COL_SIZES[place])
        total = lane_of(total_ref[...], place)
        weight = lane_of(weight_ref[...], place)
        limit = jnp.maximum(1.0, jnp.sqrt(total / entries) / CLIP_UPDATE)
        rate = RELATIVE_RATE * jnp.maximum(SCALE_FLOOR, jnp.sqrt(weight / entries))
        scale = rate / limit
        ref, at, columns = master_refs[place]
        update = update_refs[place][0][:, at : at + columns]
        refs[6 + place][...] = ref[:, at : at + columns] - scale * update


def weight_kernel(*refs):
    lane = lax.broadcasted_iota(jnp.int32, (1, LINE), 1)
    totals = jnp.zeros((1, LINE), FLOAT)
    for place in range(8):
        ref, at, columns = joined_pieces(refs[:3])[place]
        matrix = ref[:, at : at + columns]
        total = jnp.sum(jnp.sum(matrix * matrix, axis=0, keepdims=True), axis=1, keepdims=True)
        totals = jnp.where(lane == place, total, totals)
    refs[3][...] = totals


def whole_call(kernel, shapes, *operands, places=0):
    memory = [pl.BlockSpec(memory_space=pltpu.SMEM)] * places
    memory += [pl.BlockSpec(memory_space=pltpu.VMEM)] * (len(operands) - places)
    return pl.pallas_call(
        kernel,
        in_specs=memory,
        out_specs=[pl.BlockSpec(memory_space=pltpu.VMEM)] * len(shapes),
        out_shape=[jax.ShapeDtypeStruct(shape, FLOAT) for shape in shapes],
        compiler_params=room(48),
        cost_estimate=LIGHT,
    )(*operands)


GELU_WIDTH = 0.7978845608028654
GELU_CUBE = 0.044715


def gelu_parts(values):
    square = values * values
    bend = jnp.tanh(values * (GELU_WIDTH + GELU_WIDTH * GELU_CUBE * square))
    half = 0.5 + 0.5 * bend
    slope = GELU_WIDTH + 3.0 * GELU_WIDTH * GELU_CUBE * square
    return values * half, half + (0.5 * values) * (1.0 - bend * bend) * slope


ROWS = 512
SHIFT_SELF, SCALE_SELF, GATE_SELF, SHIFT_MLP, SCALE_MLP, GATE_MLP = range(6)


def block_of(modulation_ref, place):
    return modulation_ref[:, place * D : (place + 1) * D]


def over_rows(frames, body, start=None):
    def step(place, carry):
        return body(pl.ds(pl.multiple_of(place * ROWS, ROWS), ROWS), carry)

    return lax.fori_loop(0, frames // ROWS, step, start)


def normed(values):
    centered = values - jnp.mean(values, axis=-1, keepdims=True)
    rate = lax.rsqrt(jnp.mean(centered * centered, axis=-1, keepdims=True) + EPS_NORM)
    return centered * rate, rate


def normed_back(grad, norm, rate):
    inner = jnp.mean(grad * norm, axis=-1, keepdims=True)
    return rate * (grad - jnp.mean(grad, axis=-1, keepdims=True) - norm * inner)


def down(values):
    return jnp.sum(values, axis=0, keepdims=True)


def no_sums(count):
    return (jnp.zeros((1, D), FLOAT),) * count


def first_kernel(
    in_ref, modulation_ref, query_weight_ref, pair_weight_ref, self_input_ref, query_ref, pair_ref
):
    shift = block_of(modulation_ref, SHIFT_SELF)
    scale = 1.0 + block_of(modulation_ref, SCALE_SELF)

    def some(rows, carry):
        norm, _ = normed(in_ref[rows, :].astype(FLOAT))
        self_input_ref[rows, :] = (norm * scale + shift).astype(BFLOAT)
        return carry

    over_rows(in_ref.shape[0], some)
    pair_ref[...] = nn(self_input_ref[...], pair_weight_ref[...]).astype(BFLOAT)
    query_ref[...] = nn(self_input_ref[...], query_weight_ref[...]).astype(BFLOAT)


def between_kernel(
    attn_ref,
    project_ref,
    in_ref,
    modulation_ref,
    query_weight_ref,
    text_ref,
    text_weight_ref,
    branch_ref,
    after_ref,
    cross_input_ref,
    query_ref,
    text_pair_ref,
):
    branch_ref[...] = nn(attn_ref[...], project_ref[...])
    text_pair_ref[...] = nn(text_ref[...], text_weight_ref[...]).astype(BFLOAT)
    gate = block_of(modulation_ref, GATE_SELF)

    def some(rows, carry):
        after = in_ref[rows, :].astype(FLOAT) + gate * branch_ref[rows, :]
        after_ref[rows, :] = after
        norm, _ = normed(after)
        cross_input_ref[rows, :] = norm.astype(BFLOAT)
        return carry

    over_rows(in_ref.shape[0], some)
    query_ref[...] = nn(cross_input_ref[...], query_weight_ref[...]).astype(BFLOAT)


def mlp_kernel(
    attn_ref,
    project_ref,
    after_ref,
    modulation_ref,
    out_grad_ref,
    fc1_ref,
    fc2_ref,
    out_ref,
    res_grad_ref,
    cross_out_grad_ref,
    attn_grad_ref,
    sums_ref,
    part_ref,
    input_ref,
    grad_ref,
    input_t,
    grad_t,
    joined_ref,
    branch_ref,
    in_grad_ref,
):
    step = pl.program_id(0) * pl.num_programs(1) + pl.program_id(1)
    last = pl.num_programs(0) * pl.num_programs(1) - 1
    frames = attn_ref.shape[0]
    gate = block_of(modulation_ref, GATE_MLP)
    scale = 1.0 + block_of(modulation_ref, SCALE_MLP)

    @pl.when(step == 0)
    def _():
        shift = block_of(modulation_ref, SHIFT_MLP)
        joined_ref[...] = after_ref[...] + nn(attn_ref[...], project_ref[...])

        def some(rows, carry):
            norm, _ = normed(joined_ref[rows, :])
            input_ref[rows, :] = (norm * scale + shift).astype(BFLOAT)
            grad_ref[rows, :] = (gate * out_grad_ref[rows, :].astype(FLOAT)).astype(BFLOAT)
            return carry

        over_rows(frames, some)
        input_t[...] = input_ref[...].T
        grad_t[...] = grad_ref[...].T

    fc1, fc2 = fc1_ref[0], fc2_ref[0]
    act, slope = gelu_parts(nn(input_ref[...], fc1))
    act = act.astype(BFLOAT)
    pre_grad = (nn(grad_ref[...], fc2) * slope).astype(BFLOAT)
    branch, in_grad = nt(act, fc2), nt(pre_grad, fc1)

    @pl.when(step == 0)
    def _():
        branch_ref[...] = branch
        in_grad_ref[...] = in_grad

    @pl.when(step > 0)
    def _():
        branch_ref[...] += branch
        in_grad_ref[...] += in_grad

    far, size = part_ref.shape[2], part_ref.shape[4]
    for kind, product in enumerate((nn(input_t[...], pre_grad), nn(grad_t[...], act))):
        product = product.astype(BFLOAT)
        for place in range(4 * far):
            part_ref[0, place % 4, place // 4, kind] = product[place * size : (place + 1) * size]

    @pl.when(step == last)
    def _():
        def some(rows, carry):
            gate_sum, shift_sum, scale_sum = carry
            joined, branch_here = joined_ref[rows, :], branch_ref[rows, :]
            out_grad, in_grad_here = out_grad_ref[rows, :].astype(FLOAT), in_grad_ref[rows, :]
            out_ref[rows, :] = (joined + gate * branch_here).astype(BFLOAT)
            norm, rate = normed(joined)
            res_grad = out_grad + normed_back(in_grad_here * scale, norm, rate)
            res_grad_ref[rows, :] = res_grad
            cross_out_grad_ref[rows, :] = res_grad.astype(BFLOAT)
            return (
                gate_sum + down(out_grad * branch_here),
                shift_sum + down(in_grad_here),
                scale_sum + down(in_grad_here * norm),
            )

        gate_sum, shift_sum, scale_sum = over_rows(frames, some, no_sums(3))
        sums_ref[:, :D] = shift_sum
        sums_ref[:, D : 2 * D] = scale_sum
        sums_ref[:, 2 * D :] = gate_sum
        attn_grad_ref[...] = nt(cross_out_grad_ref[...], project_ref[...]).astype(BFLOAT)


def between_back_kernel(
    query_grad_ref,
    query_weight_ref,
    after_ref,
    res_grad_ref,
    branch_ref,
    modulation_ref,
    project_ref,
    self_res_ref,
    out_grad_ref,
    attn_grad_ref,
    sums_ref,
    in_grad_ref,
):
    in_grad_ref[...] = nt(query_grad_ref[...], query_weight_ref[...])
    gate = block_of(modulation_ref, GATE_SELF)

    def some(rows, carry):
        norm, rate = normed(after_ref[rows, :])
        res_grad = res_grad_ref[rows, :] + normed_back(in_grad_ref[rows, :], norm, rate)
        self_res_ref[rows, :] = res_grad
        out_grad_ref[rows, :] = (gate * res_grad).astype(BFLOAT)
        return (carry[0] + down(res_grad * branch_ref[rows, :]),)

    (sums_ref[...],) = over_rows(after_ref.shape[0], some, no_sums(1))
    attn_grad_ref[...] = nt(out_grad_ref[...], project_ref[...]).astype(BFLOAT)


def first_back_kernel(
    query_grad_ref,
    pair_grad_ref,
    query_weight_ref,
    pair_weight_ref,
    in_ref,
    modulation_ref,
    self_res_ref,
    out_ref,
    sums_ref,
    in_grad_ref,
):
    in_grad_ref[...] = nt(query_grad_ref[...], query_weight_ref[...]) + nt(
        pair_grad_ref[...], pair_weight_ref[...]
    )
    scale = 1.0 + block_of(modulation_ref, SCALE_SELF)

    def some(rows, carry):
        norm, rate = normed(in_ref[rows, :].astype(FLOAT))
        grad = in_grad_ref[rows, :]
        res_grad = self_res_ref[rows, :] + normed_back(grad * scale, norm, rate)
        out_ref[rows, :] = res_grad.astype(BFLOAT)
        return carry[0] + down(grad), carry[1] + down(grad * norm)

    shift_sum, scale_sum = over_rows(in_ref.shape[0], some, no_sums(2))
    sums_ref[:, :D] = shift_sum
    sums_ref[:, D:] = scale_sum


def left_half(weights):
    return weights, pl.BlockSpec((D, D), lambda step: (0, 0))


def right_half(weights):
    return weights, pl.BlockSpec((D, D), lambda step: (0, 1))


def frame_call(kernel, results, *operands, scratch=()):
    specs, arrays = [], []
    for operand in operands:
        if isinstance(operand, tuple):
            arrays.append(operand[0])
            specs.append(operand[1])
        else:
            arrays.append(operand)
            specs.append(whole_block(operand.shape))
    return pl.pallas_call(
        kernel,
        grid=(1,),
        in_specs=specs,
        out_specs=[whole_block(shape) for shape, _ in results],
        out_shape=[jax.ShapeDtypeStruct(shape, kind) for shape, kind in results],
        scratch_shapes=[pltpu.VMEM(shape, kind) for shape, kind in scratch],
        compiler_params=room(48),
        cost_estimate=LIGHT,
    )(*arrays)


MLP_TILE = 768


def mlp_both(cross_attn, project, after_self, modulation, out_grad, weights):
    frames = cross_attn.shape[0]
    far = lax.axis_size("far")
    rows = D // (4 * far)
    tiles = HALF // MLP_TILE
    once = dict(pipeline_mode=pl.Buffered(1))
    whole = pl.BlockSpec((frames, D), lambda half, tile: (0, 0), **once)
    square = (frames, D)
    return pl.pallas_call(
        mlp_kernel,
        grid=(2, tiles),
        in_specs=[
            whole,
            pl.BlockSpec((D, D), lambda half, tile: (0, 1), **once),
            whole,
            pl.BlockSpec((1, 6 * D), lambda half, tile: (0, 0)),
            whole,
            pl.BlockSpec((1, D, MLP_TILE), lambda half, tile: (half, 0, tile)),
            pl.BlockSpec((1, D, MLP_TILE), lambda half, tile: (half, 0, tile + tiles)),
        ],
        out_specs=[whole] * 4
        + [
            pl.BlockSpec((1, 3 * D), lambda half, tile: (0, 0)),
            pl.BlockSpec(
                (1, 4, far, 2, rows, MLP_TILE), lambda half, tile: (half, 0, 0, 0, 0, tile)
            ),
        ],
        out_shape=[
            jax.ShapeDtypeStruct(square, BFLOAT),
            jax.ShapeDtypeStruct(square, FLOAT),
            jax.ShapeDtypeStruct(square, BFLOAT),
            jax.ShapeDtypeStruct(square, BFLOAT),
            jax.ShapeDtypeStruct((1, 3 * D), FLOAT),
            jax.ShapeDtypeStruct((2, 4, far, 2, rows, HALF), BFLOAT),
        ],
        scratch_shapes=[
            pltpu.VMEM(square, BFLOAT),
            pltpu.VMEM(square, BFLOAT),
            pltpu.VMEM((D, frames), BFLOAT),
            pltpu.VMEM((D, frames), BFLOAT),
            pltpu.VMEM(square, FLOAT),
            pltpu.VMEM(square, FLOAT),
            pltpu.VMEM(square, FLOAT),
        ],
        compiler_params=room(48),
        cost_estimate=LIGHT,
    )(cross_attn, project, after_self, modulation, out_grad, weights, weights)


def per_device(
    block_in,
    text,
    timesteps,
    frame_mask,
    text_mask,
    cotangent,
    w_ada,
    w_qkv,
    w_out,
    w_cq,
    w_cout,
    w_ckv,
    w_fc1,
    w_fc2,
    row_state,
    col_state,
):
    clips = lax.axis_size(DP)
    devices = clips * 2
    data_at = lax.axis_index(DP)
    head_at = lax.axis_index("head")
    flat_at = data_at * 2 + head_at
    frames = block_in.shape[1]
    rows = w_qkv.shape[0]

    far = far_links()
    x_first = [far[0], row_link(), core_link()]
    y_first = [row_link(), far[0], core_link()]
    first = [
        gather_chain(
            with_bits(
                jnp.concatenate([w_qkv[:, :D], w_out, w_qkv[:, D:]], axis=1).astype(BFLOAT), "last"
            ),
            "last",
            far[:0:-1],
        )
    ]
    second = [
        gather_chain(
            with_bits(jnp.concatenate([w_cq, w_cout], axis=1).astype(BFLOAT), "last"),
            "last",
            far[:0:-1] + x_first,
        ),
        gather_chain(
            with_bits(w_ckv.astype(BFLOAT).reshape(w_ckv.shape[0], D), "columns"),
            "columns",
            far[:0:-1] + y_first,
        ),
    ]
    mlp_shard = jnp.concatenate([w_fc1.astype(BFLOAT), w_fc2.T.astype(BFLOAT)], axis=1)
    inputs = swap_place(block_in[0])
    joint_mask = jnp.concatenate([frame_mask[0], text_mask[0]])

    def add_step(link):
        return lambda state: state + cross(state, link)

    def project(steps):
        condition = embed_part(steps, flat_at * rows, rows)
        product = jnp.dot(condition, w_ada.astype(BFLOAT), preferred_element_type=FLOAT)
        return condition, product.reshape(clips // 2, 2, 6 * D)

    def keep_step(link):
        def step(state):
            condition, product = state
            bit = bit_of(link)
            dim = 1 if link == row_link() else dp_bits() - link[1].bit_length()
            kept = lax.dynamic_slice_in_dim(product, bit, 1, axis=dim)
            sent = lax.dynamic_slice_in_dim(product, 1 - bit, 1, axis=dim)
            product = kept + cross(sent, link)
            if link == row_link():
                product = product.reshape((2,) * (dp_bits() - 1) + (6 * D,))
            return condition, product

        return step

    def last_step(state):
        condition, product = state
        return condition, (product + cross(product, core_link())).reshape(1, 6 * D)

    steps = lax.dynamic_update_slice(jnp.zeros((clips,), jnp.int32), timesteps, (data_at,))
    timing = Chain(
        steps,
        [add_step(link) for link in [core_link()] + far_links()[1:] + far_links()[:1]]
        + [lambda steps: keep_step(row_link())(project(steps))]
        + [keep_step(link) for link in far_links()[1:] + far_links()[:1]]
        + [last_step],
    )
    far_count = len(far) - 1
    slots = far_count + 3
    for slot in range(slots):
        if slot < far_count:
            timing.advance(1 + (slot == 0) + (slot == far_count - 1))
        else:
            timing.advance((1, far_count, 2)[slot - far_count])
        if slot == far_count:
            joint = first[0].state
            first = [
                gather_chain(joint[..., : 2 * D], "last", x_first),
                gather_chain(joint[..., 2 * D :], "last", y_first),
            ]
        for chain in first:
            chain.advance()
        if slot >= 2:
            for chain in second:
                chain.advance()
        if slot == far_count - 1:
            inputs, mlp_shard, joint_mask, text = tie(
                [timing] + first + second, inputs, mlp_shard, joint_mask, text
            )
            mlp_all = lax.all_gather(mlp_shard, HEAD + DP, axis=0, tiled=True)
            masks = from_clip_core(joint_mask)
            clip_text = from_clip_core(text[0])
        elif slot < slots - 1:
            tie([timing] + first + (second if slot == far_count else []))
        else:
            wide = tie([timing] + first, w_ada, w_qkv, w_out, w_cq, w_cout, w_fc1, w_fc2)
            masters = [
                jnp.concatenate(wide[:5], axis=1),
                w_ckv.reshape(w_ckv.shape[0], D),
                jnp.concatenate([wide[5], wide[6].T], axis=1),
            ]
            (weight_squares,) = whole_call(weight_kernel, [(1, LINE)], *masters)
    condition, modulation = timing.finish()
    query_out, w_key_value = [chain.finish().reshape(D, 2 * D) for chain in first]
    square = (frames, D)
    core_at = data_at % 2
    own_allowed = lax.dynamic_slice_in_dim(masks, core_at * frames, frames)
    other_allowed = lax.dynamic_slice_in_dim(masks, (1 - core_at) * frames, frames)
    own_bias, other_bias = bias_of(own_allowed), bias_of(other_allowed)
    text_bias = bias_of(masks[2 * frames :])

    self_input, query, key_value = frame_call(
        first_kernel,
        [(square, BFLOAT), (square, BFLOAT), ((frames, 2 * D), BFLOAT)],
        inputs,
        modulation,
        left_half(query_out),
        w_key_value,
    )
    other_key_value = cross(key_value, core_link())
    query, other_key_value = tie(second, query, other_key_value)
    for chain in second:
        chain.advance()

    self_keys = [(key_value, own_bias), (other_key_value, other_bias)]
    self_attn, self_logs = attend(query, self_keys, plain_places, 2)
    self_attn, cotangent = tie(second, self_attn, cotangent)
    swapped_cotangent = swap_only(cotangent[0])
    cross_pair, w_text = [chain.finish() for chain in second]
    cross_pair, w_text = cross_pair.reshape(D, 2 * D), w_text.reshape(DT, 2 * D)
    self_branch, after_self, cross_input, cross_query, text_pair = frame_call(
        between_kernel,
        [
            (square, FLOAT),
            (square, FLOAT),
            (square, BFLOAT),
            (square, BFLOAT),
            ((clip_text.shape[0], 2 * D), BFLOAT),
        ],
        self_attn,
        right_half(query_out),
        inputs,
        modulation,
        left_half(cross_pair),
        clip_text,
        w_text,
    )

    text_keys = [(text_pair, text_bias)]
    cross_attn, cross_logs = attend(cross_query, text_keys, half_places, PAIRS // 2)

    cross_attn, own, cotangent = tie([], cross_attn, on_own_chip(), cotangent)
    out_grad = jnp.where(own, cotangent[0], swapped_cotangent)
    block_out, cross_res_grad, cross_out_grad, cross_attn_grad, mlp_sums, mlp_part = mlp_both(
        cross_attn,
        cross_pair,
        after_self,
        modulation,
        out_grad,
        mlp_all.reshape(2, D, 2 * HALF),
    )
    mlp_part = lax.psum_scatter(
        mlp_part.reshape((8,) + mlp_part.shape[2:]),
        HEAD + ("near", "core"),
        scatter_dimension=0,
        tiled=False,
    )

    cross_query_grad, text_pair_grad = attend_back(
        cross_query, cross_attn, cross_attn_grad, cross_logs, text_keys, half_places, PAIRS // 2
    )
    self_res_grad, self_out_grad, self_attn_grad, gate_self_grad = frame_call(
        between_back_kernel,
        [(square, FLOAT), (square, BFLOAT), (square, BFLOAT), ((1, D), FLOAT)],
        cross_query_grad,
        left_half(cross_pair),
        after_self,
        cross_res_grad,
        self_branch,
        modulation,
        right_half(query_out),
        scratch=[(square, FLOAT)],
    )

    query_grad, own_pair_grad, other_pair_grad = attend_back(
        query, self_attn, self_attn_grad, self_logs, self_keys, plain_places, 2
    )
    pair_grad = (
        own_pair_grad.astype(FLOAT) + cross(other_pair_grad, core_link()).astype(FLOAT)
    ).astype(BFLOAT)
    last_chains = [
        scatter_chain(
            outer((self_input, query_grad), (self_attn, self_out_grad)), "last", False
        ),
        scatter_chain(outer((self_input, pair_grad)), "last", True),
    ]
    cross_query_grad, text_pair_grad = tie(last_chains, cross_query_grad, text_pair_grad)
    for chain in last_chains:
        chain.advance()
    cross_chains = [
        scatter_chain(
            outer((cross_input, cross_query_grad), (cross_attn, cross_out_grad)), "last", False
        ),
        scatter_chain(outer((clip_text, text_pair_grad)), "columns", True),
    ]
    query_grad, pair_grad = tie(cross_chains + last_chains, query_grad, pair_grad)
    for chain in last_chains + cross_chains:
        chain.advance()
    input_grad, self_sums = frame_call(
        first_back_kernel,
        [(square, BFLOAT), ((1, 2 * D), FLOAT)],
        query_grad,
        pair_grad,
        left_half(query_out),
        w_key_value,
        inputs,
        modulation,
        self_res_grad,
        scratch=[(square, FLOAT)],
    )
    modulation_grad = jnp.concatenate([self_sums, gate_self_grad, mlp_sums], axis=-1)

    def join_step(link):
        def step(state):
            other = cross(state, link)
            upper = bit_of(link) == 1
            dim = dp_bits() - 1 if link[0] == HEAD else dp_bits() - link[1].bit_length()
            low, high = jnp.where(upper, other, state), jnp.where(upper, state, other)
            return jnp.concatenate([low, high], axis=dim)

        return step

    far = far_links()
    shape = (1,) * dp_bits() + (6 * D,)
    joining = Chain(
        modulation_grad,
        [lambda state: (state + cross(state, core_link())).reshape(shape)]
        + [join_step(link) for link in far[:0:-1] + [far[0], row_link()]],
    )

    chains = last_chains + cross_chains
    joining.advance()
    block_out, input_grad, mlp_part = tie([joining] + chains, block_out, input_grad, mlp_part)
    mlp_raw = lax.psum_scatter(mlp_part, "far", scatter_dimension=0, tiled=False).astype(FLOAT)
    for chain in chains:
        chain.advance()
    joining.advance(len(far) - 1)
    block_out, input_grad = tie([joining] + chains, block_out, input_grad)
    for chain in chains:
        chain.advance()
    joining.advance(2)
    block_out, input_grad, mlp_raw = tie([joining] + chains, block_out, input_grad, mlp_raw)
    for chain in chains:
        chain.advance()
    block_out, input_grad = tie(chains, block_out, input_grad)
    other_out, other_grad = swap_only(block_out), swap_only(input_grad)
    for chain in cross_chains:
        chain.advance()
    tie(cross_chains)
    modulation_grad = joining.finish()
    ada_raw = jnp.einsum(
        "cr,cx->rx",
        condition.astype(FLOAT),
        modulation_grad.reshape(clips, 6 * D),
        precision=PRECISE,
    )

    cross_raw, ckv_raw = [chain.finish() for chain in cross_chains]
    query_out_raw, pair_raw = [chain.finish() for chain in last_chains]

    place = jnp.stack([data_at, head_at]).astype(jnp.int32)
    raw_grads = [ada_raw, query_out_raw, pair_raw, cross_raw, ckv_raw, mlp_raw]
    (statistics,) = whole_call(
        statistics_kernel, [(STAT_LINES, LINE)], place, weight_squares, *raw_grads, places=1
    )
    sums = sum_all(statistics)
    shapes = [(rows, columns) for columns in COL_SIZES[:5]]
    shapes += [masters[1].shape] + [(rows * 2, HALF)] * 2
    line = (1, LINE)
    row_new, col_new, norm, update_squares, *rest = whole_call(
        update_kernel,
        [(ROW_LINES, LINE), (COL_LINES, LINE), line, line]
        + shapes
        + [master.shape for master in masters],
        place,
        sums,
        row_state.reshape(ROW_LINES, LINE),
        col_state.reshape(COL_LINES, LINE),
        *raw_grads,
        places=1,
    )
    clipped, updates = list(rest[:8]), rest[8:]
    clipped[5] = clipped[5].reshape(w_ckv.shape)
    clipped[7] = clipped[7].T
    late, _ = tie([], on_own_chip(), update_squares)
    block_out = jnp.where(late, block_out, other_out)
    input_grad = jnp.where(late, input_grad, other_grad)
    update_squares, block_out, input_grad, *clipped = tie(
        [], sum_all(update_squares), block_out, input_grad, *clipped
    )
    updated = list(
        whole_call(
            apply_kernel,
            shapes,
            update_squares,
            sums[STAT_LINES - 2 : STAT_LINES - 1],
            *masters,
            *updates,
        )
    )
    updated[5] = updated[5].reshape(w_ckv.shape)
    updated[7] = updated[7].T
    return (
        block_out[None],
        input_grad[None],
        norm[0, 0],
        row_new.reshape(-1),
        col_new.reshape(-1),
        *clipped,
        *updated,
    )


def solution(mesh):
    devices = mesh.devices
    refined = jax.sharding.Mesh(devices.reshape(devices.shape[0] // 4, 2, 2, 2), ALL)
    return jax.shard_map(
        per_device,
        mesh=refined,
        in_specs=(
            P(DP, "head", None),
            P(DP, None, None),
            P(DP),
            P(DP, None),
            P(DP, None),
            P(DP, "head", None),
            P(ALL, None),
            P(ALL, None),
            P(ALL, None),
            P(ALL, None),
            P(ALL, None),
            P(DP, None, "head"),
            P(DP, "head"),
            P("head", DP),
            P(),
            P(),
        ),
        out_specs=(
            P(DP, "head", None),
            P(DP, "head", None),
            P(),
            P(),
            P(),
            P(ALL, None),
            P(ALL, None),
            P(ALL, None),
            P(ALL, None),
            P(ALL, None),
            P(DP, None, "head"),
            P(DP, "head"),
            P("head", DP),
            P(ALL, None),
            P(ALL, None),
            P(ALL, None),
            P(ALL, None),
            P(ALL, None),
            P(DP, None, "head"),
            P(DP, "head"),
            P("head", DP),
        ),
        check_vma=False,
    )
```
